32 devices in a mesh: narrow: 4 (over y, x), wide: 8 (over z, core).
Axes of the slice: x: 2, y: 2, z: 4, core: 2. Of those that a mesh axis runs over, the one named last changes fastest.
Arguments:
- hidden_in: bfloat16 [32768, 768], P(('narrow', 'wide')), may hold values from -6 to 6
- norm_gain_one: float32 [768], replicated, may hold values from 0.5 to 1.5
- w_qkv: bfloat16 [768, 2304], replicated, may hold values from -0.21875 to 0.21875
- w_out: bfloat16 [768, 768], replicated, may hold values from -0.875 to 0.875
- pos_table: float32 [32, 12], replicated, may hold values from -4 to 4
- norm_gain_two: float32 [768], replicated, may hold values from 0.5 to 1.5
- w_router: bfloat16 [768, 32], replicated, may hold values from -0.08984375 to 0.08984375
- w_in: bfloat16 [32, 768, 3072], P(('narrow', 'wide')), may hold values from -0.21875 to 0.21875
- w_down: bfloat16 [32, 3072, 768], P(('narrow', 'wide')), may hold values from -3.453125 to 3.453125
- expert_ids: int32 [32768, 1], P(('narrow', 'wide')), may hold values from 0 to 31
- segment_ids: int32 [64, 512], P(('narrow', 'wide')), may hold values from 0 to 3, never falling along the last dimension, each value on 1 to 256 neighbouring positions
- rel_buckets: int32 [512, 512], replicated, may hold values from 0 to 31
- out_grad: bfloat16 [32768, 768], P(('narrow', 'wide')), may hold values from -6 to 6
Outputs:
- layer_out: bfloat16 [32768, 768], P(('narrow', 'wide'))
- in_grad: float32 [32768, 768], P(('narrow', 'wide'))
- gain_one_grad: float32 [768], replicated
- qkv_grad: float32 [768, 2304], replicated
- out_proj_grad: float32 [768, 768], replicated
- table_grad: float32 [32, 12], replicated
- gain_two_grad: float32 [768], replicated
- router_grad: float32 [768, 32], replicated
- w_in_grad: float32 [32, 768, 3072], P(('narrow', 'wide'))
- w_down_grad: float32 [32, 3072, 768], P(('narrow', 'wide'))
The draws below stay inside these ranges and needn't reach their ends.
Inputs may be any that keep to these rules, and one draw needn't show every extreme that they name: `segment_ids`: document numbers never fall along a row.
All inputs are finite; a program needn't handle non-finite values.
Results may differ from the reference program's by a relative error of at most 0.015.
Values may be sent and summed in bfloat16 or wider, within the bound.
A program may use at most 256 MiB of HBM per device.

```python
import math
import jax
import jax.numpy as jnp
import numpy as np
from jax import lax

D = 768
FF = 3072
HEADS = 12
HEAD_DIM = 64
LEN = 512
BUCKETS = 32
TOK_DEV = 1024
SEQS = 64
TOKENS = 32768
EXPERTS = 32
CAP = 40


def plant(values, own_key, least, largest):
    index_at = [jax.random.randint(jax.random.fold_in(own_key, axis), (), 0, length) for axis, length in enumerate(values.shape)]
    main_axis = values.shape.index(max(values.shape))
    beside = index_at[:main_axis] + [(index_at[main_axis] + 1) % values.shape[main_axis]] + index_at[main_axis + 1:]
    return values.at[tuple(index_at)].set(least).at[tuple(beside)].set(largest)


def steps_of(own_key, dims, shards, low, largest):
    level, own = 1.0, jax.random.fold_in(own_key, 6)
    for dim, blocks in shards:
        draws = jnp.exp(jax.random.uniform(jax.random.fold_in(own, dim), (blocks,), jnp.float32, low / len(shards), largest / len(shards)))
        level = level * jnp.repeat(draws, dims[dim] // blocks).reshape([-1 if axis == dim else 1 for axis in range(len(dims))])
    return level


def picks_of(stream_key, rows, amount, top, lift):
    ranking = jax.random.permutation(jax.random.fold_in(stream_key, 1), amount)
    favour = ranking
    for power in range(3):
        favour = favour * favour // amount
    favour = favour * lift // amount
    tickets = jax.random.randint(jax.random.fold_in(stream_key, 2), (rows, amount), 0, 4096) + favour
    holders = jax.random.permutation(jax.random.fold_in(stream_key, 3), rows)[jnp.arange(amount) % rows]
    tickets = jnp.where(jnp.arange(rows)[:, None] == holders[None, :], 1 << 14, tickets)
    merit = tickets * amount + jnp.arange(amount)
    return lax.top_k(merit.astype(jnp.int32), top)[1].astype(jnp.int32)


def profile(amount, total, limit, lean):
    weights = [(1 << 20) // math.isqrt(rank ** lean) + 1 for rank in range(2, amount + 1)]
    surplus, holding = total - limit - (amount - 1), [1] * (amount - 1)
    while surplus > 0:
        free = [i for i in range(amount - 1) if holding[i] < limit]
        whole, left = sum([weights[i] for i in free]), surplus
        for i in free:
            extra = min(limit - holding[i], max(1, left * weights[i] // whole), surplus)
            holding[i] = holding[i] + extra
            surplus = surplus - extra
    return np.array([limit] + holding)


def uneven(own_key, amount, total, bound, skew):
    if amount == 2:
        one = jax.random.randint(own_key, (), max(1, total - bound), min(bound, total - 1) + 1)
        return jnp.stack([one, total - one])
    lengths = jnp.asarray(profile(amount, total, bound, skew), jnp.int32)
    pairs = (amount - 1) // 2
    donor, taker = lengths[1:1 + 2 * pairs:2], lengths[2:2 + 2 * pairs:2]
    margin = jnp.minimum(donor - 1, bound - taker)
    passed = jax.random.randint(jax.random.fold_in(own_key, 1), (pairs,), 0, 1 << 20) % (margin + 1)
    lengths = lengths.at[1:1 + 2 * pairs:2].set(donor - passed).at[2:2 + 2 * pairs:2].set(taker + passed)
    return lengths[jax.random.permutation(jax.random.fold_in(own_key, 2), amount)]


def scatter_about(rng, shape, width, limit, pieces=(), kind=jnp.bfloat16):
    gain = steps_of(rng, shape, pieces, -0.22, 0.18) if pieces else 1.0
    entries = jax.random.normal(rng, shape, jnp.float32) * width * gain
    return jnp.minimum(jnp.maximum(entries, -limit), limit).astype(kind)


def setup_inputs(seed: int = 0) -> dict:
    key_list = jax.random.split(jax.random.key(seed), 14)
    return {
        "hidden_in": scatter_about(key_list[0], (TOKENS, D), 1.0, 6.0, ((0, 32),)),
        "norm_gain_one": jnp.clip(1.0 + 0.1 * jax.random.normal(key_list[1], (D,), jnp.float32), 0.5, 1.5),
        "w_qkv": scatter_about(key_list[2], (D, 3 * D), D ** -0.5, 0.21875),
        "w_out": scatter_about(key_list[3], (D, D), (D // 16) ** -0.5, 0.875),
        "pos_table": scatter_about(key_list[4], (BUCKETS, HEADS), 1.0, 4.0, (), jnp.float32),
        "norm_gain_two": jnp.clip(1.0 + 0.1 * jax.random.normal(key_list[5], (D,), jnp.float32), 0.5, 1.5),
        "w_router": scatter_about(key_list[6], (D, EXPERTS), (0.5 * D ** -0.5), 0.08984375),
        "w_in": scatter_about(key_list[7], (EXPERTS, D, FF), D ** -0.5, 0.21875, ((0, 32),)),
        "w_down": scatter_about(key_list[8], (EXPERTS, FF, D), (1.5 * EXPERTS * FF ** -0.5), 3.453125, ((0, 32),)),
        "expert_ids": picks_of(key_list[9], TOKENS, EXPERTS, 1, 0),
        "segment_ids": jax.vmap(lambda own: jnp.searchsorted(jnp.cumsum(uneven(own, 4, LEN, LEN // 2, 1)), jnp.arange(LEN), side="right"))(jax.random.split(key_list[10], SEQS)).reshape((SEQS, LEN)).astype(jnp.int32),
        "rel_buckets": plant(jax.random.randint(key_list[11], (LEN, LEN), 0, BUCKETS), jax.random.fold_in(key_list[11], 1), 0, BUCKETS - 1).astype(jnp.int32),
        "out_grad": scatter_about(key_list[12], (TOKENS, D), 1.0, 6.0, ((0, 32),)),
    }


@jax.custom_vjp
def low(v):
    return lax.optimization_barrier(v.astype(jnp.bfloat16)).astype(jnp.float32)

@jax.custom_vjp
def low_back(v):
    return v

def low_keep(v):
    return (low(v), None)

def low_pass(kept, grad):
    return (grad,)

def back_keep(v):
    return (v, None)

def back_low(kept, grad):
    return (low(grad),)
low.defvjp(low_keep, low_pass)
low_back.defvjp(back_keep, back_low)
EPS = 1e-06
HIGH = lax.Precision.HIGHEST

def matmul(a, b):
    return jnp.dot(a, b, precision=HIGH, preferred_element_type=jnp.float32)

def rms_scale(v):
    return lax.rsqrt(lax.optimization_barrier(jnp.mean(v * v, axis=-1, keepdims=True)) + EPS)

def slot_numbers(expert_list):
    groups = expert_list.reshape(-1, TOK_DEV)
    onehot = (groups[:, :, None] == jnp.arange(EXPERTS, dtype=jnp.int32)[None, None, :]).astype(jnp.int32)
    before = jnp.cumsum(onehot, axis=1) - onehot
    position = lax.optimization_barrier(jnp.sum(before * onehot, axis=2)).astype(jnp.int32)
    return jnp.where(position < CAP, groups * CAP + position, -1).astype(jnp.int32)

def forward(source, gain_one, w_qkv, w_out, pos_table, gain_two, w_router, w_in, w_down, slots, expert_list, segment_ids, rel_buckets):
    tok_total = source.shape[0]
    group_count = tok_total // TOK_DEV
    normed_one = low(source * rms_scale(source) * gain_one)
    qkv = low(low_back(matmul(normed_one, w_qkv)))
    bucket_hot = (rel_buckets[:, :, None] == jnp.arange(BUCKETS, dtype=jnp.int32)[None, None, :]).astype(jnp.float32)
    bias = jnp.einsum('qkb,bh->hqk', bucket_hot, pos_table, precision=HIGH)
    blocks = qkv.reshape(SEQS, LEN, 3, HEADS, HEAD_DIM)
    factor = HEAD_DIM ** (-0.5)

    def attend(pair):
        block, segs = pair
        raw = jnp.einsum('qhd,khd->hqk', block[:, 0], block[:, 1], precision=HIGH) * factor + bias
        same = segs[:, None] == segs[None, :]
        scores = low_back(jnp.where(same[None], raw, -1000000000.0))
        probs = low(jax.nn.softmax(scores, axis=-1))
        return jnp.einsum('hqk,khd->qhd', probs, block[:, 2], precision=HIGH).reshape(LEN, D)
    mixed = lax.map(jax.checkpoint(attend), (blocks, segment_ids))
    attn = low(low_back(mixed.reshape(tok_total, D)))
    resid = source + low_back(matmul(attn, w_out))
    normed_two = low(resid * rms_scale(resid) * gain_two)
    logits = low_back(matmul(normed_two, w_router))
    route = jax.nn.softmax(logits, axis=-1)
    route_hot = (expert_list[:, None] == jnp.arange(EXPERTS, dtype=jnp.int32)[None, :]).astype(jnp.float32)
    gate = lax.optimization_barrier(jnp.sum(route * route_hot, axis=-1))
    slot_index = jnp.arange(EXPERTS * CAP, dtype=jnp.int32)

    def pack(pair):
        rows, numbers = pair
        table = (slot_index[:, None] == numbers[None, :]).astype(jnp.float32)
        return matmul(table, rows)
    packed = lax.map(pack, (normed_two.reshape(group_count, TOK_DEV, D), slots))
    expert_rows = packed.reshape(group_count, EXPERTS, CAP, D).transpose(1, 0, 2, 3).reshape(EXPERTS, group_count * CAP, D)
    expert_rows = low_back(expert_rows)

    def expert(triple):
        rows, first, second = triple
        inner = low_back(matmul(rows, first))
        active = low(jax.nn.gelu(inner))
        return low(low_back(matmul(active, second)))
    returned = lax.map(jax.checkpoint(expert), (expert_rows, w_in, w_down))
    back_rows = returned.reshape(EXPERTS, group_count, CAP, D).transpose(1, 0, 2, 3).reshape(group_count, EXPERTS * CAP, D)

    def unpack(pair):
        rows, numbers = pair
        table = (slot_index[:, None] == numbers[None, :]).astype(jnp.float32)
        return jnp.dot(table.T, rows, precision=HIGH, preferred_element_type=jnp.float32)
    combined = lax.map(unpack, (back_rows, slots)).reshape(tok_total, D)
    return resid + gate[:, None] * combined

def reference(hidden_in, norm_gain_one, w_qkv, w_out, pos_table, norm_gain_two, w_router, w_in, w_down, expert_ids, segment_ids, rel_buckets, out_grad):
    expert_list = expert_ids[:, 0]
    slots = slot_numbers(expert_list)

    def apply(source, gain_one, wq, wo, table, gain_two, wr, wi, wd):
        return forward(source, gain_one, wq, wo, table, gain_two, wr, wi, wd, slots, expert_list, segment_ids, rel_buckets)
    floats = (hidden_in.astype(jnp.float32), norm_gain_one, w_qkv.astype(jnp.float32), w_out.astype(jnp.float32), pos_table, norm_gain_two, w_router.astype(jnp.float32), w_in.astype(jnp.float32), w_down.astype(jnp.float32))
    result, pull = jax.vjp(apply, *floats)
    grads = pull(out_grad.astype(jnp.float32))
    return (result.astype(jnp.bfloat16), grads[0], grads[1], grads[2], grads[3], grads[4], grads[5], grads[6], grads[7], grads[8])
```

```python
import functools
import jax
import jax.numpy as jnp
from jax import lax
from jax.experimental import pallas as pl
from jax.experimental.pallas import tpu as pltpu
from jax.sharding import PartitionSpec as P

HEADS = 12
HEAD_DIM = 64
LEN = 512
BUCKETS = 32
EPS = 1e-06
LANES = 128
HALF = 256
GROUP = 4
PAIR = 2
GROUPS = HEADS // GROUP
GW = GROUP * HEAD_DIM
F32 = jnp.float32
BF16 = jnp.bfloat16
MIB = 1024 * 1024


def dot_nn(a, b):
    return lax.dot_general(a, b, (((1,), (0,)), ((), ())), preferred_element_type=F32)


def dot_tn(a, b):
    return lax.dot_general(a, b, (((0,), (0,)), ((), ())), preferred_element_type=F32)


def dot_nt(a, b):
    return lax.dot_general(a, b, (((1,), (1,)), ((), ())), preferred_element_type=F32)


def whole(shape):
    rank = len(shape)
    return pl.BlockSpec(shape, lambda *g: (0,) * rank, pipeline_mode=pl.Buffered(1))


def split3(v):
    high = v.astype(BF16)
    rest = v - high.astype(F32)
    mid = rest.astype(BF16)
    low = (rest - mid.astype(F32)).astype(BF16)
    return high, mid, low


def slots_kernel(experts, cap, capp, ids_ref, g_ref, slot_ref, pos_ref, packed_ref):
    tok = ids_ref.shape[1]
    ids = ids_ref[...]
    hot = lax.broadcasted_iota(jnp.int32, (experts, tok), 0) == ids
    before = (
        lax.broadcasted_iota(jnp.int32, (tok, tok), 0)
        < lax.broadcasted_iota(jnp.int32, (tok, tok), 1)
    )
    counts = dot_nn(hot.astype(F32).astype(BF16), before.astype(F32).astype(BF16))
    pos = jnp.sum(jnp.where(hot, counts, 0.0), axis=0, keepdims=True).astype(jnp.int32)
    kept = pos < cap
    slot = jnp.where(kept, ids * capp + pos, -1)
    slot_ref[...] = slot
    pos_ref[...] = jnp.where(kept, pos, -1)
    rows = packed_ref.shape[0]
    step = 256

    @pl.loop(0, rows // step)
    def _(r):
        base = pl.multiple_of(r * step, step)
        table = (lax.broadcasted_iota(jnp.int32, (step, tok), 0) + base == slot)
        packed_ref[pl.ds(base, step), :] = dot_nn(
            table.astype(F32).astype(BF16), g_ref[...]
        ).astype(BF16)


def make_slots(experts, cap, capp, ids_row, g):
    tok, width = g.shape
    return pl.pallas_call(
        functools.partial(slots_kernel, experts, cap, capp),
        out_shape=(
            jax.ShapeDtypeStruct((1, tok), jnp.int32),
            jax.ShapeDtypeStruct((1, tok), jnp.int32),
            jax.ShapeDtypeStruct((experts * capp, width), BF16),
        ),
        compiler_params=pltpu.CompilerParams(vmem_limit_bytes=40 * MIB),
        name="slots",
    )(ids_row, g)


def front_kernel(
    hid_ref, gain1_ref, wq_ref, wk_ref, wv_ref, wout_ref, tab_ref, gain2_ref, wr_ref,
    ids_ref, slot_ref, pos_ref, segr_ref, segc_ref, rel_ref,
    n1_ref, q_ref, k_ref, v_ref, p_ref, attn_ref, resid_ref, n2_ref, route_ref, gate_ref,
    packed_ref, gpack_ref,
    relt, mask, bias,
):
    step = pl.program_id(0)
    seqs = segr_ref.shape[0]
    tok = hid_ref.shape[0]

    @pl.when(step == 0)
    def _():
        for t in range(0, tok, HALF):
            x = hid_ref[t:t + HALF, :].astype(F32).T
            scale = lax.rsqrt(jnp.mean(x * x, axis=0, keepdims=True) + EPS)
            n1_ref[:, t:t + HALF] = (x * scale * gain1_ref[...]).astype(BF16)
        relt[...] = rel_ref[...].T
        for s in range(seqs):
            mask[s] = jnp.where(segc_ref[s] == segr_ref[s], 0.0, -1000000000.0)

    for w_ref, o_ref in ((wq_ref, q_ref), (wk_ref, k_ref), (wv_ref, v_ref)):
        o_ref[...] = dot_tn(w_ref[...], n1_ref[...]).astype(BF16)

    @pl.loop(0, GROUP)
    def _(h):
        head = step * GROUP + h
        row = tab_ref[pl.ds(head, 1), :]
        line = jnp.broadcast_to(row, (LEN, LANES))
        for c in range(0, LEN, LANES):
            bias[:, c:c + LANES] = jnp.take_along_axis(line, relt[:, c:c + LANES], axis=1)
        at = pl.ds(pl.multiple_of(h * HEAD_DIM, HEAD_DIM), HEAD_DIM)
        out_at = pl.ds(pl.multiple_of(head * HEAD_DIM, HEAD_DIM), HEAD_DIM)
        for s in range(seqs):
            key = k_ref[at, s * LEN:(s + 1) * LEN]
            value = v_ref[at, s * LEN:(s + 1) * LEN]
            for c in range(0, LEN, HALF):
                cols = slice(s * LEN + c, s * LEN + c + HALF)
                query = q_ref[at, cols] * jnp.asarray(HEAD_DIM ** -0.5, BF16)
                score = dot_tn(key, query) + bias[:, c:c + HALF] + mask[s, :, c:c + HALF]
                peak = jnp.max(score, axis=0, keepdims=True)
                weight = jnp.exp(score - peak)
                total = jnp.sum(weight, axis=0, keepdims=True)
                prob = (weight * (1.0 / total)).astype(BF16)
                p_ref[h, s, :, c:c + HALF] = prob
                attn_ref[out_at, cols] = dot_nn(value, prob).astype(BF16)

    @pl.when(step == pl.num_programs(0) - 1)
    def _():
        experts = route_ref.shape[0]
        for t in range(0, tok, HALF):
            cols = slice(t, t + HALF)
            x = hid_ref[t:t + HALF, :].astype(F32).T
            resid = x + dot_tn(wout_ref[...], attn_ref[:, cols])
            resid_ref[:, cols] = resid
            scale = lax.rsqrt(jnp.mean(resid * resid, axis=0, keepdims=True) + EPS)
            n2 = (resid * scale * gain2_ref[...]).astype(BF16)
            n2_ref[:, cols] = n2
            logits = dot_tn(wr_ref[...], n2)
            top = jnp.max(logits, axis=0, keepdims=True)
            e = jnp.exp(logits - top)
            route = e / jnp.sum(e, axis=0, keepdims=True)
            route_ref[:, cols] = route
            hot = lax.broadcasted_iota(jnp.int32, (experts, HALF), 0) == ids_ref[:, cols]
            gate_ref[:, cols] = jnp.sum(jnp.where(hot, route, 0.0), axis=0, keepdims=True)
        hot = lax.broadcasted_iota(jnp.int32, (experts, tok), 0) == ids_ref[...]
        gates = jnp.where(hot, gate_ref[...], 0.0)
        place = (
            lax.broadcasted_iota(jnp.int32, (LANES, tok), 0) == pos_ref[...]
        ).astype(F32).astype(BF16)
        parts = [dot_nt(part, place) for part in split3(gates)]
        which = lax.broadcasted_iota(jnp.int32, (experts, 8, LANES), 1)
        spread = [jnp.broadcast_to(part[:, None, :], which.shape) for part in parts]
        gpack_ref[...] = jnp.where(
            which == 0, spread[0],
            jnp.where(which == 1, spread[1], jnp.where(which == 2, spread[2], 0.0)),
        ).astype(BF16)
        rows = packed_ref.shape[0]

        @pl.loop(0, rows // HALF)
        def _(r):
            base = pl.multiple_of(r * HALF, HALF)
            table = (lax.broadcasted_iota(jnp.int32, (HALF, tok), 0) + base == slot_ref[...])
            packed_ref[pl.ds(base, HALF), :] = dot_nt(
                table.astype(F32).astype(BF16), n2_ref[...]
            ).astype(BF16)


def front(hidden, gain1, w_qkv, w_out, table, gain2, w_router, ids, slot, pos, seg, rel, rows):
    tok, width = hidden.shape
    experts = w_router.shape[1]
    seqs = seg.shape[0]
    wspec = lambda part: pl.BlockSpec((width, GW), lambda i: (0, part * GROUPS + i))
    qspec = pl.BlockSpec((GW, tok), lambda i: (i, 0))
    sd = jax.ShapeDtypeStruct
    outs = (
        sd((width, tok), BF16), sd((width, tok), BF16), sd((width, tok), BF16),
        sd((width, tok), BF16), sd((HEADS, seqs, LEN, LEN), BF16), sd((width, tok), BF16),
        sd((width, tok), F32), sd((width, tok), BF16), sd((experts, tok), F32), sd((1, tok), F32),
        sd((rows, width), BF16), sd((experts, 8, LANES), BF16),
    )
    return pl.pallas_call(
        front_kernel,
        grid=(GROUPS,),
        in_specs=[
            whole((tok, width)), whole((width, 1)), wspec(0), wspec(1), wspec(2),
            whole((width, width)), whole((HEADS, LANES)), whole((width, 1)),
            whole((width, experts)), whole((1, tok)), whole((1, tok)), whole((1, tok)),
            whole((seqs, 1, LEN)), whole((seqs, LEN, 1)), whole((LEN, LEN)),
        ],
        out_specs=(
            whole((width, tok)), qspec, qspec, qspec,
            pl.BlockSpec((GROUP, seqs, LEN, LEN), lambda i: (i, 0, 0, 0)),
            whole((width, tok)), whole((width, tok)), whole((width, tok)),
            whole((experts, tok)), whole((1, tok)), whole((rows, width)),
            whole((experts, 8, LANES)),
        ),
        out_shape=outs,
        scratch_shapes=[
            pltpu.VMEM((LEN, LEN), jnp.int32),
            pltpu.VMEM((seqs, LEN, LEN), F32),
            pltpu.VMEM((LEN, LEN), F32),
        ],
        compiler_params=pltpu.CompilerParams(vmem_limit_bytes=58 * MIB),
        name="front",
    )(
        hidden, gain1.reshape(width, 1), w_qkv, w_qkv, w_qkv, w_out, table,
        gain2.reshape(width, 1), w_router, ids, slot, pos,
        seg.reshape(seqs, 1, LEN), seg.reshape(seqs, LEN, 1), rel,
    )


def combine_kernel(rows_ref, slot_ref, gate_ref, resid_ref, out_ref):
    total = rows_ref.shape[0]
    cols = slot_ref.shape[1]
    table = lax.broadcasted_iota(jnp.int32, (total, cols), 0) == slot_ref[...]
    combined = dot_tn(rows_ref[...], table.astype(F32).astype(BF16))
    out_ref[...] = (resid_ref[...] + gate_ref[...] * combined).T.astype(BF16)


def combine(rows, slot, gate, resid):
    total, width = rows.shape
    tok = slot.shape[1]
    line = pl.BlockSpec((1, HALF), lambda i: (0, i))
    return pl.pallas_call(
        combine_kernel,
        grid=(tok // HALF,),
        in_specs=[
            whole((total, width)), line, line, pl.BlockSpec((width, HALF), lambda i: (0, i)),
        ],
        out_specs=pl.BlockSpec((HALF, width), lambda i: (i, 0)),
        out_shape=jax.ShapeDtypeStruct((tok, width), BF16),
        compiler_params=pltpu.CompilerParams(vmem_limit_bytes=40 * MIB),
        name="combine",
    )(rows, slot, gate, resid)


def norm_back(grad, source, gain):
    scale = lax.rsqrt(jnp.mean(source * source, axis=0, keepdims=True) + EPS)
    normed = source * scale
    scaled = grad * gain
    inner = jnp.mean(scaled * normed, axis=0, keepdims=True)
    return scale * (scaled - normed * inner), jnp.sum(grad * normed, axis=1, keepdims=True)


def back_kernel(
    dx_ref, gg_ref, slot_ref, pos_ref, ids_ref, route_ref, gate_ref, resid_ref, n2_ref, attn_ref,
    g_ref, hid_ref, n1_ref, q_ref, k_ref, v_ref, p_ref, gain1_ref, gain2_ref, wr_ref, wout_ref,
    wq_ref, wk_ref, wv_ref,
    ingrad_ref, gain1g_ref, gq_ref, gk_ref, gv_ref, outg_ref, gain2g_ref, routerg_ref, ds_ref,
    gres, ga, gn1, dq, dk, dv,
):
    step = pl.program_id(0)
    pair = pl.program_id(1)
    tok = hid_ref.shape[0]
    seqs = tok // LEN
    experts = route_ref.shape[0]
    total = dx_ref.shape[0]

    @pl.when((step == 0) & (pair == 0))
    def _():
        hot = lax.broadcasted_iota(jnp.int32, (experts, tok), 0) == ids_ref[...]
        place = (
            lax.broadcasted_iota(jnp.int32, (LANES, tok), 0) == pos_ref[...]
        ).astype(F32).astype(BF16)
        found = dot_nn(gg_ref[...].reshape(experts * 8, LANES), place)
        found = jnp.sum(found.reshape(experts, 8, tok), axis=1)
        grad_gate = jnp.sum(jnp.where(hot, found, 0.0), axis=0, keepdims=True)
        grad_logits = (
            (grad_gate * gate_ref[...]) * (hot.astype(F32) - route_ref[...])
        ).astype(BF16)
        routerg_ref[...] = dot_nt(n2_ref[...], grad_logits)
        gain_grad = jnp.zeros(gain2g_ref.shape, F32)
        for t in range(0, tok, HALF):
            cols = slice(t, t + HALF)
            table = lax.broadcasted_iota(jnp.int32, (total, HALF), 0) == slot_ref[:, cols]
            gn2 = dot_tn(dx_ref[...], table.astype(F32).astype(BF16))
            gn2 = gn2 + dot_nn(wr_ref[...], grad_logits[:, cols])
            branch, part = norm_back(gn2, resid_ref[:, cols], gain2_ref[...])
            gain_grad = gain_grad + part
            gr = g_ref[t:t + HALF, :].astype(F32).T + branch
            gres[:, cols] = gr
            ga[:, cols] = gr.astype(BF16)
        gain2g_ref[...] = gain_grad
        outg_ref[...] = dot_nt(attn_ref[...], ga[...])
        for t in range(0, tok, HALF):
            cols = slice(t, t + HALF)
            ga[:, cols] = dot_nn(wout_ref[...], ga[:, cols]).astype(BF16)
        gn1[...] = jnp.zeros_like(gn1)

    @pl.loop(0, PAIR)
    def _(h):
        inside = pair * PAIR + h
        head = step * GROUP + inside
        at = pl.ds(pl.multiple_of(inside * HEAD_DIM, HEAD_DIM), HEAD_DIM)
        all_at = pl.ds(pl.multiple_of(head * HEAD_DIM, HEAD_DIM), HEAD_DIM)
        for s in range(seqs):
            row = slice(s * LEN, (s + 1) * LEN)
            value = v_ref[at, row]
            for c in range(0, LEN, HALF):
                cols = slice(s * LEN + c, s * LEN + c + HALF)
                grad = ga[all_at, cols]
                inner = jnp.sum(
                    grad.astype(F32) * attn_ref[all_at, cols].astype(F32), axis=0, keepdims=True
                )
                gp = dot_tn(value, grad)
                ds_ref[h, s, :, c:c + HALF] = (
                    p_ref[h, s, :, c:c + HALF].astype(F32) * (gp - inner)
                ).astype(BF16)
            ds = ds_ref[h, s]
            dv[at, row] = dot_nt(ga[all_at, row], p_ref[h, s]).astype(BF16)
            factor = HEAD_DIM ** -0.5
            dq[at, row] = (dot_nn(k_ref[at, row], ds) * factor).astype(BF16)
            dk[at, row] = (dot_nt(q_ref[at, row], ds) * factor).astype(BF16)

    @pl.when(pair == pl.num_programs(1) - 1)
    def _():
        for d, o_ref, w_ref in ((dq, gq_ref, wq_ref), (dk, gk_ref, wk_ref), (dv, gv_ref, wv_ref)):
            o_ref[...] = dot_nt(n1_ref[...], d[...])
            gn1[...] += dot_nn(w_ref[...], d[...])

    @pl.when((step == pl.num_programs(0) - 1) & (pair == pl.num_programs(1) - 1))
    def _():
        gain_grad = jnp.zeros(gain1g_ref.shape, F32)
        for t in range(0, tok, HALF):
            cols = slice(t, t + HALF)
            x = hid_ref[t:t + HALF, :].astype(F32).T
            branch, part = norm_back(gn1[:, cols], x, gain1_ref[...])
            gain_grad = gain_grad + part
            ingrad_ref[t:t + HALF, :] = (gres[:, cols] + branch).T
        gain1g_ref[...] = gain_grad


def back(dx, gg, slot, pos, ids, route, gate, resid, n2, attn, g, hidden, n1, q, k, v, p, gain1, gain2,
         w_router, w_out, w_qkv):
    tok, width = hidden.shape
    experts = w_router.shape[1]
    total = dx.shape[0]
    seqs = p.shape[1]
    wspec = lambda part: pl.BlockSpec((width, GW), lambda i, j: (0, part * GROUPS + i))
    qspec = pl.BlockSpec((GW, tok), lambda i, j: (i, 0))
    pspec = pl.BlockSpec((PAIR, seqs, LEN, LEN), lambda i, j: (i * (GROUP // PAIR) + j, 0, 0, 0))
    gspec = pl.BlockSpec((width, GW), lambda i, j: (0, i))
    sd = jax.ShapeDtypeStruct
    return pl.pallas_call(
        back_kernel,
        grid=(GROUPS, GROUP // PAIR),
        in_specs=[
            whole((total, width)), whole((experts, 8, LANES)), whole((1, tok)), whole((1, tok)),
            whole((1, tok)), whole((experts, tok)), whole((1, tok)), whole((width, tok)),
            whole((width, tok)), whole((width, tok)), whole((tok, width)), whole((tok, width)),
            whole((width, tok)), qspec, qspec, qspec, pspec, whole((width, 1)), whole((width, 1)),
            whole((width, experts)), whole((width, width)), wspec(0), wspec(1), wspec(2),
        ],
        out_specs=(
            whole((tok, width)), whole((width, 1)), gspec, gspec, gspec, whole((width, width)),
            whole((width, 1)), whole((width, experts)), pspec,
        ),
        out_shape=(
            sd((tok, width), F32), sd((width, 1), F32), sd((width, width), F32),
            sd((width, width), F32), sd((width, width), F32), sd((width, width), F32),
            sd((width, 1), F32), sd((width, experts), F32), sd((HEADS, seqs, LEN, LEN), BF16),
        ),
        scratch_shapes=[
            pltpu.VMEM((width, tok), F32), pltpu.VMEM((width, tok), BF16),
            pltpu.VMEM((width, tok), F32), pltpu.VMEM((GW, tok), BF16),
            pltpu.VMEM((GW, tok), BF16), pltpu.VMEM((GW, tok), BF16),
        ],
        compiler_params=pltpu.CompilerParams(vmem_limit_bytes=62 * MIB),
        name="back",
    )(
        dx, gg, slot, pos, ids, route, gate, resid, n2, attn, g, hidden, n1, q, k, v, p,
        gain1.reshape(width, 1), gain2.reshape(width, 1), w_router, w_out, w_qkv, w_qkv, w_qkv,
    )


TROWS = 16


def table_kernel(ds_ref, rel_ref, out_ref, acc):
    step = pl.program_id(0)
    pairs = ds_ref.shape[0] * ds_ref.shape[1]
    block = ds_ref.shape[2]

    @pl.when(step == 0)
    def _():
        acc[...] = jnp.zeros_like(acc)

    @pl.loop(0, block // TROWS)
    def _(r):
        base = pl.multiple_of(r * TROWS, TROWS)
        lhs = ds_ref[:, :, pl.ds(base, TROWS), :].reshape(pairs * TROWS, LEN)
        rel = rel_ref[pl.ds(base, TROWS), :]
        hot = (
            rel[:, None, :] == lax.broadcasted_iota(jnp.int32, (TROWS, BUCKETS, LEN), 1)
        ).astype(F32).astype(BF16).reshape(TROWS * BUCKETS, LEN)
        acc[...] += dot_nt(lhs, hot)

    @pl.when(step == pl.num_programs(0) - 1)
    def _():
        rows = lax.broadcasted_iota(jnp.int32, acc.shape, 0) % TROWS
        cols = lax.broadcasted_iota(jnp.int32, acc.shape, 1) // BUCKETS
        kept = jnp.where(rows == cols, acc[...], 0.0)
        per_head = jnp.sum(kept.reshape(HEADS, pairs * TROWS // HEADS, acc.shape[1]), axis=1)
        fold = (
            lax.broadcasted_iota(jnp.int32, (BUCKETS, acc.shape[1]), 1) % BUCKETS
            == lax.broadcasted_iota(jnp.int32, (BUCKETS, acc.shape[1]), 0)
        ).astype(F32)
        out_ref[...] = lax.dot_general(
            fold, per_head, (((1,), (1,)), ((), ())), precision=lax.Precision.HIGHEST,
            preferred_element_type=F32,
        )


def table_grad(ds, relt):
    seqs = ds.shape[1]
    block = 128
    return pl.pallas_call(
        table_kernel,
        grid=(LEN // block,),
        in_specs=[
            pl.BlockSpec((HEADS, seqs, block, LEN), lambda i: (0, 0, i, 0)),
            pl.BlockSpec((block, LEN), lambda i: (i, 0)),
        ],
        out_specs=whole((BUCKETS, HEADS)),
        out_shape=jax.ShapeDtypeStruct((BUCKETS, HEADS), F32),
        scratch_shapes=[pltpu.VMEM((HEADS * seqs * TROWS, TROWS * BUCKETS), F32)],
        compiler_params=pltpu.CompilerParams(vmem_limit_bytes=40 * MIB),
        name="table_grad",
    )(ds, relt)


def matmul(a, b):
    return jnp.dot(a, b, preferred_element_type=F32)


AXES = ("narrow", "wide")


def exchange(v):
    return lax.all_to_all(v, AXES, split_axis=0, concat_axis=0, tiled=True)


def local(
    hidden_in, norm_gain_one, w_qkv, w_out, pos_table, norm_gain_two, w_router, w_in, w_down,
    expert_ids, segment_ids, rel_buckets, out_grad,
):
    experts = lax.axis_size("narrow") * lax.axis_size("wide")
    tok, width = hidden_in.shape
    cap = max(2, (5 * tok + 4 * experts - 1) // (4 * experts))
    capp = (cap + 7) // 8 * 8
    rows = experts * capp
    ids = expert_ids.reshape(1, tok)
    slot, pos, g_packed = make_slots(experts, cap, capp, ids, out_grad)
    g_rows = exchange(g_packed.reshape(experts, capp, width)).reshape(rows, width)
    table = jnp.pad(pos_table.T, ((0, 0), (0, LANES - BUCKETS)))
    (n1, q, k, v, p, attn, resid, n2, route, gate, packed, gpack) = front(
        hidden_in, norm_gain_one, w_qkv, w_out, table, norm_gain_two, w_router, ids, slot, pos,
        segment_ids, rel_buckets, rows,
    )
    expert_in = exchange(packed.reshape(experts, capp, width)).reshape(rows, width)
    gates = jnp.sum(exchange(gpack).astype(F32), axis=1)[:, :capp].reshape(rows, 1)
    inner = matmul(expert_in, w_in[0])
    active = jax.nn.gelu(inner).astype(BF16)
    expert_out = matmul(active, w_down[0]).astype(BF16)
    gg = jnp.sum(g_rows.astype(F32) * expert_out.astype(F32), axis=1).reshape(experts, capp)
    gg = jnp.pad(gg, ((0, 0), (0, LANES - capp)))
    gg = jnp.pad(jnp.stack(split3(gg), axis=1), ((0, 0), (0, 5), (0, 0)))
    grad_slots = (gates * g_rows.astype(F32)).astype(BF16)
    grad_active = lax.dot_general(grad_slots, w_down[0], (((1,), (1,)), ((), ())), preferred_element_type=F32)
    unused, pull = jax.vjp(jax.nn.gelu, inner)
    grad_inner = pull(grad_active)[0].astype(BF16)
    grad_rows = lax.dot_general(grad_inner, w_in[0], (((1,), (1,)), ((), ())), preferred_element_type=F32).astype(BF16)
    dx = exchange(grad_rows.reshape(experts, capp, width)).reshape(rows, width)
    gg = exchange(gg)
    out_rows = exchange(expert_out.reshape(experts, capp, width)).reshape(rows, width)
    grad_w_down = lax.dot_general(active, grad_slots, (((0,), (0,)), ((), ())), preferred_element_type=F32)
    grad_w_in = lax.dot_general(expert_in, grad_inner, (((0,), (0,)), ((), ())), preferred_element_type=F32)
    (in_grad, gain1g, gq, gk, gv, outg, gain2g, routerg, ds) = back(
        dx, gg, slot, pos, ids, route, gate, resid, n2, attn, out_grad, hidden_in, n1, q, k, v, p,
        norm_gain_one, norm_gain_two, w_router, w_out, w_qkv,
    )
    tableg = table_grad(ds, rel_buckets.T)
    layer_out = combine(out_rows, slot, gate, resid)
    gq, gk, gv, outg, tableg, gain1g, gain2g, routerg = lax.psum(
        (gq, gk, gv, outg, tableg, gain1g, gain2g, routerg), AXES
    )
    return (
        layer_out, in_grad, gain1g.reshape(width), jnp.concatenate((gq, gk, gv), axis=1), outg,
        tableg, gain2g.reshape(width), routerg, grad_w_in[None], grad_w_down[None],
    )


def solution(mesh):
    split = P(AXES, None)
    cube = P(AXES, None, None)
    return jax.shard_map(
        local,
        mesh=mesh,
        in_specs=(
            split, P(), P(), P(), P(), P(), P(), cube, cube, split, split, P(), split,
        ),
        out_specs=(split, split, P(), P(), P(), P(), P(), P(), cube, cube),
        check_vma=False,
    )
```

```python
import functools
import jax
import jax.numpy as jnp
from jax import lax
from jax.experimental import pallas as pl
from jax.experimental.pallas import tpu as pltpu
from jax.sharding import PartitionSpec as P

HEADS = 12
HEAD_DIM = 64
LEN = 512
BUCKETS = 32
EPS = 1e-06
LANES = 128
HALF = 256
GROUP = 4
PAIR = 2
GROUPS = HEADS // GROUP
GW = GROUP * HEAD_DIM
F32 = jnp.float32
BF16 = jnp.bfloat16
MIB = 1024 * 1024
MICRO = 1150000000


def dot_nn(a, b):
    return lax.dot_general(a, b, (((1,), (0,)), ((), ())), preferred_element_type=F32)


def dot_tn(a, b):
    return lax.dot_general(a, b, (((0,), (0,)), ((), ())), preferred_element_type=F32)


def dot_nt(a, b):
    return lax.dot_general(a, b, (((1,), (1,)), ((), ())), preferred_element_type=F32)


def whole(shape):
    rank = len(shape)
    return pl.BlockSpec(shape, lambda *g: (0,) * rank, pipeline_mode=pl.Buffered(1))


def split3(v):
    high = v.astype(BF16)
    rest = v - high.astype(F32)
    mid = rest.astype(BF16)
    low = (rest - mid.astype(F32)).astype(BF16)
    return high, mid, low


def slots_kernel(experts, cap, capp, ids_ref, g_ref, slot_ref, pos_ref, packed_ref):
    tok = ids_ref.shape[1]
    ids = ids_ref[...]
    hot = lax.broadcasted_iota(jnp.int32, (experts, tok), 0) == ids
    before = (
        lax.broadcasted_iota(jnp.int32, (tok, tok), 0)
        < lax.broadcasted_iota(jnp.int32, (tok, tok), 1)
    )
    counts = dot_nn(hot.astype(F32).astype(BF16), before.astype(F32).astype(BF16))
    pos = jnp.sum(jnp.where(hot, counts, 0.0), axis=0, keepdims=True).astype(jnp.int32)
    kept = pos < cap
    slot = jnp.where(kept, ids * capp + pos, -1)
    slot_ref[...] = slot
    pos_ref[...] = jnp.where(kept, pos, -1)
    rows = packed_ref.shape[0]
    step = 256

    @pl.loop(0, rows // step)
    def _(r):
        base = pl.multiple_of(r * step, step)
        table = (lax.broadcasted_iota(jnp.int32, (step, tok), 0) + base == slot)
        packed_ref[pl.ds(base, step), :] = dot_nn(
            table.astype(F32).astype(BF16), g_ref[...]
        ).astype(BF16)


def make_slots(experts, cap, capp, ids_row, g):
    tok, width = g.shape
    return pl.pallas_call(
        functools.partial(slots_kernel, experts, cap, capp),
        out_shape=(
            jax.ShapeDtypeStruct((1, tok), jnp.int32),
            jax.ShapeDtypeStruct((1, tok), jnp.int32),
            jax.ShapeDtypeStruct((experts * capp, width), BF16),
        ),
        compiler_params=pltpu.CompilerParams(vmem_limit_bytes=40 * MIB),
        cost_estimate=pl.CostEstimate(flops=5 * MICRO, bytes_accessed=4 * MIB, transcendentals=0),
        name="slots",
    )(ids_row, g)


def front_kernel(
    hid_ref, gain1_ref, wq_ref, wk_ref, wv_ref, wout_ref, tab_ref, gain2_ref, wr_ref,
    ids_ref, slot_ref, pos_ref, segr_ref, segc_ref, rel_ref,
    n1_ref, q_ref, k_ref, v_ref, p_ref, attn_ref, resid_ref, n2_ref, route_ref, gate_ref,
    packed_ref, gpack_ref,
    relt, mask, bias,
):
    step = pl.program_id(0)
    seqs = segr_ref.shape[0]
    tok = hid_ref.shape[0]

    @pl.when(step == 0)
    def _():
        for t in range(0, tok, HALF):
            x = hid_ref[t:t + HALF, :].astype(F32).T
            scale = lax.rsqrt(jnp.mean(x * x, axis=0, keepdims=True) + EPS)
            n1_ref[:, t:t + HALF] = (x * scale * gain1_ref[...]).astype(BF16)
        relt[...] = rel_ref[...].T
        for s in range(seqs):
            mask[s] = jnp.where(segc_ref[s] == segr_ref[s], 0.0, -1000000000.0)

    for w_ref, o_ref in ((wq_ref, q_ref), (wk_ref, k_ref), (wv_ref, v_ref)):
        o_ref[...] = dot_tn(w_ref[...], n1_ref[...]).astype(BF16)

    @pl.loop(0, GROUP)
    def _(h):
        head = step * GROUP + h
        row = tab_ref[pl.ds(head, 1), :]
        line = jnp.broadcast_to(row, (LEN, LANES))
        for c in range(0, LEN, LANES):
            bias[:, c:c + LANES] = jnp.take_along_axis(line, relt[:, c:c + LANES], axis=1)
        at = pl.ds(pl.multiple_of(h * HEAD_DIM, HEAD_DIM), HEAD_DIM)
        out_at = pl.ds(pl.multiple_of(head * HEAD_DIM, HEAD_DIM), HEAD_DIM)
        for s in range(seqs):
            key = k_ref[at, s * LEN:(s + 1) * LEN]
            value = v_ref[at, s * LEN:(s + 1) * LEN]
            for c in range(0, LEN, HALF):
                cols = slice(s * LEN + c, s * LEN + c + HALF)
                query = q_ref[at, cols] * jnp.asarray(HEAD_DIM ** -0.5, BF16)
                score = dot_tn(key, query) + bias[:, c:c + HALF] + mask[s, :, c:c + HALF]
                peak = jnp.max(score, axis=0, keepdims=True)
                weight = jnp.exp(score - peak)
                total = jnp.sum(weight, axis=0, keepdims=True)
                prob = (weight * (1.0 / total)).astype(BF16)
                p_ref[h, s, :, c:c + HALF] = prob
                attn_ref[out_at, cols] = dot_nn(value, prob).astype(BF16)

    @pl.when(step == pl.num_programs(0) - 1)
    def _():
        experts = route_ref.shape[0]
        for t in range(0, tok, HALF):
            cols = slice(t, t + HALF)
            x = hid_ref[t:t + HALF, :].astype(F32).T
            resid = x + dot_tn(wout_ref[...], attn_ref[:, cols])
            resid_ref[:, cols] = resid
            scale = lax.rsqrt(jnp.mean(resid * resid, axis=0, keepdims=True) + EPS)
            n2 = (resid * scale * gain2_ref[...]).astype(BF16)
            n2_ref[:, cols] = n2
            logits = dot_tn(wr_ref[...], n2)
            top = jnp.max(logits, axis=0, keepdims=True)
            e = jnp.exp(logits - top)
            route = e / jnp.sum(e, axis=0, keepdims=True)
            route_ref[:, cols] = route
            hot = lax.broadcasted_iota(jnp.int32, (experts, HALF), 0) == ids_ref[:, cols]
            gate_ref[:, cols] = jnp.sum(jnp.where(hot, route, 0.0), axis=0, keepdims=True)
        hot = lax.broadcasted_iota(jnp.int32, (experts, tok), 0) == ids_ref[...]
        gates = jnp.where(hot, gate_ref[...], 0.0)
        place = (
            lax.broadcasted_iota(jnp.int32, (LANES, tok), 0) == pos_ref[...]
        ).astype(F32).astype(BF16)
        parts = [dot_nt(part, place) for part in split3(gates)]
        which = lax.broadcasted_iota(jnp.int32, (experts, 8, LANES), 1)
        spread = [jnp.broadcast_to(part[:, None, :], which.shape) for part in parts]
        gpack_ref[...] = jnp.where(
            which == 0, spread[0],
            jnp.where(which == 1, spread[1], jnp.where(which == 2, spread[2], 0.0)),
        ).astype(BF16)
        rows = packed_ref.shape[0]

        @pl.loop(0, rows // HALF)
        def _(r):
            base = pl.multiple_of(r * HALF, HALF)
            table = (lax.broadcasted_iota(jnp.int32, (HALF, tok), 0) + base == slot_ref[...])
            packed_ref[pl.ds(base, HALF), :] = dot_nt(
                table.astype(F32).astype(BF16), n2_ref[...]
            ).astype(BF16)


def front(hidden, gain1, w_qkv, w_out, table, gain2, w_router, ids, slot, pos, seg, rel, rows):
    tok, width = hidden.shape
    experts = w_router.shape[1]
    seqs = seg.shape[0]
    wspec = lambda part: pl.BlockSpec((width, GW), lambda i: (0, part * GROUPS + i))
    qspec = pl.BlockSpec((GW, tok), lambda i: (i, 0))
    sd = jax.ShapeDtypeStruct
    outs = (
        sd((width, tok), BF16), sd((width, tok), BF16), sd((width, tok), BF16),
        sd((width, tok), BF16), sd((HEADS, seqs, LEN, LEN), BF16), sd((width, tok), BF16),
        sd((width, tok), F32), sd((width, tok), BF16), sd((experts, tok), F32), sd((1, tok), F32),
        sd((rows, width), BF16), sd((experts, 8, LANES), BF16),
    )
    return pl.pallas_call(
        front_kernel,
        grid=(GROUPS,),
        in_specs=[
            whole((tok, width)), whole((width, 1)), wspec(0), wspec(1), wspec(2),
            whole((width, width)), whole((HEADS, LANES)), whole((width, 1)),
            whole((width, experts)), whole((1, tok)), whole((1, tok)), whole((1, tok)),
            whole((seqs, 1, LEN)), whole((seqs, LEN, 1)), whole((LEN, LEN)),
        ],
        out_specs=(
            whole((width, tok)), qspec, qspec, qspec,
            pl.BlockSpec((GROUP, seqs, LEN, LEN), lambda i: (i, 0, 0, 0)),
            whole((width, tok)), whole((width, tok)), whole((width, tok)),
            whole((experts, tok)), whole((1, tok)), whole((rows, width)),
            whole((experts, 8, LANES)),
        ),
        out_shape=outs,
        scratch_shapes=[
            pltpu.VMEM((LEN, LEN), jnp.int32),
            pltpu.VMEM((seqs, LEN, LEN), F32),
            pltpu.VMEM((LEN, LEN), F32),
        ],
        compiler_params=pltpu.CompilerParams(vmem_limit_bytes=58 * MIB),
        cost_estimate=pl.CostEstimate(flops=50 * MICRO, bytes_accessed=30 * MIB, transcendentals=0),
        name="front",
    )(
        hidden, gain1.reshape(width, 1), w_qkv, w_qkv, w_qkv, w_out, table,
        gain2.reshape(width, 1), w_router, ids, slot, pos,
        seg.reshape(seqs, 1, LEN), seg.reshape(seqs, LEN, 1), rel,
    )


def combine_kernel(rows_ref, slot_ref, gate_ref, resid_ref, out_ref):
    total = rows_ref.shape[0]
    cols = slot_ref.shape[1]
    table = lax.broadcasted_iota(jnp.int32, (total, cols), 0) == slot_ref[...]
    combined = dot_tn(rows_ref[...], table.astype(F32).astype(BF16))
    out_ref[...] = (resid_ref[...] + gate_ref[...] * combined).T.astype(BF16)


def combine(rows, slot, gate, resid):
    total, width = rows.shape
    tok = slot.shape[1]
    line = pl.BlockSpec((1, HALF), lambda i: (0, i))
    return pl.pallas_call(
        combine_kernel,
        grid=(tok // HALF,),
        in_specs=[
            whole((total, width)), line, line, pl.BlockSpec((width, HALF), lambda i: (0, i)),
        ],
        out_specs=pl.BlockSpec((HALF, width), lambda i: (i, 0)),
        out_shape=jax.ShapeDtypeStruct((tok, width), BF16),
        compiler_params=pltpu.CompilerParams(vmem_limit_bytes=40 * MIB),
        cost_estimate=pl.CostEstimate(flops=6 * MICRO, bytes_accessed=8 * MIB, transcendentals=0),
        name="combine",
    )(rows, slot, gate, resid)


def norm_back(grad, source, gain):
    scale = lax.rsqrt(jnp.mean(source * source, axis=0, keepdims=True) + EPS)
    normed = source * scale
    scaled = grad * gain
    inner = jnp.mean(scaled * normed, axis=0, keepdims=True)
    return scale * (scaled - normed * inner), jnp.sum(grad * normed, axis=1, keepdims=True)


def back_kernel(
    dx_ref, gg_ref, slot_ref, pos_ref, ids_ref, route_ref, gate_ref, resid_ref, n2_ref, attn_ref,
    g_ref, hid_ref, n1_ref, q_ref, k_ref, v_ref, p_ref, gain1_ref, gain2_ref, wr_ref, wout_ref,
    wq_ref, wk_ref, wv_ref,
    ingrad_ref, gain1g_ref, gq_ref, gk_ref, gv_ref, outg_ref, gain2g_ref, routerg_ref, ds_ref,
    gres, ga, gn1, dq, dk, dv,
):
    step = pl.program_id(0)
    pair = pl.program_id(1)
    tok = hid_ref.shape[0]
    seqs = tok // LEN
    experts = route_ref.shape[0]
    total = dx_ref.shape[0]

    @pl.when((step == 0) & (pair == 0))
    def _():
        hot = lax.broadcasted_iota(jnp.int32, (experts, tok), 0) == ids_ref[...]
        place = (
            lax.broadcasted_iota(jnp.int32, (LANES, tok), 0) == pos_ref[...]
        ).astype(F32).astype(BF16)
        found = dot_nn(gg_ref[...].reshape(experts * 8, LANES), place)
        found = jnp.sum(found.reshape(experts, 8, tok), axis=1)
        grad_gate = jnp.sum(jnp.where(hot, found, 0.0), axis=0, keepdims=True)
        grad_logits = (
            (grad_gate * gate_ref[...]) * (hot.astype(F32) - route_ref[...])
        ).astype(BF16)
        routerg_ref[...] = dot_nt(grad_logits, n2_ref[...]).astype(BF16)
        gain_grad = jnp.zeros(gain2g_ref.shape, F32)
        for t in range(0, tok, HALF):
            cols = slice(t, t + HALF)
            table = lax.broadcasted_iota(jnp.int32, (total, HALF), 0) == slot_ref[:, cols]
            gn2 = dot_tn(dx_ref[...], table.astype(F32).astype(BF16))
            gn2 = gn2 + dot_nn(wr_ref[...], grad_logits[:, cols])
            branch, part = norm_back(gn2, resid_ref[:, cols], gain2_ref[...])
            gain_grad = gain_grad + part
            gr = g_ref[t:t + HALF, :].astype(F32).T + branch
            gres[:, cols] = gr
            ga[:, cols] = gr.astype(BF16)
        gain2g_ref[...] = gain_grad
        outg_ref[...] = dot_nt(attn_ref[...], ga[...]).astype(BF16)
        for t in range(0, tok, HALF):
            cols = slice(t, t + HALF)
            ga[:, cols] = dot_nn(wout_ref[...], ga[:, cols]).astype(BF16)
        gn1[...] = jnp.zeros_like(gn1)

    @pl.loop(0, PAIR)
    def _(h):
        inside = pair * PAIR + h
        head = step * GROUP + inside
        at = pl.ds(pl.multiple_of(inside * HEAD_DIM, HEAD_DIM), HEAD_DIM)
        all_at = pl.ds(pl.multiple_of(head * HEAD_DIM, HEAD_DIM), HEAD_DIM)
        for s in range(seqs):
            row = slice(s * LEN, (s + 1) * LEN)
            value = v_ref[at, row]
            for c in range(0, LEN, HALF):
                cols = slice(s * LEN + c, s * LEN + c + HALF)
                grad = ga[all_at, cols]
                inner = jnp.sum(
                    grad.astype(F32) * attn_ref[all_at, cols].astype(F32), axis=0, keepdims=True
                )
                gp = dot_tn(value, grad)
                ds_ref[h, s, :, c:c + HALF] = (
                    p_ref[h, s, :, c:c + HALF].astype(F32) * (gp - inner)
                ).astype(BF16)
            ds = ds_ref[h, s]
            dv[at, row] = dot_nt(ga[all_at, row], p_ref[h, s]).astype(BF16)
            factor = HEAD_DIM ** -0.5
            dq[at, row] = (dot_nn(k_ref[at, row], ds) * factor).astype(BF16)
            dk[at, row] = (dot_nt(q_ref[at, row], ds) * factor).astype(BF16)

    @pl.when(pair == pl.num_programs(1) - 1)
    def _():
        for d, o_ref, w_ref in ((dq, gq_ref, wq_ref), (dk, gk_ref, wk_ref), (dv, gv_ref, wv_ref)):
            o_ref[...] = dot_nt(n1_ref[...], d[...]).astype(BF16)
            gn1[...] += dot_nn(w_ref[...], d[...])

    @pl.when((step == pl.num_programs(0) - 1) & (pair == pl.num_programs(1) - 1))
    def _():
        gain_grad = jnp.zeros(gain1g_ref.shape, F32)
        for t in range(0, tok, HALF):
            cols = slice(t, t + HALF)
            x = hid_ref[t:t + HALF, :].astype(F32).T
            branch, part = norm_back(gn1[:, cols], x, gain1_ref[...])
            gain_grad = gain_grad + part
            ingrad_ref[t:t + HALF, :] = (gres[:, cols] + branch).T
        gain1g_ref[...] = gain_grad


def back(dx, gg, slot, pos, ids, route, gate, resid, n2, attn, g, hidden, n1, q, k, v, p, gain1, gain2,
         w_router, w_out, w_qkv):
    tok, width = hidden.shape
    experts = w_router.shape[1]
    total = dx.shape[0]
    seqs = p.shape[1]
    wspec = lambda part: pl.BlockSpec((width, GW), lambda i, j: (0, part * GROUPS + i))
    qspec = pl.BlockSpec((GW, tok), lambda i, j: (i, 0))
    pspec = pl.BlockSpec((PAIR, seqs, LEN, LEN), lambda i, j: (i * (GROUP // PAIR) + j, 0, 0, 0))
    gspec = pl.BlockSpec((width, GW), lambda i, j: (0, i))
    sd = jax.ShapeDtypeStruct
    return pl.pallas_call(
        back_kernel,
        grid=(GROUPS, GROUP // PAIR),
        in_specs=[
            whole((total, width)), whole((experts, 8, LANES)), whole((1, tok)), whole((1, tok)),
            whole((1, tok)), whole((experts, tok)), whole((1, tok)), whole((width, tok)),
            whole((width, tok)), whole((width, tok)), whole((tok, width)), whole((tok, width)),
            whole((width, tok)), qspec, qspec, qspec, pspec, whole((width, 1)), whole((width, 1)),
            whole((width, experts)), whole((width, width)), wspec(0), wspec(1), wspec(2),
        ],
        out_specs=(
            whole((tok, width)), whole((width, 1)), gspec, gspec, gspec, whole((width, width)),
            whole((width, 1)), whole((experts, width)), pspec,
        ),
        out_shape=(
            sd((tok, width), F32), sd((width, 1), F32), sd((width, width), BF16),
            sd((width, width), BF16), sd((width, width), BF16), sd((width, width), BF16),
            sd((width, 1), F32), sd((experts, width), BF16), sd((HEADS, seqs, LEN, LEN), BF16),
        ),
        scratch_shapes=[
            pltpu.VMEM((width, tok), F32), pltpu.VMEM((width, tok), BF16),
            pltpu.VMEM((width, tok), F32), pltpu.VMEM((GW, tok), BF16),
            pltpu.VMEM((GW, tok), BF16), pltpu.VMEM((GW, tok), BF16),
        ],
        compiler_params=pltpu.CompilerParams(vmem_limit_bytes=62 * MIB),
        cost_estimate=pl.CostEstimate(flops=46 * MICRO, bytes_accessed=50 * MIB, transcendentals=0),
        name="back",
    )(
        dx, gg, slot, pos, ids, route, gate, resid, n2, attn, g, hidden, n1, q, k, v, p,
        gain1.reshape(width, 1), gain2.reshape(width, 1), w_router, w_out, w_qkv, w_qkv, w_qkv,
    )


TROWS = 16


def table_kernel(ds_ref, rel_ref, out_ref, acc):
    step = pl.program_id(0)
    pairs = ds_ref.shape[0] * ds_ref.shape[1]
    block = ds_ref.shape[2]

    @pl.when(step == 0)
    def _():
        acc[...] = jnp.zeros_like(acc)

    @pl.loop(0, block // TROWS)
    def _(r):
        base = pl.multiple_of(r * TROWS, TROWS)
        lhs = ds_ref[:, :, pl.ds(base, TROWS), :].reshape(pairs * TROWS, LEN)
        rel = rel_ref[pl.ds(base, TROWS), :]
        hot = (
            rel[:, None, :] == lax.broadcasted_iota(jnp.int32, (TROWS, BUCKETS, LEN), 1)
        ).astype(F32).astype(BF16).reshape(TROWS * BUCKETS, LEN)
        acc[...] += dot_nt(lhs, hot)

    @pl.when(step == pl.num_programs(0) - 1)
    def _():
        rows = lax.broadcasted_iota(jnp.int32, acc.shape, 0) % TROWS
        cols = lax.broadcasted_iota(jnp.int32, acc.shape, 1) // BUCKETS
        kept = jnp.where(rows == cols, acc[...], 0.0)
        per_head = jnp.sum(kept.reshape(HEADS, pairs * TROWS // HEADS, acc.shape[1]), axis=1)
        fold = (
            lax.broadcasted_iota(jnp.int32, (BUCKETS, acc.shape[1]), 1) % BUCKETS
            == lax.broadcasted_iota(jnp.int32, (BUCKETS, acc.shape[1]), 0)
        ).astype(F32)
        out_ref[...] = lax.dot_general(
            fold, per_head, (((1,), (1,)), ((), ())), precision=lax.Precision.HIGHEST,
            preferred_element_type=F32,
        )


def table_grad(ds, relt):
    seqs = ds.shape[1]
    block = 128
    return pl.pallas_call(
        table_kernel,
        grid=(LEN // block,),
        in_specs=[
            pl.BlockSpec((HEADS, seqs, block, LEN), lambda i: (0, 0, i, 0)),
            pl.BlockSpec((block, LEN), lambda i: (i, 0)),
        ],
        out_specs=whole((BUCKETS, HEADS)),
        out_shape=jax.ShapeDtypeStruct((BUCKETS, HEADS), F32),
        scratch_shapes=[pltpu.VMEM((HEADS * seqs * TROWS, TROWS * BUCKETS), F32)],
        compiler_params=pltpu.CompilerParams(vmem_limit_bytes=40 * MIB),
        cost_estimate=pl.CostEstimate(flops=14 * MICRO, bytes_accessed=13 * MIB, transcendentals=0),
        name="table_grad",
    )(ds, relt)


CUBE = 0.044715
ROOT = 0.7978845608028654
FTILE = 768


def gelu_pair(x):
    square = x * x
    t = jnp.tanh(ROOT * (x + CUBE * (x * square)))
    half = 0.5 + 0.5 * t
    slope = half + (0.5 * x) * (1.0 - t * t) * (ROOT + (3.0 * CUBE * ROOT) * square)
    return x * half, slope


def device_of(index):
    wide = lax.axis_size("wide")
    return (index // wide, lax.rem(index, wide))


def expert_kernel(
    block,
    packed, gpack, grows, w_in, w_down,
    dx_out, out_out, active_out, ginner_out, gs_out, x_out, gg_out,
    xbuf, gatebuf, gbuf, win, wdown, active, slope, ginner, gs, dx, outs, ggsend, ggbuf,
    x_send, x_recv, gate_send, gate_recv, gg_ssem, gg_rsem, self_sem, load_sem, store_sem,
):
    count = lax.axis_size("narrow") * lax.axis_size("wide")
    me = lax.axis_index("narrow") * lax.axis_size("wide") + lax.axis_index("wide")
    blocks = count // block
    mine = me // block
    capp = packed.shape[1]
    rows = block * capp
    hidden = w_in.shape[1]
    mesh_id = pl.DeviceIdType.MESH

    def x_copy(target, source):
        return pltpu.make_async_remote_copy(
            src_ref=packed.at[target], dst_ref=xbuf.at[source], send_sem=x_send.at[target],
            recv_sem=x_recv.at[source], device_id=device_of(target), device_id_type=mesh_id,
        )

    def gate_copy(target, source):
        return pltpu.make_async_remote_copy(
            src_ref=gpack.at[target], dst_ref=gatebuf.at[source], send_sem=gate_send.at[target],
            recv_sem=gate_recv.at[source], device_id=device_of(target), device_id_type=mesh_id,
        )

    def gg_copy(target, source):
        return pltpu.make_async_remote_copy(
            src_ref=ggsend.at[target], dst_ref=ggbuf.at[source], send_sem=gg_ssem.at[target],
            recv_sem=gg_rsem.at[source], device_id=device_of(target), device_id_type=mesh_id,
        )

    barrier = pltpu.get_barrier_semaphore()

    @pl.loop(1, count)
    def _(s):
        pl.semaphore_signal(
            barrier, inc=1, device_id=device_of(lax.rem(me + s, count)), device_id_type=mesh_id
        )

    loads = [
        pltpu.make_async_copy(w_in, win, load_sem.at[0]),
        pltpu.make_async_copy(w_down, wdown, load_sem.at[1]),
        pltpu.make_async_copy(grows, gbuf, load_sem.at[2]),
    ]
    own = [
        pltpu.make_async_copy(packed.at[me], xbuf.at[me], self_sem.at[0]),
        pltpu.make_async_copy(gpack.at[me], gatebuf.at[me], self_sem.at[1]),
    ]
    pl.semaphore_wait(barrier, count - 1)

    @pl.loop(0, blocks)
    def _(c):
        there = lax.rem(mine + blocks - c, blocks)

        @pl.loop(0, block)
        def _(j):
            target = there * block + j

            @pl.when(target != me)
            def _():
                gate_copy(target, me).start()
                x_copy(target, me).start()

    for copy in own + loads:
        copy.start()
    for copy in own + loads:
        copy.wait()

    def stores(at):
        return [
            pltpu.make_async_copy(dx.at[at], dx_out.at[at], store_sem.at[0]),
            pltpu.make_async_copy(outs.at[at], out_out.at[at], store_sem.at[1]),
            pltpu.make_async_copy(active.at[at], active_out.at[at], store_sem.at[2]),
            pltpu.make_async_copy(ginner.at[at], ginner_out.at[at], store_sem.at[3]),
            pltpu.make_async_copy(gs.at[at], gs_out.at[at], store_sem.at[4]),
        ]

    @pl.loop(0, blocks)
    def _(c):
        here = lax.rem(mine + c, blocks)
        first = here * block

        @pl.loop(0, block)
        def _(j):
            source = first + j

            @pl.when(source != me)
            def _():
                gate_copy(me, source).wait_recv()
                x_copy(me, source).wait_recv()

        at = pl.ds(pl.multiple_of(here * rows, rows), rows)
        group = pl.ds(first, block)
        x = xbuf[group].reshape(rows, xbuf.shape[2])

        @pl.loop(0, hidden // FTILE)
        def _(f):
            tile = pl.ds(pl.multiple_of(f * FTILE, FTILE), FTILE)
            value, grad = gelu_pair(dot_nn(x, win[:, tile]))
            active[at, tile] = value.astype(BF16)
            slope[:, tile] = grad

        result = dot_nn(active[at, :], wdown[...]).astype(BF16)
        outs[at, :] = result
        g = gbuf[group].astype(F32)
        diag = (
            lax.broadcasted_iota(jnp.int32, (block, capp, LANES), 1)
            == lax.broadcasted_iota(jnp.int32, (block, capp, LANES), 2)
        )
        gate = jnp.sum(gatebuf[group].astype(F32), axis=1)
        gate = jnp.sum(
            jnp.where(diag, gate[:, None, :], 0.0), axis=2, keepdims=True
        )
        gs[at, :] = (gate * g).astype(BF16).reshape(rows, g.shape[2])
        gg = jnp.sum(g * result.astype(F32).reshape(g.shape), axis=2, keepdims=True)
        gg = jnp.sum(jnp.where(diag, gg, 0.0), axis=1)
        which = lax.broadcasted_iota(jnp.int32, (block, 8, LANES), 1)
        high, mid, low = [part.astype(F32)[:, None, :] for part in split3(gg)]
        ggsend[group] = jnp.where(
            which == 0, high, jnp.where(which == 1, mid, jnp.where(which == 2, low, 0.0))
        ).astype(BF16)

        @pl.loop(0, block)
        def _(j):
            source = first + j

            @pl.when(source != me)
            def _():
                gg_copy(source, me).start()

        @pl.loop(0, hidden // FTILE)
        def _(f):
            tile = pl.ds(pl.multiple_of(f * FTILE, FTILE), FTILE)
            grad = dot_nt(gs[at, :], wdown[tile, :])
            ginner[at, tile] = (grad * slope[:, tile]).astype(BF16)

        dx[at, :] = dot_nt(ginner[at, :], win[...]).astype(BF16)

        @pl.when(c > 0)
        def _():
            for copy in stores(at):
                copy.wait()

        for copy in stores(at):
            copy.start()

    for copy in stores(pl.ds(0, rows)):
        copy.wait()
    keep = [
        pltpu.make_async_copy(xbuf, x_out, load_sem.at[0]),
        pltpu.make_async_copy(ggsend.at[me], ggbuf.at[me], self_sem.at[0]),
    ]
    for copy in keep:
        copy.start()

    @pl.loop(0, count)
    def _(other):
        @pl.when(other != me)
        def _():
            x_copy(other, me).wait_send()
            gate_copy(other, me).wait_send()
            gg_copy(other, me).wait_send()
            gg_copy(me, other).wait_recv()

    for copy in keep:
        copy.wait()
    last = pltpu.make_async_copy(ggbuf, gg_out, load_sem.at[1])
    last.start()
    last.wait()


def expert(packed, gpack, grows, w_in, w_down):
    count, capp, width = packed.shape
    hidden = w_in.shape[1]
    block = 1
    while block * 2 <= count and block * 2 * capp <= 320:
        block *= 2
    rows = block * capp
    total = count * capp
    sd = jax.ShapeDtypeStruct
    anyspec = pl.BlockSpec(memory_space=pl.ANY)
    dma = pltpu.SemaphoreType.DMA
    return pl.pallas_call(
        functools.partial(expert_kernel, block),
        in_specs=[anyspec] * 5,
        out_specs=(anyspec,) * 7,
        out_shape=(
            sd((total, width), BF16), sd((total, width), BF16), sd((total, hidden), BF16),
            sd((total, hidden), BF16), sd((total, width), BF16), sd((count, capp, width), BF16),
            sd((count, 8, LANES), BF16),
        ),
        scratch_shapes=[
            pltpu.VMEM((count, capp, width), BF16), pltpu.VMEM((count, 8, LANES), BF16),
            pltpu.VMEM((count, capp, width), BF16), pltpu.VMEM((width, hidden), BF16),
            pltpu.VMEM((hidden, width), BF16), pltpu.VMEM((total, hidden), BF16),
            pltpu.VMEM((rows, hidden), F32), pltpu.VMEM((total, hidden), BF16),
            pltpu.VMEM((total, width), BF16), pltpu.VMEM((total, width), BF16),
            pltpu.VMEM((total, width), BF16), pltpu.VMEM((count, 8, LANES), BF16),
            pltpu.VMEM((count, 8, LANES), BF16),
            dma((count,)), dma((count,)), dma((count,)), dma((count,)), dma((count,)), dma((count,)),
            dma((2,)), dma((3,)), dma((5,)),
        ],
        compiler_params=pltpu.CompilerParams(
            collective_id=0, has_side_effects=True, vmem_limit_bytes=62 * MIB
        ),
        cost_estimate=pl.CostEstimate(flops=60 * MICRO, bytes_accessed=60 * 1024 * 1024, transcendentals=0),
        name="expert",
    )(packed, gpack, grows, w_in, w_down)


def weights_kernel(active_ref, gs_ref, x_ref, ginner_ref, down_ref, in_ref, xt):
    @pl.when(pl.program_id(0) == 0)
    def _():
        total = x_ref.shape[0]
        for t in range(0, total, HALF):
            xt[:, t:t + HALF] = x_ref[t:t + HALF, :].T

    down_ref[0] = dot_tn(active_ref[...], gs_ref[...])
    in_ref[0] = dot_nn(xt[...], ginner_ref[...])


def weight_grads(active, gs, x, ginner):
    total, hidden = active.shape
    width = gs.shape[1]
    tile = HALF
    cols = pl.BlockSpec((total, tile), lambda i: (0, i))
    return pl.pallas_call(
        weights_kernel,
        grid=(hidden // tile,),
        in_specs=[cols, whole((total, width)), whole((total, width)), cols],
        out_specs=(
            pl.BlockSpec((1, tile, width), lambda i: (0, i, 0)),
            pl.BlockSpec((1, width, tile), lambda i: (0, 0, i)),
        ),
        out_shape=(
            jax.ShapeDtypeStruct((1, hidden, width), F32),
            jax.ShapeDtypeStruct((1, width, hidden), F32),
        ),
        scratch_shapes=[pltpu.VMEM((width, total), BF16)],
        compiler_params=pltpu.CompilerParams(vmem_limit_bytes=40 * MIB),
        cost_estimate=pl.CostEstimate(flops=18 * MICRO, bytes_accessed=36 * 1024 * 1024, transcendentals=0),
        name="weight_grads",
    )(active, gs, x, ginner)


PIECES = 32
SMALL = 24


def reduce_kernel(
    a, b, c, d, router, small, sums_out, router_out, small_out,
    own, full, got0, got1, got2, got3, extra, rown, rgot, sown, sgot,
    send, recv, xsend, xrecv, tsend, trecv, load_sem, store_sem,
):
    narrow_n, wide_n = lax.axis_size("narrow"), lax.axis_size("wide")
    n, w = lax.axis_index("narrow"), lax.axis_index("wide")
    core, zed = lax.rem(w, 2), lax.rem(w // 2, 4)
    ex, why = lax.rem(n, 2), lax.rem(n // 2, 2)
    more_n = (narrow_n // 4) * (wide_n // 8)
    more_w = wide_n // 8
    more = (n // 4) * more_w + w // 8
    units = own.shape[0]
    half = own.shape[4]
    mesh_id = pl.DeviceIdType.MESH
    core_dev = (n, w + 1 - 2 * core)
    ex_dev = (n + 1 - 2 * ex, w)
    why_dev = (n + 2 - 4 * why, w)

    def zed_dev(step):
        return (n, w + 2 * (lax.rem(zed + step, 4) - zed))

    def more_dev(step):
        other = lax.rem(more + step, more_n)
        return (n + 4 * (other // more_w - more // more_w),
                w + 8 * (lax.rem(other, more_w) - lax.rem(more, more_w)))

    def spot(q):
        first, second = (ex, why) if q == 0 else (why, ex)
        b16 = core * 16
        b8 = b16 + first * 8
        b4 = b8 + second * 4
        return first, second, b16, b8, b4

    def remote(src, dst, k, u, q, dev):
        return pltpu.make_async_remote_copy(
            src_ref=src, dst_ref=dst, send_sem=send.at[k, u, q], recv_sem=recv.at[k, u, q],
            device_id=dev, device_id_type=mesh_id,
        )

    def outgoing(phase, u, q):
        first, second, b16, b8, b4 = spot(q)
        one, two = (ex_dev, why_dev) if q == 0 else (why_dev, ex_dev)
        if phase == 0:
            return [remote(own.at[u, q, pl.ds(16 - b16, 16)], got0.at[u, q], 0, u, q, core_dev)]
        if phase == 1:
            src = own.at[u, q, pl.ds(b16 + (1 - first) * 8, 8)]
            return [remote(src, got1.at[u, q], 1, u, q, one)]
        if phase == 2:
            src = own.at[u, q, pl.ds(b8 + (1 - second) * 4, 4)]
            return [remote(src, got2.at[u, q], 2, u, q, two)]
        if phase == 3:
            return [
                remote(own.at[u, q, b4 + lax.rem(zed + step, 4)], got3.at[u, q, step - 1],
                       2 + step, u, q, zed_dev(step))
                for step in (1, 2, 3)
            ]
        if phase == 4:
            mine = full.at[u, q, b4 + zed]
            return [remote(mine, mine, 5 + step, u, q, zed_dev(step)) for step in (1, 2, 3)]
        if phase == 5:
            mine = full.at[u, q, pl.ds(b4, 4)]
            return [remote(mine, mine, 9, u, q, two)]
        if phase == 6:
            mine = full.at[u, q, pl.ds(b8, 8)]
            return [remote(mine, mine, 10, u, q, one)]
        mine = full.at[u, q, pl.ds(b16, 16)]
        return [remote(mine, mine, 11, u, q, core_dev)]

    def incoming(phase, u, q):
        first, second, b16, b8, b4 = spot(q)
        if phase < 4:
            return outgoing(phase, u, q)
        if phase == 4:
            return [
                remote(full.at[u, q, b4 + zed], full.at[u, q, b4 + lax.rem(zed + 4 - step, 4)],
                       5 + step, u, q, zed_dev(step))
                for step in (1, 2, 3)
            ]
        if phase == 5:
            there = full.at[u, q, pl.ds(b8 + (1 - second) * 4, 4)]
            return [remote(there, there, 9, u, q, core_dev)]
        if phase == 6:
            there = full.at[u, q, pl.ds(b16 + (1 - first) * 8, 8)]
            return [remote(there, there, 10, u, q, core_dev)]
        there = full.at[u, q, pl.ds(16 - b16, 16)]
        return [remote(there, there, 11, u, q, core_dev)]

    def add(u, q, start, count, got):
        @pl.loop(0, count)
        def _(i):
            own[u, q, start + i] = (
                own[u, q, start + i].astype(F32) + got[u, q, i].astype(F32)
            ).astype(BF16)

    def spread(u, q, place):
        extra[u, q, more] = full[u, q, place]
        copies = [
            pltpu.make_async_remote_copy(
                src_ref=extra.at[u, q, more], dst_ref=extra.at[u, q, more],
                send_sem=xsend.at[u, q, step], recv_sem=xrecv.at[u, q, step],
                device_id=more_dev(step), device_id_type=mesh_id,
            )
            for step in range(1, more_n)
        ]
        for copy in copies:
            copy.start()
        for step in range(1, more_n):
            other = lax.rem(more + more_n - step, more_n)
            pltpu.make_async_remote_copy(
                src_ref=extra.at[u, q, more], dst_ref=extra.at[u, q, other],
                send_sem=xsend.at[u, q, step], recv_sem=xrecv.at[u, q, step],
                device_id=more_dev(step), device_id_type=mesh_id,
            ).wait_recv()
        for copy in copies:
            copy.wait_send()
        total = extra[u, q, 0].astype(F32)
        for i in range(1, more_n):
            total = total + extra[u, q, i].astype(F32)
        full[u, q, place] = total.astype(BF16)

    def fold(phase, u, q):
        first, second, b16, b8, b4 = spot(q)
        if phase == 0:
            add(u, q, b16, 16, got0)
        elif phase == 1:
            add(u, q, b8, 8, got1)
        elif phase == 2:
            add(u, q, b4, 4, got2)
        elif phase == 3:
            place = b4 + zed
            full[u, q, place] = (
                own[u, q, place].astype(F32) + got3[u, q, 0].astype(F32)
                + (got3[u, q, 1].astype(F32) + got3[u, q, 2].astype(F32))
            ).astype(BF16)
            if more_n > 1:
                spread(u, q, place)

    bits = []
    for axis, count in (("wide", wide_n), ("narrow", narrow_n)):
        size = 1
        while size < count:
            at = lax.rem((w if axis == "wide" else n) // size, 2)
            move = size - 2 * size * at
            bits.append((n, w + move) if axis == "wide" else (n + move, w))
            size *= 2

    def tail_copies(level):
        return [
            pltpu.make_async_remote_copy(
                src_ref=src.at[level], dst_ref=dst.at[level], send_sem=tsend.at[level, k],
                recv_sem=trecv.at[level, k], device_id=bits[level], device_id_type=mesh_id,
            )
            for k, (src, dst) in enumerate(((rown, rgot), (sown, sgot)))
        ]

    inputs = [
        pltpu.make_async_copy(ref.at[:, :, pl.ds(q * half, half)], own.at[u, q], load_sem.at[u, q])
        for u, ref in enumerate((a, b, c, d)) for q in range(2)
    ]
    for copy in inputs:
        copy.start()
    rown[0] = router[...]
    sown[0] = small[...]
    barrier = pltpu.get_barrier_semaphore()
    greet = [core_dev, ex_dev, why_dev] + [zed_dev(step) for step in (1, 2, 3)]
    greet += [more_dev(step) for step in range(1, more_n)] + bits
    for dev in greet:
        pl.semaphore_signal(barrier, inc=1, device_id=dev, device_id_type=mesh_id)
    pl.semaphore_wait(barrier, len(greet))

    for copy in tail_copies(0):
        copy.start()
    for copy in inputs:
        copy.wait()

    @pl.loop(0, units)
    def _(u):
        for q in range(2):
            for copy in outgoing(0, u, q):
                copy.start()

    for phase in range(8):
        @pl.loop(0, units)
        def _(u):
            for q in range(2):
                for copy in incoming(phase, u, q):
                    copy.wait_recv()
                for copy in outgoing(phase, u, q):
                    copy.wait_send()
                fold(phase, u, q)
                if phase < 7:
                    for copy in outgoing(phase + 1, u, q):
                        copy.start()

        if phase < len(bits):
            tail(phase, bits, tail_copies, rown, rgot, sown, sgot)
    for level in range(8, len(bits)):
        tail(level, bits, tail_copies, rown, rgot, sown, sgot)
    outputs = [
        pltpu.make_async_copy(full.at[u, q], sums_out.at[u, :, :, pl.ds(q * half, half)], store_sem.at[u, q])
        for u in range(units) for q in range(2)
    ]
    for copy in outputs:
        copy.start()
    router_out[...] = rown[len(bits)]
    small_out[...] = sown[len(bits)]
    for copy in outputs:
        copy.wait()


def tail(level, bits, tail_copies, rown, rgot, sown, sgot):
    for copy in tail_copies(level):
        copy.wait_recv()
        copy.wait_send()
    rown[level + 1] = (rown[level].astype(F32) + rgot[level].astype(F32)).astype(BF16)
    sown[level + 1] = sown[level] + sgot[level]
    if level + 1 < len(bits):
        for copy in tail_copies(level + 1):
            copy.start()


def reduce_all(a, b, c, d, router, small):
    narrow_n, wide_n = lax.axis_size("narrow"), lax.axis_size("wide")
    levels = (narrow_n * wide_n).bit_length() - 1
    more_n = (narrow_n // 4) * (wide_n // 8)
    width, experts = a.shape[0], router.shape[0]
    rows, half = width // PIECES, width // 2
    units = 4
    a, b, c, d = [v.reshape(PIECES, rows, width) for v in (a, b, c, d)]
    sd = jax.ShapeDtypeStruct
    anyspec = pl.BlockSpec(memory_space=pl.ANY)
    vmem = pl.BlockSpec(memory_space=pltpu.VMEM)
    dma = pltpu.SemaphoreType.DMA
    buf = lambda *lead: pltpu.VMEM((units, 2) + lead + (rows, half), BF16)
    return pl.pallas_call(
        reduce_kernel,
        in_specs=[anyspec] * 4 + [vmem, vmem],
        out_specs=(anyspec, vmem, vmem),
        out_shape=(
            sd((units, PIECES, rows, width), BF16), sd((experts, width), BF16),
            sd((SMALL, LANES), F32),
        ),
        scratch_shapes=[
            buf(PIECES), buf(PIECES), buf(16), buf(8), buf(4), buf(3), buf(more_n),
            pltpu.VMEM((levels + 1, experts, width), BF16),
            pltpu.VMEM((levels, experts, width), BF16),
            pltpu.VMEM((levels + 1, SMALL, LANES), F32), pltpu.VMEM((levels, SMALL, LANES), F32),
            dma((12, units, 2)), dma((12, units, 2)), dma((units, 2, more_n)),
            dma((units, 2, more_n)), dma((levels, 2)), dma((levels, 2)), dma((units, 2)),
            dma((units, 2)),
        ],
        compiler_params=pltpu.CompilerParams(
            collective_id=1, has_side_effects=True, vmem_limit_bytes=50 * MIB
        ),
        cost_estimate=pl.CostEstimate(flops=50 * MICRO, bytes_accessed=20 * MIB, transcendentals=0),
        name="reduce_all",
    )(a, b, c, d, router, small)


def matmul(a, b):
    return jnp.dot(a, b, preferred_element_type=F32)


AXES = ("narrow", "wide")


def exchange(v):
    return lax.all_to_all(v, AXES, split_axis=0, concat_axis=0, tiled=True)


def local(
    hidden_in, norm_gain_one, w_qkv, w_out, pos_table, norm_gain_two, w_router, w_in, w_down,
    expert_ids, segment_ids, rel_buckets, out_grad,
):
    experts = lax.axis_size("narrow") * lax.axis_size("wide")
    tok, width = hidden_in.shape
    cap = max(2, (5 * tok + 4 * experts - 1) // (4 * experts))
    capp = (cap + 7) // 8 * 8
    rows = experts * capp
    ids = expert_ids.reshape(1, tok)
    slot, pos, g_packed = make_slots(experts, cap, capp, ids, out_grad)
    g_rows = exchange(g_packed.reshape(experts, capp, width))
    table = jnp.pad(pos_table.T, ((0, 0), (0, LANES - BUCKETS)))
    (n1, q, k, v, p, attn, resid, n2, route, gate, packed, gpack) = front(
        hidden_in, norm_gain_one, w_qkv, w_out, table, norm_gain_two, w_router, ids, slot, pos,
        segment_ids, rel_buckets, rows,
    )
    dx, out_rows, active, ginner, gs, expert_in, gg = expert(
        packed.reshape(experts, capp, width), gpack, g_rows, w_in[0], w_down[0]
    )
    dx = exchange(dx.reshape(experts, capp, width)).reshape(rows, width)
    grad_w_down, grad_w_in = weight_grads(active, gs, expert_in.reshape(rows, width), ginner)
    dx, out_rows, grad_w_down, grad_w_in = lax.optimization_barrier(
        (dx, out_rows, grad_w_down, grad_w_in)
    )
    out_rows = exchange(out_rows.reshape(experts, capp, width)).reshape(rows, width)
    (in_grad, gain1g, gq, gk, gv, outg, gain2g, routerg, ds) = back(
        dx, gg, slot, pos, ids, route, gate, resid, n2, attn, out_grad, hidden_in, n1, q, k, v, p,
        norm_gain_one, norm_gain_two, w_router, w_out, w_qkv,
    )
    tableg = table_grad(ds, rel_buckets.T)
    lines = width // LANES
    small = jnp.concatenate((
        gain1g.reshape(lines, LANES), gain2g.reshape(lines, LANES),
        jnp.pad(tableg.T, ((0, 0), (0, LANES - BUCKETS))),
    ), axis=0)
    layer_out = combine(out_rows, slot, gate, resid)
    sums, routerg, small = reduce_all(gq, gk, gv, outg, routerg, small)
    sums = sums.reshape(4, width, width).astype(F32)
    return (
        layer_out, in_grad, small[:lines].reshape(width),
        jnp.concatenate((sums[0], sums[1], sums[2]), axis=1), sums[3],
        small[2 * lines:, :BUCKETS].T, small[lines:2 * lines].reshape(width),
        routerg.T.astype(F32), grad_w_in, grad_w_down,
    )


def solution(mesh):
    split = P(AXES, None)
    cube = P(AXES, None, None)
    return jax.shard_map(
        local,
        mesh=mesh,
        in_specs=(
            split, P(), P(), P(), P(), P(), P(), cube, cube, split, split, P(), split,
        ),
        out_specs=(split, split, P(), P(), P(), P(), P(), P(), cube, cube),
        check_vma=False,
    )
```

```python
import functools
import jax
import jax.numpy as jnp
from jax import lax
from jax.experimental import pallas as pl
from jax.experimental.pallas import tpu as pltpu
from jax.sharding import PartitionSpec as P

HEADS = 12
HEAD_DIM = 64
LEN = 512
BUCKETS = 32
EPS = 1e-06
LANES = 128
HALF = 256
GROUP = 4
PAIR = 2
GROUPS = HEADS // GROUP
GW = GROUP * HEAD_DIM
F32 = jnp.float32
BF16 = jnp.bfloat16
MIB = 1024 * 1024
MICRO = 1150000000


def dot_nn(a, b):
    return lax.dot_general(a, b, (((1,), (0,)), ((), ())), preferred_element_type=F32)


def dot_tn(a, b):
    return lax.dot_general(a, b, (((0,), (0,)), ((), ())), preferred_element_type=F32)


def dot_nt(a, b):
    return lax.dot_general(a, b, (((1,), (1,)), ((), ())), preferred_element_type=F32)


def whole(shape):
    rank = len(shape)
    return pl.BlockSpec(shape, lambda *g: (0,) * rank, pipeline_mode=pl.Buffered(1))


def split3(v):
    high = v.astype(BF16)
    rest = v - high.astype(F32)
    mid = rest.astype(BF16)
    low = (rest - mid.astype(F32)).astype(BF16)
    return high, mid, low


def slots_kernel(experts, cap, capp, ids_ref, g_ref, slot_ref, pos_ref, packed_ref):
    tok = ids_ref.shape[1]
    ids = ids_ref[...]
    hot = lax.broadcasted_iota(jnp.int32, (experts, tok), 0) == ids
    before = (
        lax.broadcasted_iota(jnp.int32, (tok, tok), 0)
        < lax.broadcasted_iota(jnp.int32, (tok, tok), 1)
    )
    counts = dot_nn(hot.astype(F32).astype(BF16), before.astype(F32).astype(BF16))
    pos = jnp.sum(jnp.where(hot, counts, 0.0), axis=0, keepdims=True).astype(jnp.int32)
    kept = pos < cap
    slot = jnp.where(kept, ids * capp + pos, -1)
    slot_ref[...] = slot
    pos_ref[...] = jnp.where(kept, pos, -1)
    rows = packed_ref.shape[0]
    step = 256

    @pl.loop(0, rows // step)
    def _(r):
        base = pl.multiple_of(r * step, step)
        table = (lax.broadcasted_iota(jnp.int32, (step, tok), 0) + base == slot)
        packed_ref[pl.ds(base, step), :] = dot_nn(
            table.astype(F32).astype(BF16), g_ref[...]
        ).astype(BF16)


def make_slots(experts, cap, capp, ids_row, g):
    tok, width = g.shape
    return pl.pallas_call(
        functools.partial(slots_kernel, experts, cap, capp),
        out_shape=(
            jax.ShapeDtypeStruct((1, tok), jnp.int32),
            jax.ShapeDtypeStruct((1, tok), jnp.int32),
            jax.ShapeDtypeStruct((experts * capp, width), BF16),
        ),
        compiler_params=pltpu.CompilerParams(vmem_limit_bytes=40 * MIB),
        cost_estimate=pl.CostEstimate(flops=5 * MICRO, bytes_accessed=4 * MIB, transcendentals=0),
        name="slots",
    )(ids_row, g)


def front_kernel(
    hid_ref, gain1_ref, wq_ref, wk_ref, wv_ref, wout_ref, tab_ref, gain2_ref, wr_ref,
    ids_ref, slot_ref, pos_ref, segr_ref, segc_ref, rel_ref,
    n1_ref, q_ref, k_ref, v_ref, p_ref, attn_ref, resid_ref, n2_ref, route_ref, gate_ref,
    packed_ref, gpack_ref,
    relt, mask, bias,
):
    step = pl.program_id(0)
    seqs = segr_ref.shape[0]
    tok = hid_ref.shape[0]

    @pl.when(step == 0)
    def _():
        for t in range(0, tok, HALF):
            x = hid_ref[t:t + HALF, :].astype(F32).T
            scale = lax.rsqrt(jnp.mean(x * x, axis=0, keepdims=True) + EPS)
            n1_ref[:, t:t + HALF] = (x * scale * gain1_ref[...]).astype(BF16)
        relt[...] = rel_ref[...].T
        for s in range(seqs):
            mask[s] = jnp.where(segc_ref[s] == segr_ref[s], 0.0, -1000000000.0)

    for w_ref, o_ref in ((wq_ref, q_ref), (wk_ref, k_ref), (wv_ref, v_ref)):
        o_ref[...] = dot_tn(w_ref[...], n1_ref[...]).astype(BF16)

    @pl.loop(0, GROUP)
    def _(h):
        head = step * GROUP + h
        row = tab_ref[pl.ds(head, 1), :]
        line = jnp.broadcast_to(row, (LEN, LANES))
        for c in range(0, LEN, LANES):
            bias[:, c:c + LANES] = jnp.take_along_axis(line, relt[:, c:c + LANES], axis=1)
        at = pl.ds(pl.multiple_of(h * HEAD_DIM, HEAD_DIM), HEAD_DIM)
        out_at = pl.ds(pl.multiple_of(head * HEAD_DIM, HEAD_DIM), HEAD_DIM)
        for s in range(seqs):
            key = k_ref[at, s * LEN:(s + 1) * LEN]
            value = v_ref[at, s * LEN:(s + 1) * LEN]
            for c in range(0, LEN, HALF):
                cols = slice(s * LEN + c, s * LEN + c + HALF)
                query = q_ref[at, cols] * jnp.asarray(HEAD_DIM ** -0.5, BF16)
                score = dot_tn(key, query) + bias[:, c:c + HALF] + mask[s, :, c:c + HALF]
                peak = jnp.max(score, axis=0, keepdims=True)
                weight = jnp.exp(score - peak)
                total = jnp.sum(weight, axis=0, keepdims=True)
                prob = (weight * (1.0 / total)).astype(BF16)
                p_ref[h, s, :, c:c + HALF] = prob
                attn_ref[out_at, cols] = dot_nn(value, prob).astype(BF16)

    @pl.when(step == pl.num_programs(0) - 1)
    def _():
        experts = route_ref.shape[0]
        for t in range(0, tok, HALF):
            cols = slice(t, t + HALF)
            x = hid_ref[t:t + HALF, :].astype(F32).T
            resid = x + dot_tn(wout_ref[...], attn_ref[:, cols])
            resid_ref[:, cols] = resid
            scale = lax.rsqrt(jnp.mean(resid * resid, axis=0, keepdims=True) + EPS)
            n2 = (resid * scale * gain2_ref[...]).astype(BF16)
            n2_ref[:, cols] = n2
            logits = dot_tn(wr_ref[...], n2)
            top = jnp.max(logits, axis=0, keepdims=True)
            e = jnp.exp(logits - top)
            route = e / jnp.sum(e, axis=0, keepdims=True)
            route_ref[:, cols] = route
            hot = lax.broadcasted_iota(jnp.int32, (experts, HALF), 0) == ids_ref[:, cols]
            gate_ref[:, cols] = jnp.sum(jnp.where(hot, route, 0.0), axis=0, keepdims=True)
        hot = lax.broadcasted_iota(jnp.int32, (experts, tok), 0) == ids_ref[...]
        gates = jnp.where(hot, gate_ref[...], 0.0)
        place = (
            lax.broadcasted_iota(jnp.int32, (LANES, tok), 0) == pos_ref[...]
        ).astype(F32).astype(BF16)
        parts = [dot_nt(part, place) for part in split3(gates)]
        which = lax.broadcasted_iota(jnp.int32, (experts, 8, LANES), 1)
        spread = [jnp.broadcast_to(part[:, None, :], which.shape) for part in parts]
        gpack_ref[...] = jnp.where(
            which == 0, spread[0],
            jnp.where(which == 1, spread[1], jnp.where(which == 2, spread[2], 0.0)),
        ).astype(BF16)
        rows = packed_ref.shape[0]

        @pl.loop(0, rows // HALF)
        def _(r):
            base = pl.multiple_of(r * HALF, HALF)
            table = (lax.broadcasted_iota(jnp.int32, (HALF, tok), 0) + base == slot_ref[...])
            packed_ref[pl.ds(base, HALF), :] = dot_nt(
                table.astype(F32).astype(BF16), n2_ref[...]
            ).astype(BF16)


def front(hidden, gain1, w_qkv, w_out, table, gain2, w_router, ids, slot, pos, seg, rel, rows):
    tok, width = hidden.shape
    experts = w_router.shape[1]
    seqs = seg.shape[0]
    wspec = lambda part: pl.BlockSpec((width, GW), lambda i: (0, part * GROUPS + i))
    qspec = pl.BlockSpec((GW, tok), lambda i: (i, 0))
    sd = jax.ShapeDtypeStruct
    outs = (
        sd((width, tok), BF16), sd((width, tok), BF16), sd((width, tok), BF16),
        sd((width, tok), BF16), sd((HEADS, seqs, LEN, LEN), BF16), sd((width, tok), BF16),
        sd((width, tok), F32), sd((width, tok), BF16), sd((experts, tok), F32), sd((1, tok), F32),
        sd((rows, width), BF16), sd((experts, 8, LANES), BF16),
    )
    return pl.pallas_call(
        front_kernel,
        grid=(GROUPS,),
        in_specs=[
            whole((tok, width)), whole((width, 1)), wspec(0), wspec(1), wspec(2),
            whole((width, width)), whole((HEADS, LANES)), whole((width, 1)),
            whole((width, experts)), whole((1, tok)), whole((1, tok)), whole((1, tok)),
            whole((seqs, 1, LEN)), whole((seqs, LEN, 1)), whole((LEN, LEN)),
        ],
        out_specs=(
            whole((width, tok)), qspec, qspec, qspec,
            pl.BlockSpec((GROUP, seqs, LEN, LEN), lambda i: (i, 0, 0, 0)),
            whole((width, tok)), whole((width, tok)), whole((width, tok)),
            whole((experts, tok)), whole((1, tok)), whole((rows, width)),
            whole((experts, 8, LANES)),
        ),
        out_shape=outs,
        scratch_shapes=[
            pltpu.VMEM((LEN, LEN), jnp.int32),
            pltpu.VMEM((seqs, LEN, LEN), F32),
            pltpu.VMEM((LEN, LEN), F32),
        ],
        compiler_params=pltpu.CompilerParams(vmem_limit_bytes=58 * MIB),
        cost_estimate=pl.CostEstimate(flops=50 * MICRO, bytes_accessed=30 * MIB, transcendentals=0),
        name="front",
    )(
        hidden, gain1.reshape(width, 1), w_qkv, w_qkv, w_qkv, w_out, table,
        gain2.reshape(width, 1), w_router, ids, slot, pos,
        seg.reshape(seqs, 1, LEN), seg.reshape(seqs, LEN, 1), rel,
    )


def combine_kernel(rows_ref, slot_ref, gate_ref, resid_ref, out_ref):
    total = rows_ref.shape[0]
    cols = slot_ref.shape[1]
    table = lax.broadcasted_iota(jnp.int32, (total, cols), 0) == slot_ref[...]
    combined = dot_tn(rows_ref[...], table.astype(F32).astype(BF16))
    out_ref[...] = (resid_ref[...] + gate_ref[...] * combined).T.astype(BF16)


def combine(rows, slot, gate, resid):
    total, width = rows.shape
    tok = slot.shape[1]
    line = pl.BlockSpec((1, HALF), lambda i: (0, i))
    return pl.pallas_call(
        combine_kernel,
        grid=(tok // HALF,),
        in_specs=[
            whole((total, width)), line, line, pl.BlockSpec((width, HALF), lambda i: (0, i)),
        ],
        out_specs=pl.BlockSpec((HALF, width), lambda i: (i, 0)),
        out_shape=jax.ShapeDtypeStruct((tok, width), BF16),
        compiler_params=pltpu.CompilerParams(vmem_limit_bytes=40 * MIB),
        cost_estimate=pl.CostEstimate(flops=6 * MICRO, bytes_accessed=8 * MIB, transcendentals=0),
        name="combine",
    )(rows, slot, gate, resid)


CUBE = 0.044715
ROOT = 0.7978845608028654
FTILE = 768


def gelu_pair(x):
    square = x * x
    t = jnp.tanh(ROOT * (x + CUBE * (x * square)))
    half = 0.5 + 0.5 * t
    slope = half + (0.5 * x) * (1.0 - t * t) * (ROOT + (3.0 * CUBE * ROOT) * square)
    return x * half, slope


def device_of(index):
    wide = lax.axis_size("wide")
    return (index // wide, lax.rem(index, wide))


def expert_kernel(
    block,
    packed, gpack, grows, w_in, w_down,
    dx_out, out_got, rest_out, active_out, ginner_out, gs_out, x_out, gg_out,
    xbuf, gatebuf, gbuf, win, wdown, active, slope, ginner, gs, dx, outs, ggsend, ggbuf,
    x_send, x_recv, gate_send, gate_recv, gg_ssem, gg_rsem, o_send, o_recv, self_sem, load_sem, store_sem,
):
    count = lax.axis_size("narrow") * lax.axis_size("wide")
    me = lax.axis_index("narrow") * lax.axis_size("wide") + lax.axis_index("wide")
    blocks = count // block
    mine = me // block
    capp = packed.shape[1]
    rows = block * capp
    total = count * capp
    hidden = w_in.shape[1]
    mesh_id = pl.DeviceIdType.MESH

    def x_copy(target, source):
        return pltpu.make_async_remote_copy(
            src_ref=packed.at[target], dst_ref=xbuf.at[source], send_sem=x_send.at[target],
            recv_sem=x_recv.at[source], device_id=device_of(target), device_id_type=mesh_id,
        )

    def gate_copy(target, source):
        return pltpu.make_async_remote_copy(
            src_ref=gpack.at[target], dst_ref=gatebuf.at[source], send_sem=gate_send.at[target],
            recv_sem=gate_recv.at[source], device_id=device_of(target), device_id_type=mesh_id,
        )

    def gg_copy(target, source):
        return pltpu.make_async_remote_copy(
            src_ref=ggsend.at[target], dst_ref=ggbuf.at[source], send_sem=gg_ssem.at[target],
            recv_sem=gg_rsem.at[source], device_id=device_of(target), device_id_type=mesh_id,
        )

    ahead = blocks // 2
    inner = lax.rem(me, block)

    def out_copy(c, j):
        target = lax.rem(mine + c, blocks) * block + j
        return pltpu.make_async_remote_copy(
            src_ref=outs.at[c * block + j], dst_ref=out_got.at[c * block + inner],
            send_sem=o_send.at[c * block + j], recv_sem=o_recv.at[c * block + inner],
            device_id=device_of(target), device_id_type=mesh_id,
        )

    def out_wait(c, j):
        return pltpu.make_async_remote_copy(
            src_ref=outs.at[c * block + j], dst_ref=out_got.at[c * block + j],
            send_sem=o_send.at[c * block + j], recv_sem=o_recv.at[c * block + j],
            device_id=device_of(lax.rem(me + 1, count)), device_id_type=mesh_id,
        )

    barrier = pltpu.get_barrier_semaphore()

    @pl.loop(1, count)
    def _(s):
        pl.semaphore_signal(
            barrier, inc=1, device_id=device_of(lax.rem(me + s, count)), device_id_type=mesh_id
        )

    loads = [
        pltpu.make_async_copy(w_in, win, load_sem.at[0]),
        pltpu.make_async_copy(w_down, wdown, load_sem.at[1]),
        pltpu.make_async_copy(grows, gbuf, load_sem.at[2]),
    ]
    own = [
        pltpu.make_async_copy(packed.at[me], xbuf.at[me], self_sem.at[0]),
        pltpu.make_async_copy(gpack.at[me], gatebuf.at[me], self_sem.at[1]),
    ]
    for copy in own + loads:
        copy.start()
    pl.semaphore_wait(barrier, count - 1)

    @pl.loop(0, blocks)
    def _(c):
        there = lax.rem(mine + blocks - c, blocks)

        @pl.loop(0, block)
        def _(j):
            target = there * block + j

            @pl.when(target != me)
            def _():
                gate_copy(target, me).start()
                x_copy(target, me).start()

    for copy in own + loads:
        copy.wait()

    def stores(at):
        return [
            pltpu.make_async_copy(dx.at[at], dx_out.at[at], store_sem.at[0]),
            pltpu.make_async_copy(active.at[at], active_out.at[at], store_sem.at[1]),
            pltpu.make_async_copy(ginner.at[at], ginner_out.at[at], store_sem.at[2]),
            pltpu.make_async_copy(gs.at[at], gs_out.at[at], store_sem.at[3]),
        ]

    @pl.loop(0, blocks)
    def _(c):
        here = lax.rem(mine + c, blocks)
        first = here * block

        @pl.loop(0, block)
        def _(j):
            source = first + j

            @pl.when(source != me)
            def _():
                gate_copy(me, source).wait_recv()
                x_copy(me, source).wait_recv()

        at = pl.ds(pl.multiple_of(here * rows, rows), rows)
        group = pl.ds(first, block)
        x = xbuf[group].reshape(rows, xbuf.shape[2])

        @pl.loop(0, hidden // FTILE)
        def _(f):
            tile = pl.ds(pl.multiple_of(f * FTILE, FTILE), FTILE)
            value, grad = gelu_pair(dot_nn(x, win[:, tile]))
            active[at, tile] = value.astype(BF16)
            slope[:, tile] = grad

        result = dot_nn(active[at, :], wdown[...]).astype(BF16)
        outs[pl.ds(c * block, block)] = result.reshape(block, capp, result.shape[1])

        @pl.when(c < ahead)
        def _():
            @pl.loop(0, block)
            def _(j):
                @pl.when(first + j != me)
                def _():
                    out_copy(c, j).start()

        g = gbuf[group].astype(F32)
        diag = (
            lax.broadcasted_iota(jnp.int32, (block, capp, LANES), 1)
            == lax.broadcasted_iota(jnp.int32, (block, capp, LANES), 2)
        )
        gate = jnp.sum(gatebuf[group].astype(F32), axis=1)
        gate = jnp.sum(
            jnp.where(diag, gate[:, None, :], 0.0), axis=2, keepdims=True
        )
        gs[at, :] = (gate * g).astype(BF16).reshape(rows, g.shape[2])
        gg = jnp.sum(g * result.astype(F32).reshape(g.shape), axis=2, keepdims=True)
        gg = jnp.sum(jnp.where(diag, gg, 0.0), axis=1)
        which = lax.broadcasted_iota(jnp.int32, (block, 8, LANES), 1)
        high, mid, low = [part.astype(F32)[:, None, :] for part in split3(gg)]
        ggsend[group] = jnp.where(
            which == 0, high, jnp.where(which == 1, mid, jnp.where(which == 2, low, 0.0))
        ).astype(BF16)

        @pl.loop(0, block)
        def _(j):
            source = first + j

            @pl.when(source != me)
            def _():
                gg_copy(source, me).start()

        @pl.loop(0, hidden // FTILE)
        def _(f):
            tile = pl.ds(pl.multiple_of(f * FTILE, FTILE), FTILE)
            grad = dot_nt(gs[at, :], wdown[tile, :])
            ginner[at, tile] = (grad * slope[:, tile]).astype(BF16)

        dx[at, :] = dot_nt(ginner[at, :], win[...]).astype(BF16)

        for copy in stores(at):
            copy.start()

    for copy in stores(pl.ds(0, total)):
        copy.wait()
    keep = [
        pltpu.make_async_copy(xbuf, x_out, load_sem.at[0]),
        pltpu.make_async_copy(ggsend.at[me], ggbuf.at[me], self_sem.at[0]),
        pltpu.make_async_copy(outs.at[inner], out_got.at[inner], self_sem.at[1]),
        pltpu.make_async_copy(
            outs.at[pl.ds(ahead * block, count - ahead * block)], rest_out, load_sem.at[1]
        ),
    ]
    for copy in keep:
        copy.start()

    @pl.loop(0, count)
    def _(other):
        @pl.when(other != me)
        def _():
            x_copy(other, me).wait_send()
            gate_copy(other, me).wait_send()
            gg_copy(other, me).wait_send()
            gg_copy(me, other).wait_recv()

    @pl.loop(0, ahead * block)
    def _(i):
        @pl.when(i != inner)
        def _():
            out_wait(i // block, lax.rem(i, block)).wait_send()
            out_wait(i // block, lax.rem(i, block)).wait_recv()

    for copy in keep:
        copy.wait()
    last = pltpu.make_async_copy(ggbuf, gg_out, load_sem.at[1])
    last.start()
    last.wait()


def block_of(count, capp):
    block = 1
    while block * 4 <= count and block * 2 * capp <= 320:
        block *= 2
    return block


def expert(packed, gpack, grows, w_in, w_down):
    count, capp, width = packed.shape
    hidden = w_in.shape[1]
    block = block_of(count, capp)
    early = (count // block // 2) * block
    rows = block * capp
    total = count * capp
    sd = jax.ShapeDtypeStruct
    anyspec = pl.BlockSpec(memory_space=pl.ANY)
    dma = pltpu.SemaphoreType.DMA
    return pl.pallas_call(
        functools.partial(expert_kernel, block),
        in_specs=[anyspec] * 5,
        out_specs=(anyspec,) * 8,
        out_shape=(
            sd((total, width), BF16), sd((early, capp, width), BF16),
            sd((count - early, capp, width), BF16), sd((total, hidden), BF16), sd((total, hidden), BF16), sd((total, width), BF16), sd((count, capp, width), BF16),
            sd((count, 8, LANES), BF16),
        ),
        scratch_shapes=[
            pltpu.VMEM((count, capp, width), BF16), pltpu.VMEM((count, 8, LANES), BF16),
            pltpu.VMEM((count, capp, width), BF16), pltpu.VMEM((width, hidden), BF16),
            pltpu.VMEM((hidden, width), BF16), pltpu.VMEM((total, hidden), BF16),
            pltpu.VMEM((rows, hidden), F32), pltpu.VMEM((total, hidden), BF16),
            pltpu.VMEM((total, width), BF16), pltpu.VMEM((total, width), BF16),
            pltpu.VMEM((count, capp, width), BF16), pltpu.VMEM((count, 8, LANES), BF16),
            pltpu.VMEM((count, 8, LANES), BF16),
            dma((count,)), dma((count,)), dma((count,)), dma((count,)), dma((count,)), dma((count,)),
            dma((early,)), dma((early,)), dma((2,)), dma((3,)), dma((4,)),
        ],
        compiler_params=pltpu.CompilerParams(
            collective_id=0, has_side_effects=True, vmem_limit_bytes=62 * MIB
        ),
        cost_estimate=pl.CostEstimate(flops=60 * MICRO, bytes_accessed=60 * 1024 * 1024, transcendentals=0),
        name="expert",
    )(packed, gpack, grows, w_in, w_down)


def weights_kernel(active_ref, gs_ref, x_ref, ginner_ref, down_ref, in_ref, xt):
    @pl.when(pl.program_id(0) == 0)
    def _():
        total = x_ref.shape[0]
        for t in range(0, total, HALF):
            xt[:, t:t + HALF] = x_ref[t:t + HALF, :].T

    down_ref[0] = dot_tn(active_ref[...], gs_ref[...])
    in_ref[0] = dot_nn(xt[...], ginner_ref[...])


def weight_grads(active, gs, x, ginner):
    total, hidden = active.shape
    width = gs.shape[1]
    tile = HALF
    cols = pl.BlockSpec((total, tile), lambda i: (0, i))
    return pl.pallas_call(
        weights_kernel,
        grid=(hidden // tile,),
        in_specs=[cols, whole((total, width)), whole((total, width)), cols],
        out_specs=(
            pl.BlockSpec((1, tile, width), lambda i: (0, i, 0)),
            pl.BlockSpec((1, width, tile), lambda i: (0, 0, i)),
        ),
        out_shape=(
            jax.ShapeDtypeStruct((1, hidden, width), F32),
            jax.ShapeDtypeStruct((1, width, hidden), F32),
        ),
        scratch_shapes=[pltpu.VMEM((width, total), BF16)],
        compiler_params=pltpu.CompilerParams(vmem_limit_bytes=40 * MIB),
        cost_estimate=pl.CostEstimate(flops=18 * MICRO, bytes_accessed=36 * 1024 * 1024, transcendentals=0),
        name="weight_grads",
    )(active, gs, x, ginner)
PIECES = 32
BIG = 2
UNITS = BIG + GROUPS
TROWS = 16
LATE = 24
LAST_PHASE = 7


def norm_back(grad, source, gain):
    scale = lax.rsqrt(jnp.mean(source * source, axis=0, keepdims=True) + EPS)
    normed = source * scale
    scaled = grad * gain
    inner = jnp.mean(scaled * normed, axis=0, keepdims=True)
    part = grad * normed
    part = part[:, :LANES] + part[:, LANES:]
    return scale * (scaled - normed * inner), part


def back_kernel(
    block,
    dx_ref, gg_ref, slot_ref, pos_ref, ids_ref, route_ref, gate_ref, n2_ref, attn_ref,
    gain1_ref, gain2_ref, wr_ref, wout_ref, resid_any, g_any, hid_any, n1_any, q_any, k_any, v_any, p_any,
    wqkv_any, rel_any, rest_any,
    ingrad_any, out_got, big_out, small_out, early_out, late_out,
    gres, ga, gn1, dv, soft, hid_ref, n1_ref, q_ref, k_ref, v_ref, wqkv_ref, rel_ref, acc,
    *buffers_and_rest,
):
    big, small = buffers_and_rest[:7] + (big_out,), buffers_and_rest[7:14] + (small_out,)
    (
        early, early_got, late, late_got, send, recv, xsend, xrecv, esend, erecv, lsend, lrecv, osend, orecv, load_sem, store_sem, stage_sem,
    ) = buffers_and_rest[14:]
    dq, dk = dv.at[pl.ds(0, GW)], dv.at[pl.ds(GW, GW)]
    step = pl.program_id(0)
    pair = pl.program_id(1)
    tok = g_any.shape[0]
    seqs = tok // LEN
    experts = route_ref.shape[0]
    total = dx_ref.shape[0]
    width = g_any.shape[1]
    narrow_n, wide_n = lax.axis_size("narrow"), lax.axis_size("wide")
    n, w = lax.axis_index("narrow"), lax.axis_index("wide")
    core, zed = lax.rem(w, 2), lax.rem(w // 2, 4)
    ex, why = lax.rem(n, 2), lax.rem(n // 2, 2)
    more_n = (narrow_n // 4) * (wide_n // 8)
    more_w = wide_n // 8
    more = (n // 4) * more_w + w // 8
    mesh_id = pl.DeviceIdType.MESH
    core_dev = (n, w + 1 - 2 * core)
    ex_dev = (n + 1 - 2 * ex, w)
    why_dev = (n + 2 - 4 * why, w)

    def zed_dev(step):
        return (n, w + 2 * (lax.rem(zed + step, 4) - zed))

    def more_dev(step):
        other = lax.rem(more + step, more_n)
        return (n + 4 * (other // more_w - more // more_w),
                w + 8 * (lax.rem(other, more_w) - lax.rem(more, more_w)))

    def unit(u):
        if isinstance(u, int):
            return (big, u, u) if u < BIG else (small, u - BIG, u)
        return small, u, u + BIG

    def ref(which, u):
        group, at, _ = unit(u)
        return group[which], at

    def view(which, u, *more):
        group, at, _ = unit(u)
        return group[which].at[(at,) + more]

    def land(u, q, at):
        return view(7, u, q, at)

    def spot(q):
        first, second = (ex, why) if q == 0 else (why, ex)
        b16 = core * 16
        b8 = b16 + first * 8
        b4 = b8 + second * 4
        return first, second, b16, b8, b4

    def remote(src, dst, k, u, q, dev):
        return pltpu.make_async_remote_copy(
            src_ref=src, dst_ref=dst, send_sem=send.at[k, unit(u)[2], q], recv_sem=recv.at[k, unit(u)[2], q],
            device_id=dev, device_id_type=mesh_id,
        )

    def outgoing(phase, u, q):
        first, second, b16, b8, b4 = spot(q)
        one, two = (ex_dev, why_dev) if q == 0 else (why_dev, ex_dev)
        if phase == 0:
            return [remote(view(0, u, q, pl.ds(16 - b16, 16)), view(2, u, q), 0, u, q, core_dev)]
        if phase == 1:
            src = view(0, u, q, pl.ds(b16 + (1 - first) * 8, 8))
            return [remote(src, view(3, u, q), 1, u, q, one)]
        if phase == 2:
            src = view(0, u, q, pl.ds(b8 + (1 - second) * 4, 4))
            return [remote(src, view(4, u, q), 2, u, q, two)]
        if phase == 3:
            return [
                remote(view(0, u, q, b4 + lax.rem(zed + step, 4)), view(5, u, q, step - 1),
                       2 + step, u, q, zed_dev(step))
                for step in (1, 2, 3)
            ]
        if phase == 4:
            mine = land(u, q, b4 + zed)
            return [remote(view(1, u, q), mine, 5 + step, u, q, zed_dev(step)) for step in (1, 2, 3)]
        if phase == 5:
            mine = land(u, q, pl.ds(b4, 4))
            return [remote(mine, mine, 9, u, q, two)]
        if phase == 6:
            mine = land(u, q, pl.ds(b8, 8))
            return [remote(mine, mine, 10, u, q, one)]
        mine = land(u, q, pl.ds(b16, 16))
        return [remote(mine, mine, 11, u, q, core_dev)]

    def incoming(phase, u, q):
        first, second, b16, b8, b4 = spot(q)
        if phase < 4:
            return outgoing(phase, u, q)
        if phase == 4:
            return [
                remote(view(1, u, q), land(u, q, b4 + lax.rem(zed + 4 - step, 4)),
                       5 + step, u, q, zed_dev(step))
                for step in (1, 2, 3)
            ]
        if phase == 5:
            there = land(u, q, pl.ds(b8 + (1 - second) * 4, 4))
            return [remote(there, there, 9, u, q, core_dev)]
        if phase == 6:
            there = land(u, q, pl.ds(b16 + (1 - first) * 8, 8))
            return [remote(there, there, 10, u, q, core_dev)]
        there = land(u, q, pl.ds(16 - b16, 16))
        return [remote(there, there, 11, u, q, core_dev)]

    def add(u, q, start, count, which):
        own, at = ref(0, u)
        got = ref(which, u)[0]

        @pl.loop(0, count)
        def _(i):
            own[at, q, start + i] = (
                own[at, q, start + i].astype(F32) + got[at, q, i].astype(F32)
            ).astype(BF16)

    def spread(u, q):
        (done, at), (extra, _) = ref(1, u), ref(6, u)
        extra[at, q, more] = done[at, q]
        copies = [
            pltpu.make_async_remote_copy(
                src_ref=view(6, u, q, more), dst_ref=view(6, u, q, more),
                send_sem=xsend.at[unit(u)[2], q, step], recv_sem=xrecv.at[unit(u)[2], q, step],
                device_id=more_dev(step), device_id_type=mesh_id,
            )
            for step in range(1, more_n)
        ]
        for copy in copies:
            copy.start()
        for step in range(1, more_n):
            other = lax.rem(more + more_n - step, more_n)
            pltpu.make_async_remote_copy(
                src_ref=view(6, u, q, more), dst_ref=view(6, u, q, other),
                send_sem=xsend.at[unit(u)[2], q, step], recv_sem=xrecv.at[unit(u)[2], q, step],
                device_id=more_dev(step), device_id_type=mesh_id,
            ).wait_recv()
        for copy in copies:
            copy.wait_send()
        total = extra[at, q, 0].astype(F32)
        for i in range(1, more_n):
            total = total + extra[at, q, i].astype(F32)
        done[at, q] = total.astype(BF16)

    def keep(u, q):
        at = spot(q)[4] + zed
        return pltpu.make_async_copy(view(1, u, q), land(u, q, at), store_sem.at[unit(u)[2], q])

    def settle(phase, u, q):
        first, second, b16, b8, b4 = spot(q)
        if phase == 0:
            add(u, q, b16, 16, 2)
        elif phase == 1:
            add(u, q, b8, 8, 3)
        elif phase == 2:
            add(u, q, b4, 4, 4)
        elif phase == 3:
            (own, at), (done, _), (got, _) = ref(0, u), ref(1, u), ref(5, u)
            done[at, q] = (
                own[at, q, b4 + zed].astype(F32) + got[at, q, 0].astype(F32)
                + (got[at, q, 1].astype(F32) + got[at, q, 2].astype(F32))
            ).astype(BF16)
            if more_n > 1:
                spread(u, q)
            keep(u, q).start()
        elif phase == 4:
            keep(u, q).wait()

    bits = []
    for axis, count in (("wide", wide_n), ("narrow", narrow_n)):
        size = 1
        while size < count:
            at = lax.rem((w if axis == "wide" else n) // size, 2)
            move = size - 2 * size * at
            bits.append((n, w + move) if axis == "wide" else (n + move, w))
            size *= 2
    levels = len(bits)
    early_levels = early_got.shape[0] if early.shape[0] > 1 else 0

    def swap(level, mine, got, ssem, rsem):
        return pltpu.make_async_remote_copy(
            src_ref=mine.at[level], dst_ref=got.at[level], send_sem=ssem.at[level],
            recv_sem=rsem.at[level], device_id=bits[level], device_id_type=mesh_id,
        )

    def climb(level, mine, got, ssem, rsem):
        copy = swap(level, mine, got, ssem, rsem)
        copy.wait_recv()
        copy.wait_send()
        mine[level + 1] = mine[level] + got[level]
        if level + 1 < levels:
            swap(level + 1, mine, got, ssem, rsem).start()

    def climb_early(level):
        climb(level, early, early_got, esend, erecv)

    def climb_late(level):
        climb(level, late, late_got, lsend, lrecv)

    count = narrow_n * wide_n
    blocks = count // block
    ahead = blocks // 2
    index = n * wide_n + w
    rest = rest_any.shape[0]

    def out_copy(i):
        target = lax.rem(index // block + ahead + i // block, blocks) * block + lax.rem(i, block)
        return pltpu.make_async_remote_copy(
            src_ref=rest_any.at[i],
            dst_ref=out_got.at[(i // block) * block + lax.rem(index, block)],
            send_sem=osend.at[i], recv_sem=orecv.at[(i // block) * block + lax.rem(index, block)],
            device_id=device_of(target), device_id_type=mesh_id,
        )

    def out_wait(i):
        return pltpu.make_async_remote_copy(
            src_ref=rest_any.at[i], dst_ref=out_got.at[i], send_sem=osend.at[i],
            recv_sem=orecv.at[i], device_id=core_dev, device_id_type=mesh_id,
        )

    def begin(u):
        for q in range(2):
            for copy in outgoing(0, u, q):
                copy.start()

    def advance(u, phase):
        for q in range(2):
            for copy in incoming(phase, u, q):
                copy.wait_recv()
            for copy in outgoing(phase, u, q):
                copy.wait_send()
            settle(phase, u, q)
            if phase < LAST_PHASE:
                for copy in outgoing(phase + 1, u, q):
                    copy.start()

    def place(u, first, value):
        own, at = ref(0, u)
        half = own.shape[4]
        count = value.shape[1]
        blocks = value.reshape(PIECES, width // PIECES, count).astype(BF16)
        done = 0
        while done < count:
            q, inside = (first + done) // half, (first + done) % half
            size = min(half - inside, count - done)
            own[at, q, :, :, inside:inside + size] = blocks[:, :, done:done + size]
            done += size

    def soft_load(group):
        at = pl.ds(group * GROUP, GROUP)
        return pltpu.make_async_copy(p_any.at[at], soft.at[at], load_sem.at[group])

    pairs = ((q_any, q_ref), (k_any, k_ref), (v_any, v_ref), (n1_any, n1_ref), (wqkv_any, wqkv_ref),
             (rel_any, rel_ref))
    loads = [
        pltpu.make_async_copy(src, dst, load_sem.at[GROUPS + i]) for i, (src, dst) in enumerate(pairs)
    ]

    rows_load = [
        pltpu.make_async_copy(src, hid_ref, load_sem.at[GROUPS + 6 + i])
        for i, src in enumerate((g_any, hid_any))
    ]

    barrier = pltpu.get_barrier_semaphore()
    greet = [core_dev, ex_dev, why_dev] + [zed_dev(move) for move in (1, 2, 3)]
    greet += [more_dev(move) for move in range(1, more_n)] + bits

    @pl.when((step == 0) & (pair == 0))
    def _():
        first = pltpu.make_async_copy(resid_any, gres, stage_sem)
        first.start()
        rows_load[0].start()
        soft_load(0).start()
        for copy in loads:
            copy.start()
        for group in range(1, GROUPS):
            soft_load(group).start()
        for dev in greet:
            pl.semaphore_signal(barrier, inc=1, device_id=dev, device_id_type=mesh_id)

        @pl.loop(0, rest)
        def _(i):
            source = lax.rem(
                index // block + 2 * blocks - ahead - i // block, blocks
            ) * block + lax.rem(i, block)
            pl.semaphore_signal(
                barrier, inc=1, device_id=device_of(source), device_id_type=mesh_id
            )

        pl.semaphore_wait(barrier, len(greet) + rest)

        @pl.loop(0, rest)
        def _(i):
            out_copy(i).start()

        hot = lax.broadcasted_iota(jnp.int32, (experts, tok), 0) == ids_ref[...]
        where = (
            lax.broadcasted_iota(jnp.int32, (LANES, tok), 0) == pos_ref[...]
        ).astype(F32).astype(BF16)
        grad_gate = jnp.zeros((1, tok), F32)
        for e in range(0, experts, 32):
            found = dot_nn(gg_ref[e:e + 32].reshape(256, LANES), where)
            found = jnp.sum(found.reshape(32, 8, tok), axis=1)
            grad_gate += jnp.sum(jnp.where(hot[e:e + 32], found, 0.0), axis=0, keepdims=True)
        first.wait()
        rows_load[0].wait()
        grad_logits = (
            (grad_gate * gate_ref[...]) * (hot.astype(F32) - route_ref[...])
        ).astype(BF16)
        early[0, :experts, :] = dot_nt(grad_logits, n2_ref[...])
        gain_grad = jnp.zeros((width, LANES), F32)
        for t in range(0, tok, HALF):
            cols = slice(t, t + HALF)
            gn2 = dot_nn(wr_ref[...], grad_logits[:, cols])
            size = total if total <= 1280 else 512
            for r in range(0, total, size):
                table = lax.broadcasted_iota(jnp.int32, (size, HALF), 0) + r == slot_ref[:, cols]
                gn2 = gn2 + dot_tn(dx_ref[r:r + size, :], table.astype(F32).astype(BF16))
            branch, part = norm_back(gn2, gres[:, cols], gain2_ref[...])
            gain_grad = gain_grad + part
            gr = hid_ref[t:t + HALF, :].astype(F32).T + branch
            gres[:, cols] = gr
            ga[:, cols] = gr.astype(BF16)
        early[0, experts:, :] = jnp.broadcast_to(
            jnp.sum(gain_grad.T, axis=0, keepdims=True), (8, width)
        )
        for c in range(0, width, HALF):
            place(0, c, dot_nt(attn_ref[...], ga[c:c + HALF, :]))
        rows_load[1].start()
        begin(0)
        if early_levels:
            swap(0, early, early_got, esend, erecv).start()
        for t in range(0, tok, HALF):
            cols = slice(t, t + HALF)
            ga[:, cols] = dot_nn(wout_ref[...], ga[:, cols]).astype(BF16)
        soft_load(0).wait()
        for copy in loads:
            copy.wait()
        for group in range(1, GROUPS):
            soft_load(group).wait()

        @pl.loop(0, HEADS)
        def _(head):
            at = pl.ds(pl.multiple_of(head * HEAD_DIM, HEAD_DIM), HEAD_DIM)
            for s in range(seqs):
                row = slice(s * LEN, (s + 1) * LEN)
                dv[at, row] = dot_nt(ga[at, row], soft[head, s]).astype(BF16)

        for c in range(0, width, GW):
            place(1, c, dot_nt(n1_ref[...], dv[c:c + GW, :]))
        begin(1)
        for t in range(0, tok, HALF):
            gn1[:, t:t + HALF] = dot_nn(wqkv_ref[:, 2 * width:], dv[:, t:t + HALF])

    @pl.loop(0, PAIR)
    def _(h):
        inside = pair * PAIR + h
        head = step * GROUP + inside
        at = pl.ds(pl.multiple_of(inside * HEAD_DIM, HEAD_DIM), HEAD_DIM)
        all_at = pl.ds(pl.multiple_of(head * HEAD_DIM, HEAD_DIM), HEAD_DIM)
        for s in range(seqs):
            row = slice(s * LEN, (s + 1) * LEN)
            value = v_ref[all_at, row]
            for c in range(0, LEN, HALF):
                cols = slice(s * LEN + c, s * LEN + c + HALF)
                grad = ga[all_at, cols]
                inner = jnp.sum(
                    grad.astype(F32) * attn_ref[all_at, cols].astype(F32), axis=0, keepdims=True
                )
                gp = dot_tn(value, grad)
                soft[head, s, :, c:c + HALF] = (
                    soft[head, s, :, c:c + HALF].astype(F32) * (gp - inner)
                ).astype(BF16)
            ds = soft[head, s]
            factor = HEAD_DIM ** -0.5
            dq[at, row] = (dot_nn(k_ref[all_at, row], ds) * factor).astype(BF16)
            dk[at, row] = (dot_nt(q_ref[all_at, row], ds) * factor).astype(BF16)

        for number in range(HEADS):
            todo = [(u, phase) for u, phase, at_head in SCHEDULE if at_head == number]
            rise = [level for level, at_head in enumerate(EARLY_LEVELS)
                    if at_head == number and level < early_levels]
            if todo or rise:
                @pl.when(head == number)
                def _():
                    for u, phase in todo:
                        advance(u, phase)
                    for level in rise:
                        climb_early(level)

    @pl.when(pair == pl.num_programs(1) - 1)
    def _():
        for part, d in enumerate((dq, dk)):
            place(step, part * GW, dot_nt(n1_ref[...], d[...]))
        begin(step)
        for part, d in enumerate((dq, dk)):
            cols = pl.ds(pl.multiple_of(part * width + step * GW, GW), GW)
            gn1[...] += dot_nn(wqkv_ref[:, cols], d[...])

    @pl.when((step == pl.num_programs(0) - 1) & (pair == pl.num_programs(1) - 1))
    def _():
        planned = {(u, phase) for u, phase, at_head in SCHEDULE}
        left = {u: [phase for phase in range(LAST_PHASE + 1) if (u, phase) not in planned]
                for u in range(UNITS)}

        def push():
            for u in range(UNITS):
                if left[u]:
                    advance(u, left[u].pop(0))

        rows_load[1].wait()
        gain_grad = jnp.zeros((width, LANES), F32)
        for t in range(0, tok, HALF):
            cols = slice(t, t + HALF)
            x = hid_ref[t:t + HALF, :].astype(F32).T
            branch, part = norm_back(gn1[:, cols], x, gain1_ref[...])
            gain_grad = gain_grad + part
            gres[:, cols] = gres[:, cols] + branch
            if t == HALF:
                push()
        pltpu.make_async_copy(gres, ingrad_any, stage_sem).start()
        line = jnp.sum(gain_grad.T, axis=0, keepdims=True)
        late[0] = jnp.zeros((LATE, LANES), F32)
        for i in range(width // LANES):
            late[0, i:i + 1, :] = line[:, i * LANES:(i + 1) * LANES]
        push()
        lines = HEADS * seqs
        acc[...] = jnp.zeros_like(acc)
        chunks = 4
        for chunk in range(chunks):
            @pl.loop(chunk * (LEN // TROWS // chunks), (chunk + 1) * (LEN // TROWS // chunks))
            def _(r):
                base = pl.multiple_of(r * TROWS, TROWS)
                lhs = soft[:, :, pl.ds(base, TROWS), :].reshape(lines * TROWS, LEN)
                rel = rel_ref[pl.ds(base, TROWS), :]
                hot = (
                    rel[:, None, :]
                    == lax.broadcasted_iota(jnp.int32, (TROWS, BUCKETS, LEN), 1)
                ).astype(F32).astype(BF16).reshape(TROWS * BUCKETS, LEN)
                acc[...] += dot_nt(lhs, hot)

            push()
        rows = lax.broadcasted_iota(jnp.int32, acc.shape, 0) % TROWS
        cols = lax.broadcasted_iota(jnp.int32, acc.shape, 1) // BUCKETS
        kept = jnp.where(rows == cols, acc[...], 0.0)
        per_head = jnp.sum(kept.reshape(HEADS, seqs * TROWS, acc.shape[1]), axis=1)
        fold = (
            lax.broadcasted_iota(jnp.int32, (LANES, acc.shape[1]), 1) % BUCKETS
            == lax.broadcasted_iota(jnp.int32, (LANES, acc.shape[1]), 0)
        ).astype(F32)
        late[0, 8:8 + HEADS, :] = lax.dot_general(
            per_head, fold, (((1,), (1,)), ((), ())), precision=lax.Precision.HIGHEST,
            preferred_element_type=F32,
        )
        swap(0, late, late_got, lsend, lrecv).start()
        level = 0
        while any(left.values()) or level < levels:
            push()
            if level < levels:
                climb_late(level)
                level += 1
        for level in range(early_levels):
            if level >= len(EARLY_LEVELS):
                climb_early(level)
        pltpu.make_async_copy(gres, ingrad_any, stage_sem).wait()

        @pl.loop(0, rest)
        def _(i):
            out_wait(i).wait_send()
            out_wait(i).wait_recv()

        early_out[...] = early[early_levels]
        late_out[...] = late[levels]


EARLY_MOST = 64
EARLY_LEVELS = (1, 3, 5, 7, 9)
SCHEDULE = (
    [(0, phase, at) for phase, at in enumerate((0, 2, 4, 6, 8, 10))]
    + [(1, phase, at) for phase, at in enumerate((1, 3, 5, 8, 11))]
    + [(2, phase, at) for phase, at in enumerate((5, 7, 10))]
    + [(3, phase, at) for phase, at in enumerate((9, 11))]
)


def back(dx, gg, slot, pos, ids, route, gate, resid, n2, attn, g, hidden, n1, q, k, v, p, gain1, gain2,
         w_router, w_out, w_qkv, relt, rest, block):
    tok, width = hidden.shape
    experts = w_router.shape[1]
    total = dx.shape[0]
    seqs = p.shape[1]
    narrow_n, wide_n = lax.axis_size("narrow"), lax.axis_size("wide")
    levels = (narrow_n * wide_n).bit_length() - 1
    more_n = (narrow_n // 4) * (wide_n // 8)
    early_levels = levels if experts <= EARLY_MOST else 0
    rows = width // PIECES
    anyspec = pl.BlockSpec(memory_space=pl.ANY)
    sd = jax.ShapeDtypeStruct
    dma = pltpu.SemaphoreType.DMA
    vm = pltpu.VMEM

    def bufs(number, half):
        return [
            vm((number, 2) + lead + (rows, half), BF16)
            for lead in ((PIECES,), (), (16,), (8,), (4,), (3,), (more_n,))
        ]

    return pl.pallas_call(
        functools.partial(back_kernel, block),
        grid=(GROUPS, GROUP // PAIR),
        in_specs=[
            whole((total, width)), whole((experts, 8, LANES)), whole((1, tok)), whole((1, tok)),
            whole((1, tok)), whole((experts, tok)), whole((1, tok)), whole((width, tok)),
            whole((width, tok)), whole((width, 1)), whole((width, 1)),
            whole((width, experts)), whole((width, width)),
        ] + [anyspec] * 11,
        out_specs=(
            anyspec, anyspec, anyspec, anyspec, whole((experts + 8, width)), whole((LATE, LANES)),
        ),
        out_shape=(
            sd((width, tok), F32), sd(rest.shape, BF16), sd((BIG, 2, PIECES, rows, width // 2), BF16),
            sd((GROUPS, 2, PIECES, rows, GW), BF16),
            sd((experts + 8, width), F32), sd((LATE, LANES), F32),
        ),
        scratch_shapes=[
            vm((width, tok), F32), vm((width, tok), BF16), vm((width, tok), F32),
            vm((width, tok), BF16),
            vm((HEADS, seqs, LEN, LEN), BF16), vm((tok, width), BF16), vm((width, tok), BF16),
            vm((width, tok), BF16), vm((width, tok), BF16), vm((width, tok), BF16),
            vm(w_qkv.shape, BF16), vm((LEN, LEN), jnp.int32), vm((HEADS * seqs * TROWS, TROWS * BUCKETS), F32),
            *bufs(BIG, width // 2), *bufs(GROUPS, GW),
            vm((early_levels + 1, experts + 8, width), F32),
            vm((max(early_levels, 1), experts + 8, width) if early_levels else (1, 8, width), F32),
            vm((levels + 1, LATE, LANES), F32), vm((levels, LATE, LANES), F32),
            dma((12, UNITS, 2)), dma((12, UNITS, 2)), dma((UNITS, 2, more_n)),
            dma((UNITS, 2, more_n)), dma((levels,)), dma((levels,)), dma((levels,)), dma((levels,)),
            dma((rest.shape[0],)), dma((rest.shape[0],)),
            dma((GROUPS + 8,)), dma((UNITS, 2)), dma(()),
        ],
        compiler_params=pltpu.CompilerParams(
            collective_id=1, has_side_effects=True, vmem_limit_bytes=63 * MIB
        ),
        cost_estimate=pl.CostEstimate(flops=80 * MICRO, bytes_accessed=50 * MIB, transcendentals=0),
        name="back",
    )(
        dx, gg, slot, pos, ids, route, gate, n2, attn, gain1.reshape(width, 1),
        gain2.reshape(width, 1), w_router, w_out, resid, g, hidden, n1, q, k, v, p, w_qkv, relt, rest,
    )


def finish_kernel(
    early_ref, late_ref, slot_ref, gate_ref, resid_ref, big_ref, small_ref, grad_ref, out_ref, qkv_ref, proj_ref,
    ingrad_ref,
):
    ingrad_ref[...] = grad_ref[...].T
    rows_a = early_ref.shape[0]
    cols = slot_ref.shape[1]
    combined = None
    for base, ref in ((0, early_ref), (rows_a, late_ref)):
        table = (
            lax.broadcasted_iota(jnp.int32, (ref.shape[0], cols), 0) + base == slot_ref[...]
        )
        part = dot_tn(ref[...], table.astype(F32).astype(BF16))
        combined = part if combined is None else combined + part
    out_ref[...] = (resid_ref[...] + gate_ref[...] * combined).T.astype(BF16)
    rows = qkv_ref.shape[0]
    half = big_ref.shape[4]
    width = 2 * half
    for q in range(2):
        proj_ref[:, q * half:(q + 1) * half] = big_ref[0, q].astype(F32).reshape(rows, half)
        start = 2 * width + q * half
        qkv_ref[:, start:start + half] = big_ref[1, q].astype(F32).reshape(rows, half)
        for group in range(GROUPS):
            start = q * width + group * GW
            qkv_ref[:, start:start + GW] = small_ref[group, q].astype(F32).reshape(rows, GW)


def finish(out_a, out_b, slot, gate, resid, big, small, grad):
    tok = slot.shape[1]
    width = resid.shape[0]
    steps = tok // HALF
    line = pl.BlockSpec((1, HALF), lambda i: (0, i))
    pieces = big.shape[2] // steps
    rows = width // steps
    return pl.pallas_call(
        finish_kernel,
        grid=(steps,),
        in_specs=[
            whole(out_a.shape), whole(out_b.shape), line, line,
            pl.BlockSpec((width, HALF), lambda i: (0, i)),
            pl.BlockSpec(big.shape[:2] + (pieces,) + big.shape[3:], lambda i: (0, 0, i, 0, 0)),
            pl.BlockSpec(small.shape[:2] + (pieces,) + small.shape[3:], lambda i: (0, 0, i, 0, 0)),
            pl.BlockSpec((width, HALF), lambda i: (0, i)),
        ],
        out_specs=(
            pl.BlockSpec((HALF, width), lambda i: (i, 0)),
            pl.BlockSpec((rows, 3 * width), lambda i: (i, 0)),
            pl.BlockSpec((rows, width), lambda i: (i, 0)),
            pl.BlockSpec((HALF, width), lambda i: (i, 0)),
        ),
        out_shape=(
            jax.ShapeDtypeStruct((tok, width), BF16),
            jax.ShapeDtypeStruct((width, 3 * width), F32),
            jax.ShapeDtypeStruct((width, width), F32),
            jax.ShapeDtypeStruct((tok, width), F32),
        ),
        compiler_params=pltpu.CompilerParams(vmem_limit_bytes=40 * MIB),
        cost_estimate=pl.CostEstimate(flops=8 * MICRO, bytes_accessed=20 * MIB, transcendentals=0),
        name="finish",
    )(out_a, out_b, slot, gate, resid, big, small, grad)


def matmul(a, b):
    return jnp.dot(a, b, preferred_element_type=F32)


AXES = ("narrow", "wide")


def exchange(v):
    return lax.all_to_all(v, AXES, split_axis=0, concat_axis=0, tiled=True)


def local(
    hidden_in, norm_gain_one, w_qkv, w_out, pos_table, norm_gain_two, w_router, w_in, w_down,
    expert_ids, segment_ids, rel_buckets, out_grad,
):
    experts = lax.axis_size("narrow") * lax.axis_size("wide")
    tok, width = hidden_in.shape
    cap = max(2, (5 * tok + 4 * experts - 1) // (4 * experts))
    capp = (cap + 7) // 8 * 8
    rows = experts * capp
    ids = expert_ids.reshape(1, tok)
    slot, pos, g_packed = make_slots(experts, cap, capp, ids, out_grad)
    g_rows = exchange(g_packed.reshape(experts, capp, width))
    table = jnp.pad(pos_table.T, ((0, 0), (0, LANES - BUCKETS)))
    (n1, q, k, v, p, attn, resid, n2, route, gate, packed, gpack) = front(
        hidden_in, norm_gain_one, w_qkv, w_out, table, norm_gain_two, w_router, ids, slot, pos,
        segment_ids, rel_buckets, rows,
    )
    block = block_of(experts, capp)
    dx, out_a, rest, active, ginner, gs, expert_in, gg = expert(
        packed.reshape(experts, capp, width), gpack, g_rows, w_in[0], w_down[0]
    )
    dx = exchange(dx.reshape(experts, capp, width)).reshape(rows, width)
    grad_w_down, grad_w_in = weight_grads(active, gs, expert_in.reshape(rows, width), ginner)
    dx, grad_w_down, grad_w_in = lax.optimization_barrier((dx, grad_w_down, grad_w_in))
    grad, out_b, big, small, early, late = back(
        dx, gg, slot, pos, ids, route, gate, resid, n2, attn, out_grad, hidden_in, n1, q, k, v, p,
        norm_gain_one, norm_gain_two, w_router, w_out, w_qkv, rel_buckets.T, rest, block,
    )
    if experts > EARLY_MOST:
        early = lax.psum(early, AXES)
    blocks = experts // block
    index = lax.axis_index("narrow") * lax.axis_size("wide") + lax.axis_index("wide")
    turn = lax.rem(index // block + blocks - ids // block, blocks)
    place = jnp.where(pos >= 0, (turn * block + lax.rem(ids, block)) * capp + pos, -1)
    layer_out, qkv_grad, out_grad_w, in_grad = finish(
        out_a.reshape(-1, width), out_b.reshape(-1, width), place, gate, resid, big, small, grad
    )
    lines = width // LANES
    return (
        layer_out, in_grad, late[:lines].reshape(width), qkv_grad, out_grad_w,
        late[8:8 + HEADS, :BUCKETS].T, early[experts], early[:experts].T, grad_w_in, grad_w_down,
    )


def solution(mesh):
    split = P(AXES, None)
    cube = P(AXES, None, None)
    return jax.shard_map(
        local,
        mesh=mesh,
        in_specs=(
            split, P(), P(), P(), P(), P(), P(), cube, cube, split, split, P(), split,
        ),
        out_specs=(split, split, P(), P(), P(), P(), P(), P(), cube, cube),
        check_vma=False,
    )
```

```python
import functools
import jax
import jax.numpy as jnp
from jax import lax
from jax.experimental import pallas as pl
from jax.experimental.pallas import tpu as pltpu
from jax.sharding import PartitionSpec as P

HEADS = 12
HEAD_DIM = 64
LEN = 512
BUCKETS = 32
EPS = 1e-06
LANES = 128
HALF = 256
GROUP = 4
PAIR = 2
GROUPS = HEADS // GROUP
GW = GROUP * HEAD_DIM
F32 = jnp.float32
BF16 = jnp.bfloat16
MIB = 1024 * 1024
MICRO = 1150000000


def dot_nn(a, b):
    return lax.dot_general(a, b, (((1,), (0,)), ((), ())), preferred_element_type=F32)


def dot_tn(a, b):
    return lax.dot_general(a, b, (((0,), (0,)), ((), ())), preferred_element_type=F32)


def dot_nt(a, b):
    return lax.dot_general(a, b, (((1,), (1,)), ((), ())), preferred_element_type=F32)


def whole(shape):
    rank = len(shape)
    return pl.BlockSpec(shape, lambda *g: (0,) * rank, pipeline_mode=pl.Buffered(1))


def split3(v):
    high = v.astype(BF16)
    rest = v - high.astype(F32)
    mid = rest.astype(BF16)
    low = (rest - mid.astype(F32)).astype(BF16)
    return high, mid, low


def slots_kernel(experts, cap, capp, ids_ref, g_ref, slot_ref, pos_ref, packed_ref):
    tok = ids_ref.shape[1]
    ids = ids_ref[...]
    hot = lax.broadcasted_iota(jnp.int32, (experts, tok), 0) == ids
    before = (
        lax.broadcasted_iota(jnp.int32, (tok, tok), 0)
        < lax.broadcasted_iota(jnp.int32, (tok, tok), 1)
    )
    counts = dot_nn(hot.astype(F32).astype(BF16), before.astype(F32).astype(BF16))
    pos = jnp.sum(jnp.where(hot, counts, 0.0), axis=0, keepdims=True).astype(jnp.int32)
    kept = pos < cap
    slot = jnp.where(kept, ids * capp + pos, -1)
    slot_ref[...] = slot
    pos_ref[...] = jnp.where(kept, pos, -1)
    rows = packed_ref.shape[0]
    step = 256

    @pl.loop(0, rows // step)
    def _(r):
        base = pl.multiple_of(r * step, step)
        table = (lax.broadcasted_iota(jnp.int32, (step, tok), 0) + base == slot)
        packed_ref[pl.ds(base, step), :] = dot_nn(
            table.astype(F32).astype(BF16), g_ref[...]
        ).astype(BF16)


def make_slots(experts, cap, capp, ids_row, g):
    tok, width = g.shape
    return pl.pallas_call(
        functools.partial(slots_kernel, experts, cap, capp),
        out_shape=(
            jax.ShapeDtypeStruct((1, tok), jnp.int32),
            jax.ShapeDtypeStruct((1, tok), jnp.int32),
            jax.ShapeDtypeStruct((experts * capp, width), BF16),
        ),
        compiler_params=pltpu.CompilerParams(vmem_limit_bytes=40 * MIB),
        cost_estimate=pl.CostEstimate(flops=5 * MICRO, bytes_accessed=4 * MIB, transcendentals=0),
        name="slots",
    )(ids_row, g)


def column(row_ref):
    row = row_ref[...]
    return jnp.broadcast_to(row, (8, row.shape[1])).T[:, :1]


def front_kernel(
    hid_ref, gain1_ref, wq_ref, wk_ref, wv_ref, wout_ref, tab_ref, gain2_ref, wr_ref,
    ids_ref, slot_ref, pos_ref, segr_ref, rel_ref,
    n1_ref, q_ref, k_ref, v_ref, p_ref, attn_ref, resid_ref, n2_ref, route_ref, gate_ref,
    packed_ref, gpack_ref,
    relt, mask, bias, lines,
):
    step = pl.program_id(0)
    seqs = segr_ref.shape[0]
    tok = hid_ref.shape[0]

    @pl.when(step == 0)
    def _():
        for t in range(0, tok, HALF):
            x = hid_ref[t:t + HALF, :].astype(F32).T
            scale = lax.rsqrt(jnp.mean(x * x, axis=0, keepdims=True) + EPS)
            n1_ref[:, t:t + HALF] = (x * scale * column(gain1_ref)).astype(BF16)
        relt[...] = rel_ref[...].T
        lines[...] = jnp.zeros_like(lines)
        lines[:HEADS, :BUCKETS] = tab_ref[...]
        for s in range(seqs):
            line = segr_ref[s:s + 1, :]
            across = jnp.broadcast_to(line, (LEN, LEN))
            mask[s] = jnp.where(across.T == across, 0.0, -1000000000.0)

    for w_ref, o_ref in ((wq_ref, q_ref), (wk_ref, k_ref), (wv_ref, v_ref)):
        o_ref[...] = dot_tn(w_ref[...], n1_ref[...]).astype(BF16)

    @pl.loop(0, GROUP)
    def _(h):
        head = step * GROUP + h
        row = lines[pl.ds(head, 1), :]
        line = jnp.broadcast_to(row, (LEN, LANES))
        for c in range(0, LEN, LANES):
            bias[:, c:c + LANES] = jnp.take_along_axis(line, relt[:, c:c + LANES], axis=1)
        at = pl.ds(pl.multiple_of(h * HEAD_DIM, HEAD_DIM), HEAD_DIM)
        out_at = pl.ds(pl.multiple_of(head * HEAD_DIM, HEAD_DIM), HEAD_DIM)
        for s in range(seqs):
            key = k_ref[at, s * LEN:(s + 1) * LEN]
            value = v_ref[at, s * LEN:(s + 1) * LEN]
            for c in range(0, LEN, HALF):
                cols = slice(s * LEN + c, s * LEN + c + HALF)
                query = q_ref[at, cols] * jnp.asarray(HEAD_DIM ** -0.5, BF16)
                score = dot_tn(key, query) + bias[:, c:c + HALF] + mask[s, :, c:c + HALF]
                peak = jnp.max(score, axis=0, keepdims=True)
                weight = jnp.exp(score - peak)
                total = jnp.sum(weight, axis=0, keepdims=True)
                prob = (weight * (1.0 / total)).astype(BF16)
                p_ref[h, s, :, c:c + HALF] = prob
                attn_ref[out_at, cols] = dot_nn(value, prob).astype(BF16)

    @pl.when(step == pl.num_programs(0) - 1)
    def _():
        experts = route_ref.shape[0]
        for t in range(0, tok, HALF):
            cols = slice(t, t + HALF)
            x = hid_ref[t:t + HALF, :].astype(F32).T
            resid = x + dot_tn(wout_ref[...], attn_ref[:, cols])
            resid_ref[:, cols] = resid
            scale = lax.rsqrt(jnp.mean(resid * resid, axis=0, keepdims=True) + EPS)
            n2 = (resid * scale * column(gain2_ref)).astype(BF16)
            n2_ref[:, cols] = n2
            logits = dot_nn(wr_ref[...], n2)
            top = jnp.max(logits, axis=0, keepdims=True)
            e = jnp.exp(logits - top)
            route = e / jnp.sum(e, axis=0, keepdims=True)
            route_ref[:, cols] = route
            hot = lax.broadcasted_iota(jnp.int32, (experts, HALF), 0) == ids_ref[:, cols]
            gate_ref[:, cols] = jnp.sum(jnp.where(hot, route, 0.0), axis=0, keepdims=True)
        hot = lax.broadcasted_iota(jnp.int32, (experts, tok), 0) == ids_ref[...]
        gates = jnp.where(hot, gate_ref[...], 0.0)
        place = (
            lax.broadcasted_iota(jnp.int32, (LANES, tok), 0) == pos_ref[...]
        ).astype(F32).astype(BF16)
        parts = [dot_nt(part, place) for part in split3(gates)]
        which = lax.broadcasted_iota(jnp.int32, (experts, 8, LANES), 1)
        spread = [jnp.broadcast_to(part[:, None, :], which.shape) for part in parts]
        gpack_ref[...] = jnp.where(
            which == 0, spread[0],
            jnp.where(which == 1, spread[1], jnp.where(which == 2, spread[2], 0.0)),
        ).astype(BF16)
        rows = packed_ref.shape[0]

        @pl.loop(0, rows // HALF)
        def _(r):
            base = pl.multiple_of(r * HALF, HALF)
            table = (lax.broadcasted_iota(jnp.int32, (HALF, tok), 0) + base == slot_ref[...])
            packed_ref[pl.ds(base, HALF), :] = dot_nt(
                table.astype(F32).astype(BF16), n2_ref[...]
            ).astype(BF16)


def front(hidden, gain1, w_qkv, w_out, table, gain2, w_router, ids, slot, pos, seg, rel, rows):
    tok, width = hidden.shape
    experts = w_router.shape[0]
    seqs = seg.shape[0]
    wspec = lambda part: pl.BlockSpec((width, GW), lambda i: (0, part * GROUPS + i))
    qspec = pl.BlockSpec((GW, tok), lambda i: (i, 0))
    sd = jax.ShapeDtypeStruct
    outs = (
        sd((width, tok), BF16), sd((width, tok), BF16), sd((width, tok), BF16),
        sd((width, tok), BF16), sd((HEADS, seqs, LEN, LEN), BF16), sd((width, tok), BF16),
        sd((width, tok), F32), sd((width, tok), BF16), sd((experts, tok), F32), sd((1, tok), F32),
        sd((rows, width), BF16), sd((experts, 8, LANES), BF16),
    )
    return pl.pallas_call(
        front_kernel,
        grid=(GROUPS,),
        in_specs=[
            whole((tok, width)), whole((1, width)), wspec(0), wspec(1), wspec(2),
            whole((width, width)), whole((HEADS, BUCKETS)), whole((1, width)),
            whole((experts, width)), whole((1, tok)), whole((1, tok)), whole((1, tok)),
            whole((seqs, LEN)), whole((LEN, LEN)),
        ],
        out_specs=(
            whole((width, tok)), qspec, qspec, qspec,
            pl.BlockSpec((GROUP, seqs, LEN, LEN), lambda i: (i, 0, 0, 0)),
            whole((width, tok)), whole((width, tok)), whole((width, tok)),
            whole((experts, tok)), whole((1, tok)), whole((rows, width)),
            whole((experts, 8, LANES)),
        ),
        out_shape=outs,
        scratch_shapes=[
            pltpu.VMEM((LEN, LEN), jnp.int32),
            pltpu.VMEM((seqs, LEN, LEN), F32),
            pltpu.VMEM((LEN, LEN), F32),
            pltpu.VMEM((16, LANES), F32),
        ],
        compiler_params=pltpu.CompilerParams(vmem_limit_bytes=58 * MIB),
        cost_estimate=pl.CostEstimate(flops=50 * MICRO, bytes_accessed=30 * MIB, transcendentals=0),
        name="front",
    )(
        hidden, gain1.reshape(1, width), w_qkv, w_qkv, w_qkv, w_out, table,
        gain2.reshape(1, width), w_router, ids, slot, pos,
        seg, rel,
    )


def combine_kernel(rows_ref, slot_ref, gate_ref, resid_ref, out_ref):
    total = rows_ref.shape[0]
    cols = slot_ref.shape[1]
    table = lax.broadcasted_iota(jnp.int32, (total, cols), 0) == slot_ref[...]
    combined = dot_tn(rows_ref[...], table.astype(F32).astype(BF16))
    out_ref[...] = (resid_ref[...] + gate_ref[...] * combined).T.astype(BF16)


def combine(rows, slot, gate, resid):
    total, width = rows.shape
    tok = slot.shape[1]
    line = pl.BlockSpec((1, HALF), lambda i: (0, i))
    return pl.pallas_call(
        combine_kernel,
        grid=(tok // HALF,),
        in_specs=[
            whole((total, width)), line, line, pl.BlockSpec((width, HALF), lambda i: (0, i)),
        ],
        out_specs=pl.BlockSpec((HALF, width), lambda i: (i, 0)),
        out_shape=jax.ShapeDtypeStruct((tok, width), BF16),
        compiler_params=pltpu.CompilerParams(vmem_limit_bytes=40 * MIB),
        cost_estimate=pl.CostEstimate(flops=6 * MICRO, bytes_accessed=8 * MIB, transcendentals=0),
        name="combine",
    )(rows, slot, gate, resid)


CUBE = 0.044715
ROOT = 0.7978845608028654
FTILE = 768


def gelu_pair(x):
    square = x * x
    t = jnp.tanh(ROOT * (x + CUBE * (x * square)))
    half = 0.5 + 0.5 * t
    slope = half + (0.5 * x) * (1.0 - t * t) * (ROOT + (3.0 * CUBE * ROOT) * square)
    return x * half, slope


def device_of(index):
    wide = lax.axis_size("wide")
    return (index // wide, lax.rem(index, wide))


def expert_kernel(
    block,
    packed, gpack, grows, w_in, w_down,
    dx_out, out_got, rest_out, active_out, ginner_out, gs_out, x_out, gg_out,
    xbuf, gatebuf, gbuf, win, wdown, active, slope, ginner, gs, dx, outs, ggsend, ggbuf,
    x_send, x_recv, gate_send, gate_recv, gg_ssem, gg_rsem, o_send, o_recv, self_sem, load_sem, store_sem,
):
    count = lax.axis_size("narrow") * lax.axis_size("wide")
    me = lax.axis_index("narrow") * lax.axis_size("wide") + lax.axis_index("wide")
    blocks = count // block
    mine = me // block
    capp = packed.shape[1]
    rows = block * capp
    total = count * capp
    hidden = w_in.shape[1]
    mesh_id = pl.DeviceIdType.MESH

    def x_copy(target, source):
        return pltpu.make_async_remote_copy(
            src_ref=packed.at[target], dst_ref=xbuf.at[source], send_sem=x_send.at[target],
            recv_sem=x_recv.at[source], device_id=device_of(target), device_id_type=mesh_id,
        )

    def gate_copy(target, source):
        return pltpu.make_async_remote_copy(
            src_ref=gpack.at[target], dst_ref=gatebuf.at[source], send_sem=gate_send.at[target],
            recv_sem=gate_recv.at[source], device_id=device_of(target), device_id_type=mesh_id,
        )

    def gg_copy(target, source):
        return pltpu.make_async_remote_copy(
            src_ref=ggsend.at[target], dst_ref=ggbuf.at[source], send_sem=gg_ssem.at[target],
            recv_sem=gg_rsem.at[source], device_id=device_of(target), device_id_type=mesh_id,
        )

    ahead = blocks // 2
    inner = lax.rem(me, block)

    def out_copy(c, j):
        target = lax.rem(mine + c, blocks) * block + j
        return pltpu.make_async_remote_copy(
            src_ref=outs.at[c * block + j], dst_ref=out_got.at[c * block + inner],
            send_sem=o_send.at[c * block + j], recv_sem=o_recv.at[c * block + inner],
            device_id=device_of(target), device_id_type=mesh_id,
        )

    def out_wait(c, j):
        return pltpu.make_async_remote_copy(
            src_ref=outs.at[c * block + j], dst_ref=out_got.at[c * block + j],
            send_sem=o_send.at[c * block + j], recv_sem=o_recv.at[c * block + j],
            device_id=device_of(lax.rem(me + 1, count)), device_id_type=mesh_id,
        )

    barrier = pltpu.get_barrier_semaphore()

    @pl.loop(1, count)
    def _(s):
        pl.semaphore_signal(
            barrier, inc=1, device_id=device_of(lax.rem(me + s, count)), device_id_type=mesh_id
        )

    loads = [
        pltpu.make_async_copy(w_in, win, load_sem.at[0]),
        pltpu.make_async_copy(w_down, wdown, load_sem.at[1]),
        pltpu.make_async_copy(grows, gbuf, load_sem.at[2]),
    ]
    own = [
        pltpu.make_async_copy(packed.at[me], xbuf.at[me], self_sem.at[0]),
        pltpu.make_async_copy(gpack.at[me], gatebuf.at[me], self_sem.at[1]),
    ]
    for copy in own + loads:
        copy.start()
    pl.semaphore_wait(barrier, count - 1)

    @pl.loop(0, blocks)
    def _(c):
        there = lax.rem(mine + blocks - c, blocks)

        @pl.loop(0, block)
        def _(j):
            target = there * block + j

            @pl.when(target != me)
            def _():
                gate_copy(target, me).start()
                x_copy(target, me).start()

    for copy in own + loads:
        copy.wait()

    def stores(at):
        return [
            pltpu.make_async_copy(dx.at[at], dx_out.at[at], store_sem.at[0]),
            pltpu.make_async_copy(active.at[at], active_out.at[at], store_sem.at[1]),
            pltpu.make_async_copy(ginner.at[at], ginner_out.at[at], store_sem.at[2]),
            pltpu.make_async_copy(gs.at[at], gs_out.at[at], store_sem.at[3]),
        ]

    @pl.loop(0, blocks)
    def _(c):
        here = lax.rem(mine + c, blocks)
        first = here * block

        @pl.loop(0, block)
        def _(j):
            source = first + j

            @pl.when(source != me)
            def _():
                gate_copy(me, source).wait_recv()
                x_copy(me, source).wait_recv()

        at = pl.ds(pl.multiple_of(here * rows, rows), rows)
        group = pl.ds(first, block)
        x = xbuf[group].reshape(rows, xbuf.shape[2])

        @pl.loop(0, hidden // FTILE)
        def _(f):
            tile = pl.ds(pl.multiple_of(f * FTILE, FTILE), FTILE)
            value, grad = gelu_pair(dot_nn(x, win[:, tile]))
            active[at, tile] = value.astype(BF16)
            slope[:, tile] = grad

        result = dot_nn(active[at, :], wdown[...]).astype(BF16)
        outs[pl.ds(c * block, block)] = result.reshape(block, capp, result.shape[1])

        @pl.when(c < ahead)
        def _():
            @pl.loop(0, block)
            def _(j):
                @pl.when(first + j != me)
                def _():
                    out_copy(c, j).start()

        g = gbuf[group].astype(F32)
        diag = (
            lax.broadcasted_iota(jnp.int32, (block, capp, LANES), 1)
            == lax.broadcasted_iota(jnp.int32, (block, capp, LANES), 2)
        )
        gate = jnp.sum(gatebuf[group].astype(F32), axis=1)
        gate = jnp.sum(
            jnp.where(diag, gate[:, None, :], 0.0), axis=2, keepdims=True
        )
        gs[at, :] = (gate * g).astype(BF16).reshape(rows, g.shape[2])
        gg = jnp.sum(g * result.astype(F32).reshape(g.shape), axis=2, keepdims=True)
        gg = jnp.sum(jnp.where(diag, gg, 0.0), axis=1)
        which = lax.broadcasted_iota(jnp.int32, (block, 8, LANES), 1)
        high, mid, low = [part.astype(F32)[:, None, :] for part in split3(gg)]
        ggsend[group] = jnp.where(
            which == 0, high, jnp.where(which == 1, mid, jnp.where(which == 2, low, 0.0))
        ).astype(BF16)

        @pl.loop(0, block)
        def _(j):
            source = first + j

            @pl.when(source != me)
            def _():
                gg_copy(source, me).start()

        @pl.loop(0, hidden // FTILE)
        def _(f):
            tile = pl.ds(pl.multiple_of(f * FTILE, FTILE), FTILE)
            grad = dot_nt(gs[at, :], wdown[tile, :])
            ginner[at, tile] = (grad * slope[:, tile]).astype(BF16)

        dx[at, :] = dot_nt(ginner[at, :], win[...]).astype(BF16)

        for copy in stores(at):
            copy.start()

    for copy in stores(pl.ds(0, total)):
        copy.wait()
    keep = [
        pltpu.make_async_copy(xbuf, x_out, load_sem.at[0]),
        pltpu.make_async_copy(ggsend.at[me], ggbuf.at[me], self_sem.at[0]),
        pltpu.make_async_copy(outs.at[inner], out_got.at[inner], self_sem.at[1]),
        pltpu.make_async_copy(
            outs.at[pl.ds(ahead * block, count - ahead * block)], rest_out, load_sem.at[1]
        ),
    ]
    for copy in keep:
        copy.start()

    @pl.loop(0, count)
    def _(other):
        @pl.when(other != me)
        def _():
            x_copy(other, me).wait_send()
            gate_copy(other, me).wait_send()
            gg_copy(other, me).wait_send()
            gg_copy(me, other).wait_recv()

    @pl.loop(0, ahead * block)
    def _(i):
        @pl.when(i != inner)
        def _():
            out_wait(i // block, lax.rem(i, block)).wait_send()
            out_wait(i // block, lax.rem(i, block)).wait_recv()

    for copy in keep:
        copy.wait()
    last = pltpu.make_async_copy(ggbuf, gg_out, load_sem.at[1])
    last.start()
    last.wait()


def block_of(count, capp):
    block = 1
    while block * 4 <= count and block * 2 * capp <= 320:
        block *= 2
    return block


def expert(packed, gpack, grows, w_in, w_down):
    count, capp, width = packed.shape
    hidden = w_in.shape[1]
    block = block_of(count, capp)
    early = (count // block // 2) * block
    rows = block * capp
    total = count * capp
    sd = jax.ShapeDtypeStruct
    anyspec = pl.BlockSpec(memory_space=pl.ANY)
    dma = pltpu.SemaphoreType.DMA
    return pl.pallas_call(
        functools.partial(expert_kernel, block),
        in_specs=[anyspec] * 5,
        out_specs=(anyspec,) * 8,
        out_shape=(
            sd((total, width), BF16), sd((early, capp, width), BF16),
            sd((count - early, capp, width), BF16), sd((total, hidden), BF16), sd((total, hidden), BF16), sd((total, width), BF16), sd((count, capp, width), BF16),
            sd((count, 8, LANES), BF16),
        ),
        scratch_shapes=[
            pltpu.VMEM((count, capp, width), BF16), pltpu.VMEM((count, 8, LANES), BF16),
            pltpu.VMEM((count, capp, width), BF16), pltpu.VMEM((width, hidden), BF16),
            pltpu.VMEM((hidden, width), BF16), pltpu.VMEM((total, hidden), BF16),
            pltpu.VMEM((rows, hidden), F32), pltpu.VMEM((total, hidden), BF16),
            pltpu.VMEM((total, width), BF16), pltpu.VMEM((total, width), BF16),
            pltpu.VMEM((count, capp, width), BF16), pltpu.VMEM((count, 8, LANES), BF16),
            pltpu.VMEM((count, 8, LANES), BF16),
            dma((count,)), dma((count,)), dma((count,)), dma((count,)), dma((count,)), dma((count,)),
            dma((early,)), dma((early,)), dma((2,)), dma((3,)), dma((4,)),
        ],
        compiler_params=pltpu.CompilerParams(
            collective_id=0, has_side_effects=True, vmem_limit_bytes=62 * MIB
        ),
        cost_estimate=pl.CostEstimate(flops=60 * MICRO, bytes_accessed=60 * 1024 * 1024, transcendentals=0),
        name="expert",
    )(packed, gpack, grows, w_in, w_down)


def weights_kernel(active_ref, gs_ref, x_ref, ginner_ref, down_ref, in_ref, xt):
    @pl.when(pl.program_id(0) == 0)
    def _():
        total = x_ref.shape[0]
        for t in range(0, total, HALF):
            xt[:, t:t + HALF] = x_ref[t:t + HALF, :].T

    down_ref[0] = dot_tn(active_ref[...], gs_ref[...])
    in_ref[0] = dot_nn(xt[...], ginner_ref[...])


def weight_grads(active, gs, x, ginner):
    total, hidden = active.shape
    width = gs.shape[1]
    tile = HALF
    cols = pl.BlockSpec((total, tile), lambda i: (0, i))
    return pl.pallas_call(
        weights_kernel,
        grid=(hidden // tile,),
        in_specs=[cols, whole((total, width)), whole((total, width)), cols],
        out_specs=(
            pl.BlockSpec((1, tile, width), lambda i: (0, i, 0)),
            pl.BlockSpec((1, width, tile), lambda i: (0, 0, i)),
        ),
        out_shape=(
            jax.ShapeDtypeStruct((1, hidden, width), F32),
            jax.ShapeDtypeStruct((1, width, hidden), F32),
        ),
        scratch_shapes=[pltpu.VMEM((width, total), BF16)],
        compiler_params=pltpu.CompilerParams(vmem_limit_bytes=62 * MIB),
        cost_estimate=pl.CostEstimate(flops=18 * MICRO, bytes_accessed=36 * 1024 * 1024, transcendentals=0),
        name="weight_grads",
    )(active, gs, x, ginner)
PIECES = 32
BIG = 2
UNITS = BIG + GROUPS
TROWS = 16
LATE = 24
LAST_PHASE = 7


def norm_back(grad, source, gain):
    scale = lax.rsqrt(jnp.mean(source * source, axis=0, keepdims=True) + EPS)
    normed = source * scale
    scaled = grad * gain
    inner = jnp.mean(scaled * normed, axis=0, keepdims=True)
    part = grad * normed
    part = part[:, :LANES] + part[:, LANES:]
    return scale * (scaled - normed * inner), part


def back_kernel(
    block,
    dx_ref, gg_ref, slot_ref, pos_ref, ids_ref, route_ref, gate_ref, n2_ref, attn_ref,
    gain1_ref, gain2_ref, wr_ref, wout_ref, resid_any, g_any, hid_any, n1_any, q_any, k_any, v_any, p_any,
    wqkv_any, rel_any, rest_any,
    ingrad_any, out_got, big_out, small_out, early_out, late_out,
    gres, ga, gn1, dv, soft, hid_ref, n1_ref, q_ref, k_ref, v_ref, wqkv_ref, rel_ref, acc,
    *buffers_and_rest,
):
    buffers = buffers_and_rest[:16]
    inside = buffers[7].shape == big_out.shape
    big = buffers[:7] + (buffers[7] if inside else big_out,)
    small = buffers[8:15] + (buffers[15] if inside else small_out,)
    (
        early, early_got, late, late_got, send, recv, xsend, xrecv, esend, erecv, lsend, lrecv, osend, orecv, load_sem, store_sem, stage_sem, write_sem,
    ) = buffers_and_rest[16:]
    dq, dk = dv.at[pl.ds(0, GW)], dv.at[pl.ds(GW, GW)]
    step = pl.program_id(0)
    pair = pl.program_id(1)
    tok = g_any.shape[0]
    seqs = tok // LEN
    experts = route_ref.shape[0]
    total = dx_ref.shape[0]
    width = g_any.shape[1]
    narrow_n, wide_n = lax.axis_size("narrow"), lax.axis_size("wide")
    n, w = lax.axis_index("narrow"), lax.axis_index("wide")
    core, zed = lax.rem(w, 2), lax.rem(w // 2, 4)
    ex, why = lax.rem(n, 2), lax.rem(n // 2, 2)
    more_n = (narrow_n // 4) * (wide_n // 8)
    more_w = wide_n // 8
    more = (n // 4) * more_w + w // 8
    mesh_id = pl.DeviceIdType.MESH
    core_dev = (n, w + 1 - 2 * core)
    ex_dev = (n + 1 - 2 * ex, w)
    why_dev = (n + 2 - 4 * why, w)

    def zed_dev(step):
        return (n, w + 2 * (lax.rem(zed + step, 4) - zed))

    def more_dev(step):
        other = lax.rem(more + step, more_n)
        return (n + 4 * (other // more_w - more // more_w),
                w + 8 * (lax.rem(other, more_w) - lax.rem(more, more_w)))

    def unit(u):
        if isinstance(u, int):
            return (big, u, u) if u < BIG else (small, u - BIG, u)
        return small, u, u + BIG

    def ref(which, u):
        group, at, _ = unit(u)
        return group[which], at

    def view(which, u, *more):
        group, at, _ = unit(u)
        return group[which].at[(at,) + more]

    def land(u, q, at):
        return view(7, u, q, at)

    def spot(q):
        first, second = (ex, why) if q == 0 else (why, ex)
        b16 = core * 16
        b8 = b16 + first * 8
        b4 = b8 + second * 4
        return first, second, b16, b8, b4

    def remote(src, dst, k, u, q, dev):
        return pltpu.make_async_remote_copy(
            src_ref=src, dst_ref=dst, send_sem=send.at[k, unit(u)[2], q], recv_sem=recv.at[k, unit(u)[2], q],
            device_id=dev, device_id_type=mesh_id,
        )

    def outgoing(phase, u, q):
        first, second, b16, b8, b4 = spot(q)
        one, two = (ex_dev, why_dev) if q == 0 else (why_dev, ex_dev)
        if phase == 0:
            return [remote(view(0, u, q, pl.ds(16 - b16, 16)), view(2, u, q), 0, u, q, core_dev)]
        if phase == 1:
            src = view(0, u, q, pl.ds(b16 + (1 - first) * 8, 8))
            return [remote(src, view(3, u, q), 1, u, q, one)]
        if phase == 2:
            src = view(0, u, q, pl.ds(b8 + (1 - second) * 4, 4))
            return [remote(src, view(4, u, q), 2, u, q, two)]
        if phase == 3:
            return [
                remote(view(0, u, q, b4 + lax.rem(zed + step, 4)), view(5, u, q, step - 1),
                       2 + step, u, q, zed_dev(step))
                for step in (1, 2, 3)
            ]
        if phase == 4:
            mine = land(u, q, b4 + zed)
            return [remote(view(1, u, q), mine, 5 + step, u, q, zed_dev(step)) for step in (1, 2, 3)]
        if phase == 5:
            mine = land(u, q, pl.ds(b4, 4))
            return [remote(mine, mine, 9, u, q, two)]
        if phase == 6:
            mine = land(u, q, pl.ds(b8, 8))
            return [remote(mine, mine, 10, u, q, one)]
        mine = land(u, q, pl.ds(b16, 16))
        return [remote(mine, mine, 11, u, q, core_dev)]

    def incoming(phase, u, q):
        first, second, b16, b8, b4 = spot(q)
        if phase < 4:
            return outgoing(phase, u, q)
        if phase == 4:
            return [
                remote(view(1, u, q), land(u, q, b4 + lax.rem(zed + 4 - step, 4)),
                       5 + step, u, q, zed_dev(step))
                for step in (1, 2, 3)
            ]
        if phase == 5:
            there = land(u, q, pl.ds(b8 + (1 - second) * 4, 4))
            return [remote(there, there, 9, u, q, core_dev)]
        if phase == 6:
            there = land(u, q, pl.ds(b16 + (1 - first) * 8, 8))
            return [remote(there, there, 10, u, q, core_dev)]
        there = land(u, q, pl.ds(16 - b16, 16))
        return [remote(there, there, 11, u, q, core_dev)]

    def add(u, q, start, count, which):
        own, at = ref(0, u)
        got = ref(which, u)[0]

        @pl.loop(0, count)
        def _(i):
            own[at, q, start + i] = (
                own[at, q, start + i].astype(F32) + got[at, q, i].astype(F32)
            ).astype(BF16)

    def spread(u, q):
        (done, at), (extra, _) = ref(1, u), ref(6, u)
        extra[at, q, more] = done[at, q]
        copies = [
            pltpu.make_async_remote_copy(
                src_ref=view(6, u, q, more), dst_ref=view(6, u, q, more),
                send_sem=xsend.at[unit(u)[2], q, step], recv_sem=xrecv.at[unit(u)[2], q, step],
                device_id=more_dev(step), device_id_type=mesh_id,
            )
            for step in range(1, more_n)
        ]
        for copy in copies:
            copy.start()
        for step in range(1, more_n):
            other = lax.rem(more + more_n - step, more_n)
            pltpu.make_async_remote_copy(
                src_ref=view(6, u, q, more), dst_ref=view(6, u, q, other),
                send_sem=xsend.at[unit(u)[2], q, step], recv_sem=xrecv.at[unit(u)[2], q, step],
                device_id=more_dev(step), device_id_type=mesh_id,
            ).wait_recv()
        for copy in copies:
            copy.wait_send()
        total = extra[at, q, 0].astype(F32)
        for i in range(1, more_n):
            total = total + extra[at, q, i].astype(F32)
        done[at, q] = total.astype(BF16)

    def keep(u, q):
        at = spot(q)[4] + zed
        return pltpu.make_async_copy(view(1, u, q), land(u, q, at), store_sem.at[unit(u)[2], q])

    def settle(phase, u, q):
        first, second, b16, b8, b4 = spot(q)
        if phase == 0:
            add(u, q, b16, 16, 2)
        elif phase == 1:
            add(u, q, b8, 8, 3)
        elif phase == 2:
            add(u, q, b4, 4, 4)
        elif phase == 3:
            (own, at), (done, _), (got, _) = ref(0, u), ref(1, u), ref(5, u)
            done[at, q] = (
                own[at, q, b4 + zed].astype(F32) + got[at, q, 0].astype(F32)
                + (got[at, q, 1].astype(F32) + got[at, q, 2].astype(F32))
            ).astype(BF16)
            if more_n > 1:
                spread(u, q)
            keep(u, q).start()
        elif phase == 4:
            keep(u, q).wait()

    bits = []
    for axis, count in (("wide", wide_n), ("narrow", narrow_n)):
        size = 1
        while size < count:
            at = lax.rem((w if axis == "wide" else n) // size, 2)
            move = size - 2 * size * at
            bits.append((n, w + move) if axis == "wide" else (n + move, w))
            size *= 2
    levels = len(bits)
    early_levels = early_got.shape[0] if early.shape[0] > 1 else 0

    def swap(level, mine, got, ssem, rsem):
        return pltpu.make_async_remote_copy(
            src_ref=mine.at[level], dst_ref=got.at[level], send_sem=ssem.at[level],
            recv_sem=rsem.at[level], device_id=bits[level], device_id_type=mesh_id,
        )

    def climb(level, mine, got, ssem, rsem):
        copy = swap(level, mine, got, ssem, rsem)
        copy.wait_recv()
        copy.wait_send()
        mine[level + 1] = mine[level] + got[level]
        if level + 1 < levels:
            swap(level + 1, mine, got, ssem, rsem).start()

    def climb_early(level):
        climb(level, early, early_got, esend, erecv)

    def climb_late(level):
        climb(level, late, late_got, lsend, lrecv)

    count = narrow_n * wide_n
    blocks = count // block
    ahead = blocks // 2
    index = n * wide_n + w
    rest = rest_any.shape[0]

    def out_copy(i):
        target = lax.rem(index // block + ahead + i // block, blocks) * block + lax.rem(i, block)
        return pltpu.make_async_remote_copy(
            src_ref=rest_any.at[i],
            dst_ref=out_got.at[(i // block) * block + lax.rem(index, block)],
            send_sem=osend.at[i], recv_sem=orecv.at[(i // block) * block + lax.rem(index, block)],
            device_id=device_of(target), device_id_type=mesh_id,
        )

    def out_wait(i):
        return pltpu.make_async_remote_copy(
            src_ref=rest_any.at[i], dst_ref=out_got.at[i], send_sem=osend.at[i],
            recv_sem=orecv.at[i], device_id=core_dev, device_id_type=mesh_id,
        )

    def begin(u):
        for q in range(2):
            for copy in outgoing(0, u, q):
                copy.start()

    def advance(u, phase):
        for q in range(2):
            for copy in incoming(phase, u, q):
                copy.wait_recv()
            for copy in outgoing(phase, u, q):
                copy.wait_send()
            settle(phase, u, q)
            if phase < LAST_PHASE:
                for copy in outgoing(phase + 1, u, q):
                    copy.start()
        if inside and phase == LAST_PHASE:
            write_out(u).start()

    def write_out(u):
        group, at, flat = unit(u)
        out = big_out if u < BIG else small_out
        return pltpu.make_async_copy(group[7].at[at], out.at[at], write_sem.at[flat])

    def place(u, first, value):
        own, at = ref(0, u)
        half = own.shape[4]
        count = value.shape[1]
        blocks = value.reshape(PIECES, width // PIECES, count).astype(BF16)
        done = 0
        while done < count:
            q, within = (first + done) // half, (first + done) % half
            size = min(half - within, count - done)
            own[at, q, :, :, within:within + size] = blocks[:, :, done:done + size]
            done += size

    def soft_load(group):
        at = pl.ds(group * GROUP, GROUP)
        return pltpu.make_async_copy(p_any.at[at], soft.at[at], load_sem.at[group])

    pairs = ((q_any, q_ref), (k_any, k_ref), (v_any, v_ref), (n1_any, n1_ref), (wqkv_any, wqkv_ref),
             (rel_any, rel_ref))
    loads = [
        pltpu.make_async_copy(src, dst, load_sem.at[GROUPS + i]) for i, (src, dst) in enumerate(pairs)
    ]

    rows_load = [
        pltpu.make_async_copy(src, hid_ref, load_sem.at[GROUPS + 6 + i])
        for i, src in enumerate((g_any, hid_any))
    ]

    barrier = pltpu.get_barrier_semaphore()
    greet = [core_dev, ex_dev, why_dev] + [zed_dev(move) for move in (1, 2, 3)]
    greet += [more_dev(move) for move in range(1, more_n)] + bits

    @pl.when((step == 0) & (pair == 0))
    def _():
        first = pltpu.make_async_copy(resid_any, gres, stage_sem)
        first.start()
        rows_load[0].start()
        soft_load(0).start()
        for copy in loads:
            copy.start()
        for group in range(1, GROUPS):
            soft_load(group).start()
        for dev in greet:
            pl.semaphore_signal(barrier, inc=1, device_id=dev, device_id_type=mesh_id)

        @pl.loop(0, rest)
        def _(i):
            source = lax.rem(
                index // block + 2 * blocks - ahead - i // block, blocks
            ) * block + lax.rem(i, block)
            pl.semaphore_signal(
                barrier, inc=1, device_id=device_of(source), device_id_type=mesh_id
            )

        pl.semaphore_wait(barrier, len(greet) + rest)

        @pl.loop(0, rest)
        def _(i):
            out_copy(i).start()

        hot = lax.broadcasted_iota(jnp.int32, (experts, tok), 0) == ids_ref[...]
        where = (
            lax.broadcasted_iota(jnp.int32, (LANES, tok), 0) == pos_ref[...]
        ).astype(F32).astype(BF16)
        grad_gate = jnp.zeros((1, tok), F32)
        for e in range(0, experts, 32):
            found = dot_nn(gg_ref[e:e + 32].reshape(256, LANES), where)
            found = jnp.sum(found.reshape(32, 8, tok), axis=1)
            grad_gate += jnp.sum(jnp.where(hot[e:e + 32], found, 0.0), axis=0, keepdims=True)
        first.wait()
        rows_load[0].wait()
        grad_logits = (
            (grad_gate * gate_ref[...]) * (hot.astype(F32) - route_ref[...])
        ).astype(BF16)
        early[0, :experts, :] = dot_nt(grad_logits, n2_ref[...])
        gain_grad = jnp.zeros((width, LANES), F32)
        for t in range(0, tok, HALF):
            cols = slice(t, t + HALF)
            gn2 = dot_tn(wr_ref[...], grad_logits[:, cols])
            size = total if total <= 1280 else 512
            for r in range(0, total, size):
                table = lax.broadcasted_iota(jnp.int32, (size, HALF), 0) + r == slot_ref[:, cols]
                gn2 = gn2 + dot_tn(dx_ref[r:r + size, :], table.astype(F32).astype(BF16))
            branch, part = norm_back(gn2, gres[:, cols], column(gain2_ref))
            gain_grad = gain_grad + part
            gr = hid_ref[t:t + HALF, :].astype(F32).T + branch
            gres[:, cols] = gr
            ga[:, cols] = gr.astype(BF16)
        early[0, experts:, :] = jnp.broadcast_to(
            jnp.sum(gain_grad.T, axis=0, keepdims=True), (8, width)
        )
        for c in range(0, width, HALF):
            place(0, c, dot_nt(attn_ref[...], ga[c:c + HALF, :]))
        rows_load[1].start()
        begin(0)
        if early_levels:
            swap(0, early, early_got, esend, erecv).start()
        for t in range(0, tok, HALF):
            cols = slice(t, t + HALF)
            ga[:, cols] = dot_nn(wout_ref[...], ga[:, cols]).astype(BF16)
        soft_load(0).wait()
        for copy in loads:
            copy.wait()
        for group in range(1, GROUPS):
            soft_load(group).wait()

        @pl.loop(0, HEADS)
        def _(head):
            at = pl.ds(pl.multiple_of(head * HEAD_DIM, HEAD_DIM), HEAD_DIM)
            for s in range(seqs):
                row = slice(s * LEN, (s + 1) * LEN)
                dv[at, row] = dot_nt(ga[at, row], soft[head, s]).astype(BF16)

        for c in range(0, width, GW):
            place(1, c, dot_nt(n1_ref[...], dv[c:c + GW, :]))
        begin(1)
        for t in range(0, tok, HALF):
            gn1[:, t:t + HALF] = dot_nn(wqkv_ref[:, 2 * width:], dv[:, t:t + HALF])

    @pl.loop(0, PAIR)
    def _(h):
        turn = pair * PAIR + h
        head = step * GROUP + turn
        at = pl.ds(pl.multiple_of(turn * HEAD_DIM, HEAD_DIM), HEAD_DIM)
        all_at = pl.ds(pl.multiple_of(head * HEAD_DIM, HEAD_DIM), HEAD_DIM)
        for s in range(seqs):
            row = slice(s * LEN, (s + 1) * LEN)
            value = v_ref[all_at, row]
            for c in range(0, LEN, HALF):
                cols = slice(s * LEN + c, s * LEN + c + HALF)
                grad = ga[all_at, cols]
                inner = jnp.sum(
                    grad.astype(F32) * attn_ref[all_at, cols].astype(F32), axis=0, keepdims=True
                )
                gp = dot_tn(value, grad)
                soft[head, s, :, c:c + HALF] = (
                    soft[head, s, :, c:c + HALF].astype(F32) * (gp - inner)
                ).astype(BF16)
            ds = soft[head, s]
            factor = HEAD_DIM ** -0.5
            dq[at, row] = (dot_nn(k_ref[all_at, row], ds) * factor).astype(BF16)
            dk[at, row] = (dot_nt(q_ref[all_at, row], ds) * factor).astype(BF16)

        for number in range(HEADS):
            todo = [(u, phase) for u, phase, at_head in SCHEDULE if at_head == number]
            rise = [level for level, at_head in enumerate(EARLY_LEVELS)
                    if at_head == number and level < early_levels]
            if todo or rise:
                @pl.when(head == number)
                def _():
                    for u, phase in todo:
                        advance(u, phase)
                    for level in rise:
                        climb_early(level)

    @pl.when(pair == pl.num_programs(1) - 1)
    def _():
        for part, d in enumerate((dq, dk)):
            place(step, part * GW, dot_nt(n1_ref[...], d[...]))
        begin(step)
        for part, d in enumerate((dq, dk)):
            cols = pl.ds(pl.multiple_of(part * width + step * GW, GW), GW)
            gn1[...] += dot_nn(wqkv_ref[:, cols], d[...])

    @pl.when((step == pl.num_programs(0) - 1) & (pair == pl.num_programs(1) - 1))
    def _():
        planned = {(u, phase) for u, phase, at_head in SCHEDULE}
        left = {u: [phase for phase in range(LAST_PHASE + 1) if (u, phase) not in planned]
                for u in range(UNITS)}

        def push():
            for u in range(UNITS):
                if left[u]:
                    advance(u, left[u].pop(0))

        rows_load[1].wait()
        gain_grad = jnp.zeros((width, LANES), F32)
        for t in range(0, tok, HALF):
            cols = slice(t, t + HALF)
            x = hid_ref[t:t + HALF, :].astype(F32).T
            branch, part = norm_back(gn1[:, cols], x, column(gain1_ref))
            gain_grad = gain_grad + part
            gres[:, cols] = gres[:, cols] + branch
            if t == HALF:
                push()
        pltpu.make_async_copy(gres, ingrad_any, stage_sem).start()
        line = jnp.sum(gain_grad.T, axis=0, keepdims=True)
        late[0] = jnp.zeros((LATE, LANES), F32)
        for i in range(width // LANES):
            late[0, i:i + 1, :] = line[:, i * LANES:(i + 1) * LANES]
        push()
        lines = HEADS * seqs
        acc[...] = jnp.zeros_like(acc)
        chunks = 4
        for chunk in range(chunks):
            @pl.loop(chunk * (LEN // TROWS // chunks), (chunk + 1) * (LEN // TROWS // chunks))
            def _(r):
                base = pl.multiple_of(r * TROWS, TROWS)
                lhs = soft[:, :, pl.ds(base, TROWS), :].reshape(lines * TROWS, LEN)
                rel = rel_ref[pl.ds(base, TROWS), :]
                hot = (
                    rel[:, None, :]
                    == lax.broadcasted_iota(jnp.int32, (TROWS, BUCKETS, LEN), 1)
                ).astype(F32).astype(BF16).reshape(TROWS * BUCKETS, LEN)
                acc[...] += dot_nt(lhs, hot)

            push()
        rows = lax.broadcasted_iota(jnp.int32, acc.shape, 0) % TROWS
        cols = lax.broadcasted_iota(jnp.int32, acc.shape, 1) // BUCKETS
        kept = jnp.where(rows == cols, acc[...], 0.0)
        per_head = jnp.sum(kept.reshape(HEADS, seqs * TROWS, acc.shape[1]), axis=1)
        fold = (
            lax.broadcasted_iota(jnp.int32, (LANES, acc.shape[1]), 1) % BUCKETS
            == lax.broadcasted_iota(jnp.int32, (LANES, acc.shape[1]), 0)
        ).astype(F32)
        late[0, 8:8 + HEADS, :] = lax.dot_general(
            per_head, fold, (((1,), (1,)), ((), ())), precision=lax.Precision.HIGHEST,
            preferred_element_type=F32,
        )
        swap(0, late, late_got, lsend, lrecv).start()
        level = 0
        while any(left.values()) or level < levels:
            push()
            if level < levels:
                climb_late(level)
                level += 1
        for level in range(early_levels):
            if level >= len(EARLY_LEVELS):
                climb_early(level)
        pltpu.make_async_copy(gres, ingrad_any, stage_sem).wait()

        @pl.loop(0, rest)
        def _(i):
            out_wait(i).wait_send()
            out_wait(i).wait_recv()

        if inside:
            for u in range(UNITS):
                write_out(u).wait()
        early_out[...] = early[early_levels]
        late_out[...] = late[levels]


EARLY_MOST = 64
EARLY_LEVELS = (1, 3, 5, 7, 9)
SCHEDULE = (
    [(0, phase, at) for phase, at in enumerate((0, 2, 4, 6, 8, 10))]
    + [(1, phase, at) for phase, at in enumerate((1, 3, 5, 8, 11))]
    + [(2, phase, at) for phase, at in enumerate((5, 7, 10))]
    + [(3, phase, at) for phase, at in enumerate((9, 11))]
)


def back(dx, gg, slot, pos, ids, route, gate, resid, n2, attn, g, hidden, n1, q, k, v, p, gain1, gain2,
         w_router, w_out, w_qkv, relt, rest, block):
    tok, width = hidden.shape
    experts = w_router.shape[0]
    total = dx.shape[0]
    seqs = p.shape[1]
    narrow_n, wide_n = lax.axis_size("narrow"), lax.axis_size("wide")
    levels = (narrow_n * wide_n).bit_length() - 1
    more_n = (narrow_n // 4) * (wide_n // 8)
    early_levels = levels if experts <= EARLY_MOST else 0
    rows = width // PIECES
    anyspec = pl.BlockSpec(memory_space=pl.ANY)
    sd = jax.ShapeDtypeStruct
    dma = pltpu.SemaphoreType.DMA
    vm = pltpu.VMEM

    def bufs(number, half):
        return [
            vm((number, 2) + lead + (rows, half), BF16)
            for lead in ((PIECES,), (), (16,), (8,), (4,), (3,), (more_n,))
        ] + [vm((number, 2, PIECES, rows, half) if more_n == 1 else (8, LANES), BF16)]

    return pl.pallas_call(
        functools.partial(back_kernel, block),
        grid=(GROUPS, GROUP // PAIR),
        in_specs=[
            whole((total, width)), whole((experts, 8, LANES)), whole((1, tok)), whole((1, tok)),
            whole((1, tok)), whole((experts, tok)), whole((1, tok)), whole((width, tok)),
            whole((width, tok)), whole((1, width)), whole((1, width)),
            whole((experts, width)), whole((width, width)),
        ] + [anyspec] * 11,
        out_specs=(
            anyspec, anyspec, anyspec, anyspec, whole((experts + 8, width)), whole((LATE, LANES)),
        ),
        out_shape=(
            sd((width, tok), F32), sd(rest.shape, BF16), sd((BIG, 2, PIECES, rows, width // 2), BF16),
            sd((GROUPS, 2, PIECES, rows, GW), BF16),
            sd((experts + 8, width), F32), sd((LATE, LANES), F32),
        ),
        scratch_shapes=[
            vm((width, tok), F32), vm((width, tok), BF16), vm((width, tok), F32),
            vm((width, tok), BF16),
            vm((HEADS, seqs, LEN, LEN), BF16), vm((tok, width), BF16), vm((width, tok), BF16),
            vm((width, tok), BF16), vm((width, tok), BF16), vm((width, tok), BF16),
            vm(w_qkv.shape, BF16), vm((LEN, LEN), jnp.int32), vm((HEADS * seqs * TROWS, TROWS * BUCKETS), F32),
            *bufs(BIG, width // 2), *bufs(GROUPS, GW),
            vm((early_levels + 1, experts + 8, width), F32),
            vm((max(early_levels, 1), experts + 8, width) if early_levels else (1, 8, width), F32),
            vm((levels + 1, LATE, LANES), F32), vm((levels, LATE, LANES), F32),
            dma((12, UNITS, 2)), dma((12, UNITS, 2)), dma((UNITS, 2, more_n)),
            dma((UNITS, 2, more_n)), dma((levels,)), dma((levels,)), dma((levels,)), dma((levels,)),
            dma((rest.shape[0],)), dma((rest.shape[0],)),
            dma((GROUPS + 8,)), dma((UNITS, 2)), dma(()), dma((UNITS,)),
        ],
        compiler_params=pltpu.CompilerParams(
            collective_id=1, has_side_effects=True, vmem_limit_bytes=63 * MIB
        ),
        cost_estimate=pl.CostEstimate(flops=80 * MICRO, bytes_accessed=50 * MIB, transcendentals=0),
        name="back",
    )(
        dx, gg, slot, pos, ids, route, gate, n2, attn, gain1.reshape(1, width),
        gain2.reshape(1, width), w_router, w_out, resid, g, hidden, n1, q, k, v, p, w_qkv, relt, rest,
    )


def finish_kernel(
    early_ref, late_ref, slot_ref, gate_ref, resid_ref, big_ref, small_ref, grad_ref,
    router_ref, tail_ref,
    out_ref, qkv_ref, proj_ref, ingrad_ref, gain1_ref, gain2_ref, table_ref, routerg_ref,
):

    @pl.when(pl.program_id(0) == 0)
    def _():
        experts = routerg_ref.shape[0]
        for i in range(gain1_ref.shape[1] // LANES):
            gain1_ref[:, i * LANES:(i + 1) * LANES] = tail_ref[i:i + 1, :]
        gain2_ref[...] = router_ref[experts:experts + 1, :]
        table_ref[...] = tail_ref[8:8 + HEADS, :BUCKETS]
        routerg_ref[...] = router_ref[:experts, :]

    ingrad_ref[...] = grad_ref[...].T
    rows_a = early_ref.shape[0]
    cols = slot_ref.shape[1]
    combined = None
    for base, ref in ((0, early_ref), (rows_a, late_ref)):
        table = (
            lax.broadcasted_iota(jnp.int32, (ref.shape[0], cols), 0) + base == slot_ref[...]
        )
        part = dot_tn(ref[...], table.astype(F32).astype(BF16))
        combined = part if combined is None else combined + part
    out_ref[...] = (resid_ref[...] + gate_ref[...] * combined).T.astype(BF16)
    rows = qkv_ref.shape[0]
    half = big_ref.shape[4]
    width = 2 * half
    for q in range(2):
        proj_ref[:, q * half:(q + 1) * half] = big_ref[0, q].astype(F32).reshape(rows, half)
        start = 2 * width + q * half
        qkv_ref[:, start:start + half] = big_ref[1, q].astype(F32).reshape(rows, half)
        for group in range(GROUPS):
            start = q * width + group * GW
            qkv_ref[:, start:start + GW] = small_ref[group, q].astype(F32).reshape(rows, GW)


def finish(out_a, out_b, slot, gate, resid, big, small, grad, router, tail):
    tok = slot.shape[1]
    width = resid.shape[0]
    steps = tok // HALF
    line = pl.BlockSpec((1, HALF), lambda i: (0, i))
    pieces = big.shape[2] // steps
    rows = width // steps
    return pl.pallas_call(
        finish_kernel,
        grid=(steps,),
        in_specs=[
            whole(out_a.shape), whole(out_b.shape), line, line,
            pl.BlockSpec((width, HALF), lambda i: (0, i)),
            pl.BlockSpec(big.shape[:2] + (pieces,) + big.shape[3:], lambda i: (0, 0, i, 0, 0)),
            pl.BlockSpec(small.shape[:2] + (pieces,) + small.shape[3:], lambda i: (0, 0, i, 0, 0)),
            pl.BlockSpec((width, HALF), lambda i: (0, i)), whole(router.shape), whole(tail.shape),
        ],
        out_specs=(
            pl.BlockSpec((HALF, width), lambda i: (i, 0)),
            pl.BlockSpec((rows, 3 * width), lambda i: (i, 0)),
            pl.BlockSpec((rows, width), lambda i: (i, 0)),
            pl.BlockSpec((HALF, width), lambda i: (i, 0)), whole((1, width)), whole((1, width)),
            whole((HEADS, BUCKETS)), whole((router.shape[0] - 8, width)),
        ),
        out_shape=(
            jax.ShapeDtypeStruct((tok, width), BF16),
            jax.ShapeDtypeStruct((width, 3 * width), F32),
            jax.ShapeDtypeStruct((width, width), F32),
            jax.ShapeDtypeStruct((tok, width), F32), jax.ShapeDtypeStruct((1, width), F32),
            jax.ShapeDtypeStruct((1, width), F32), jax.ShapeDtypeStruct((HEADS, BUCKETS), F32),
            jax.ShapeDtypeStruct((router.shape[0] - 8, width), F32),
        ),
        compiler_params=pltpu.CompilerParams(vmem_limit_bytes=62 * MIB),
        cost_estimate=pl.CostEstimate(flops=8 * MICRO, bytes_accessed=20 * MIB, transcendentals=0),
        name="finish",
    )(out_a, out_b, slot, gate, resid, big, small, grad, router, tail)


def matmul(a, b):
    return jnp.dot(a, b, preferred_element_type=F32)


AXES = ("narrow", "wide")


def exchange(v):
    return lax.all_to_all(v, AXES, split_axis=0, concat_axis=0, tiled=True)


def local(
    hidden_in, norm_gain_one, w_qkv, w_out, pos_table, norm_gain_two, w_router, w_in, w_down,
    expert_ids, segment_ids, rel_buckets, out_grad,
):
    experts = lax.axis_size("narrow") * lax.axis_size("wide")
    tok, width = hidden_in.shape
    w_router = w_router.T
    cap = max(2, (5 * tok + 4 * experts - 1) // (4 * experts))
    capp = (cap + 7) // 8 * 8
    rows = experts * capp
    ids = expert_ids.reshape(1, tok)
    slot, pos, g_packed = make_slots(experts, cap, capp, ids, out_grad)
    g_rows = exchange(g_packed.reshape(experts, capp, width))
    (n1, q, k, v, p, attn, resid, n2, route, gate, packed, gpack) = front(
        hidden_in, norm_gain_one, w_qkv, w_out, pos_table.T, norm_gain_two, w_router, ids, slot, pos,
        segment_ids, rel_buckets, rows,
    )
    block = block_of(experts, capp)
    dx, out_a, rest, active, ginner, gs, expert_in, gg = expert(
        packed.reshape(experts, capp, width), gpack, g_rows, w_in[0], w_down[0]
    )
    dx = exchange(dx.reshape(experts, capp, width)).reshape(rows, width)
    grad_w_down, grad_w_in = weight_grads(active, gs, expert_in.reshape(rows, width), ginner)
    dx, grad_w_down, grad_w_in = lax.optimization_barrier((dx, grad_w_down, grad_w_in))
    grad, out_b, big, small, early, late = back(
        dx, gg, slot, pos, ids, route, gate, resid, n2, attn, out_grad, hidden_in, n1, q, k, v, p,
        norm_gain_one, norm_gain_two, w_router, w_out, w_qkv, rel_buckets.T, rest, block,
    )
    if experts > EARLY_MOST:
        early = lax.psum(early, AXES)
    blocks = experts // block
    index = lax.axis_index("narrow") * lax.axis_size("wide") + lax.axis_index("wide")
    turn = lax.rem(index // block + blocks - ids // block, blocks)
    place = jnp.where(pos >= 0, (turn * block + lax.rem(ids, block)) * capp + pos, -1)
    layer_out, qkv_grad, out_grad_w, in_grad, gain1g, gain2g, tableg, routerg = finish(
        out_a.reshape(-1, width), out_b.reshape(-1, width), place, gate, resid, big, small, grad,
        early, late,
    )
    return (
        layer_out, in_grad, gain1g.reshape(width), qkv_grad, out_grad_w, tableg.T,
        gain2g.reshape(width), routerg.T, grad_w_in, grad_w_down,
    )


def solution(mesh):
    split = P(AXES, None)
    cube = P(AXES, None, None)
    return jax.shard_map(
        local,
        mesh=mesh,
        in_specs=(
            split, P(), P(), P(), P(), P(), P(), cube, cube, split, split, P(), split,
        ),
        out_specs=(split, split, P(), P(), P(), P(), P(), P(), cube, cube),
        check_vma=False,
    )
```

```python
import functools
import jax
import jax.numpy as jnp
from jax import lax
from jax.experimental import pallas as pl
from jax.experimental.pallas import tpu as pltpu
from jax.sharding import PartitionSpec as P

HEADS = 12
HEAD_DIM = 64
LEN = 512
BUCKETS = 32
EPS = 1e-06
LANES = 128
HALF = 256
GROUP = 4
PAIR = 2
GROUPS = HEADS // GROUP
GW = GROUP * HEAD_DIM
F32 = jnp.float32
BF16 = jnp.bfloat16
MIB = 1024 * 1024
MICRO = 1150000000


def dot_nn(a, b):
    return lax.dot_general(a, b, (((1,), (0,)), ((), ())), preferred_element_type=F32)


def dot_tn(a, b):
    return lax.dot_general(a, b, (((0,), (0,)), ((), ())), preferred_element_type=F32)


def dot_nt(a, b):
    return lax.dot_general(a, b, (((1,), (1,)), ((), ())), preferred_element_type=F32)


def whole(shape):
    rank = len(shape)
    return pl.BlockSpec(shape, lambda *g: (0,) * rank, pipeline_mode=pl.Buffered(1))


def split3(v):
    high = v.astype(BF16)
    rest = v - high.astype(F32)
    mid = rest.astype(BF16)
    low = (rest - mid.astype(F32)).astype(BF16)
    return high, mid, low


def slots_kernel(experts, cap, capp, ids_ref, g_ref, slot_ref, pos_ref, packed_ref):
    tok = ids_ref.shape[1]
    ids = ids_ref[...]
    hot = lax.broadcasted_iota(jnp.int32, (experts, tok), 0) == ids
    before = (
        lax.broadcasted_iota(jnp.int32, (tok, tok), 0)
        < lax.broadcasted_iota(jnp.int32, (tok, tok), 1)
    )
    counts = dot_nn(hot.astype(F32).astype(BF16), before.astype(F32).astype(BF16))
    pos = jnp.sum(jnp.where(hot, counts, 0.0), axis=0, keepdims=True).astype(jnp.int32)
    kept = pos < cap
    slot = jnp.where(kept, ids * capp + pos, -1)
    slot_ref[...] = slot
    pos_ref[...] = jnp.where(kept, pos, -1)
    rows = packed_ref.shape[0]
    step = 256

    @pl.loop(0, rows // step)
    def _(r):
        base = pl.multiple_of(r * step, step)
        table = (lax.broadcasted_iota(jnp.int32, (step, tok), 0) + base == slot)
        packed_ref[pl.ds(base, step), :] = dot_nn(
            table.astype(F32).astype(BF16), g_ref[...]
        ).astype(BF16)


def make_slots(experts, cap, capp, ids_row, g):
    tok, width = g.shape
    return pl.pallas_call(
        functools.partial(slots_kernel, experts, cap, capp),
        out_shape=(
            jax.ShapeDtypeStruct((1, tok), jnp.int32),
            jax.ShapeDtypeStruct((1, tok), jnp.int32),
            jax.ShapeDtypeStruct((experts * capp, width), BF16),
        ),
        compiler_params=pltpu.CompilerParams(vmem_limit_bytes=40 * MIB),
        cost_estimate=pl.CostEstimate(flops=5 * MICRO, bytes_accessed=4 * MIB, transcendentals=0),
        name="slots",
    )(ids_row, g)


def column(row_ref):
    row = row_ref[...]
    return jnp.broadcast_to(row, (8, row.shape[1])).T[:, :1]


def front_kernel(
    hid_ref, gain1_ref, wq_ref, wk_ref, wv_ref, wout_ref, tab_ref, gain2_ref, wr_ref,
    ids_ref, slot_ref, pos_ref, segr_ref, rel_ref,
    n1_ref, q_ref, k_ref, v_ref, p_ref, attn_ref, resid_ref, n2_ref, route_ref, gate_ref,
    packed_ref, gpack_ref,
    relt, mask, bias, lines,
):
    step = pl.program_id(0)
    seqs = segr_ref.shape[0]
    tok = hid_ref.shape[0]

    @pl.when(step == 0)
    def _():
        for t in range(0, tok, HALF):
            x = hid_ref[t:t + HALF, :].astype(F32).T
            scale = lax.rsqrt(jnp.mean(x * x, axis=0, keepdims=True) + EPS)
            n1_ref[:, t:t + HALF] = (x * scale * column(gain1_ref)).astype(BF16)
        relt[...] = rel_ref[...].T
        lines[...] = jnp.zeros_like(lines)
        lines[:HEADS, :BUCKETS] = tab_ref[...]
        for s in range(seqs):
            line = segr_ref[s:s + 1, :]
            across = jnp.broadcast_to(line, (LEN, LEN))
            mask[s] = jnp.where(across.T == across, 0.0, -1000000000.0)

    for w_ref, o_ref in ((wq_ref, q_ref), (wk_ref, k_ref), (wv_ref, v_ref)):
        o_ref[...] = dot_tn(w_ref[...], n1_ref[...]).astype(BF16)

    @pl.loop(0, GROUP)
    def _(h):
        head = step * GROUP + h
        row = lines[pl.ds(head, 1), :]
        line = jnp.broadcast_to(row, (LEN, LANES))
        for c in range(0, LEN, LANES):
            bias[:, c:c + LANES] = jnp.take_along_axis(line, relt[:, c:c + LANES], axis=1)
        at = pl.ds(pl.multiple_of(h * HEAD_DIM, HEAD_DIM), HEAD_DIM)
        out_at = pl.ds(pl.multiple_of(head * HEAD_DIM, HEAD_DIM), HEAD_DIM)
        for s in range(seqs):
            key = k_ref[at, s * LEN:(s + 1) * LEN]
            value = v_ref[at, s * LEN:(s + 1) * LEN]
            for c in range(0, LEN, HALF):
                cols = slice(s * LEN + c, s * LEN + c + HALF)
                query = q_ref[at, cols] * jnp.asarray(HEAD_DIM ** -0.5, BF16)
                score = dot_tn(key, query) + bias[:, c:c + HALF] + mask[s, :, c:c + HALF]
                peak = jnp.max(score, axis=0, keepdims=True)
                weight = jnp.exp(score - peak)
                total = jnp.sum(weight, axis=0, keepdims=True)
                prob = (weight * (1.0 / total)).astype(BF16)
                p_ref[h, s, :, c:c + HALF] = prob
                attn_ref[out_at, cols] = dot_nn(value, prob).astype(BF16)

    @pl.when(step == pl.num_programs(0) - 1)
    def _():
        experts = route_ref.shape[0]
        for t in range(0, tok, HALF):
            cols = slice(t, t + HALF)
            x = hid_ref[t:t + HALF, :].astype(F32).T
            resid = x + dot_tn(wout_ref[...], attn_ref[:, cols])
            resid_ref[:, cols] = resid
            scale = lax.rsqrt(jnp.mean(resid * resid, axis=0, keepdims=True) + EPS)
            n2 = (resid * scale * column(gain2_ref)).astype(BF16)
            n2_ref[:, cols] = n2
            logits = dot_nn(wr_ref[...], n2)
            top = jnp.max(logits, axis=0, keepdims=True)
            e = jnp.exp(logits - top)
            route = e / jnp.sum(e, axis=0, keepdims=True)
            route_ref[:, cols] = route
            hot = lax.broadcasted_iota(jnp.int32, (experts, HALF), 0) == ids_ref[:, cols]
            gate_ref[:, cols] = jnp.sum(jnp.where(hot, route, 0.0), axis=0, keepdims=True)
        hot = lax.broadcasted_iota(jnp.int32, (experts, tok), 0) == ids_ref[...]
        gates = jnp.where(hot, gate_ref[...], 0.0)
        place = (
            lax.broadcasted_iota(jnp.int32, (LANES, tok), 0) == pos_ref[...]
        ).astype(F32).astype(BF16)
        parts = [dot_nt(part, place) for part in split3(gates)]
        which = lax.broadcasted_iota(jnp.int32, (experts, 8, LANES), 1)
        spread = [jnp.broadcast_to(part[:, None, :], which.shape) for part in parts]
        gpack_ref[...] = jnp.where(
            which == 0, spread[0],
            jnp.where(which == 1, spread[1], jnp.where(which == 2, spread[2], 0.0)),
        ).astype(BF16)
        rows = packed_ref.shape[0]

        @pl.loop(0, rows // HALF)
        def _(r):
            base = pl.multiple_of(r * HALF, HALF)
            table = (lax.broadcasted_iota(jnp.int32, (HALF, tok), 0) + base == slot_ref[...])
            packed_ref[pl.ds(base, HALF), :] = dot_nt(
                table.astype(F32).astype(BF16), n2_ref[...]
            ).astype(BF16)


def front(hidden, gain1, w_qkv, w_out, table, gain2, w_router, ids, slot, pos, seg, rel, rows):
    tok, width = hidden.shape
    experts = w_router.shape[0]
    seqs = seg.shape[0]
    wspec = lambda part: pl.BlockSpec((width, GW), lambda i: (0, part * GROUPS + i))
    qspec = pl.BlockSpec((GW, tok), lambda i: (i, 0))
    sd = jax.ShapeDtypeStruct
    outs = (
        sd((width, tok), BF16), sd((width, tok), BF16), sd((width, tok), BF16),
        sd((width, tok), BF16), sd((HEADS, seqs, LEN, LEN), BF16), sd((width, tok), BF16),
        sd((width, tok), F32), sd((width, tok), BF16), sd((experts, tok), F32), sd((1, tok), F32),
        sd((rows, width), BF16), sd((experts, 8, LANES), BF16),
    )
    return pl.pallas_call(
        front_kernel,
        grid=(GROUPS,),
        in_specs=[
            whole((tok, width)), whole((1, width)), wspec(0), wspec(1), wspec(2),
            whole((width, width)), whole((HEADS, BUCKETS)), whole((1, width)),
            whole((experts, width)), whole((1, tok)), whole((1, tok)), whole((1, tok)),
            whole((seqs, LEN)), whole((LEN, LEN)),
        ],
        out_specs=(
            whole((width, tok)), qspec, qspec, qspec,
            pl.BlockSpec((GROUP, seqs, LEN, LEN), lambda i: (i, 0, 0, 0)),
            whole((width, tok)), whole((width, tok)), whole((width, tok)),
            whole((experts, tok)), whole((1, tok)), whole((rows, width)),
            whole((experts, 8, LANES)),
        ),
        out_shape=outs,
        scratch_shapes=[
            pltpu.VMEM((LEN, LEN), jnp.int32),
            pltpu.VMEM((seqs, LEN, LEN), F32),
            pltpu.VMEM((LEN, LEN), F32),
            pltpu.VMEM((16, LANES), F32),
        ],
        compiler_params=pltpu.CompilerParams(vmem_limit_bytes=58 * MIB),
        cost_estimate=pl.CostEstimate(flops=50 * MICRO, bytes_accessed=30 * MIB, transcendentals=0),
        name="front",
    )(
        hidden, gain1.reshape(1, width), w_qkv, w_qkv, w_qkv, w_out, table,
        gain2.reshape(1, width), w_router, ids, slot, pos,
        seg, rel,
    )


def combine_kernel(rows_ref, slot_ref, gate_ref, resid_ref, out_ref):
    total = rows_ref.shape[0]
    cols = slot_ref.shape[1]
    table = lax.broadcasted_iota(jnp.int32, (total, cols), 0) == slot_ref[...]
    combined = dot_tn(rows_ref[...], table.astype(F32).astype(BF16))
    out_ref[...] = (resid_ref[...] + gate_ref[...] * combined).T.astype(BF16)


def combine(rows, slot, gate, resid):
    total, width = rows.shape
    tok = slot.shape[1]
    line = pl.BlockSpec((1, HALF), lambda i: (0, i))
    return pl.pallas_call(
        combine_kernel,
        grid=(tok // HALF,),
        in_specs=[
            whole((total, width)), line, line, pl.BlockSpec((width, HALF), lambda i: (0, i)),
        ],
        out_specs=pl.BlockSpec((HALF, width), lambda i: (i, 0)),
        out_shape=jax.ShapeDtypeStruct((tok, width), BF16),
        compiler_params=pltpu.CompilerParams(vmem_limit_bytes=40 * MIB),
        cost_estimate=pl.CostEstimate(flops=6 * MICRO, bytes_accessed=8 * MIB, transcendentals=0),
        name="combine",
    )(rows, slot, gate, resid)


CUBE = 0.044715
ROOT = 0.7978845608028654
FTILE = 768


def gelu_pair(x):
    square = x * x
    t = jnp.tanh(ROOT * (x + CUBE * (x * square)))
    half = 0.5 + 0.5 * t
    slope = half + (0.5 * x) * (1.0 - t * t) * (ROOT + (3.0 * CUBE * ROOT) * square)
    return x * half, slope


def device_of(index):
    wide = lax.axis_size("wide")
    return (index // wide, lax.rem(index, wide))


def expert_kernel(
    block,
    packed, gpack, grows, w_in, w_down,
    dx_out, out_got, rest_out, active_out, ginner_out, gs_out, x_out, gg_out,
    xbuf, gatebuf, gbuf, win, wdown, active, slope, ginner, gs, dx, outs, ggsend, ggbuf,
    x_send, x_recv, gate_send, gate_recv, gg_ssem, gg_rsem, o_send, o_recv, self_sem, load_sem, store_sem,
):
    count = lax.axis_size("narrow") * lax.axis_size("wide")
    me = lax.axis_index("narrow") * lax.axis_size("wide") + lax.axis_index("wide")
    blocks = count // block
    mine = me // block
    capp = packed.shape[1]
    rows = block * capp
    total = count * capp
    hidden = w_in.shape[1]
    mesh_id = pl.DeviceIdType.MESH

    def x_copy(target, source):
        return pltpu.make_async_remote_copy(
            src_ref=packed.at[target], dst_ref=xbuf.at[source], send_sem=x_send.at[target],
            recv_sem=x_recv.at[source], device_id=device_of(target), device_id_type=mesh_id,
        )

    def gate_copy(target, source):
        return pltpu.make_async_remote_copy(
            src_ref=gpack.at[target], dst_ref=gatebuf.at[source], send_sem=gate_send.at[target],
            recv_sem=gate_recv.at[source], device_id=device_of(target), device_id_type=mesh_id,
        )

    def gg_copy(target, source):
        return pltpu.make_async_remote_copy(
            src_ref=ggsend.at[target], dst_ref=ggbuf.at[source], send_sem=gg_ssem.at[target],
            recv_sem=gg_rsem.at[source], device_id=device_of(target), device_id_type=mesh_id,
        )

    ahead = blocks // 2
    inner = lax.rem(me, block)

    def out_copy(c, j):
        target = lax.rem(mine + c, blocks) * block + j
        return pltpu.make_async_remote_copy(
            src_ref=outs.at[c * block + j], dst_ref=out_got.at[c * block + inner],
            send_sem=o_send.at[c * block + j], recv_sem=o_recv.at[c * block + inner],
            device_id=device_of(target), device_id_type=mesh_id,
        )

    def out_wait(c, j):
        return pltpu.make_async_remote_copy(
            src_ref=outs.at[c * block + j], dst_ref=out_got.at[c * block + j],
            send_sem=o_send.at[c * block + j], recv_sem=o_recv.at[c * block + j],
            device_id=device_of(lax.rem(me + 1, count)), device_id_type=mesh_id,
        )

    barrier = pltpu.get_barrier_semaphore()

    @pl.loop(1, count)
    def _(s):
        pl.semaphore_signal(
            barrier, inc=1, device_id=device_of(lax.rem(me + s, count)), device_id_type=mesh_id
        )

    loads = [
        pltpu.make_async_copy(w_in, win, load_sem.at[0]),
        pltpu.make_async_copy(w_down, wdown, load_sem.at[1]),
        pltpu.make_async_copy(grows, gbuf, load_sem.at[2]),
    ]
    own = [
        pltpu.make_async_copy(packed.at[me], xbuf.at[me], self_sem.at[0]),
        pltpu.make_async_copy(gpack.at[me], gatebuf.at[me], self_sem.at[1]),
    ]
    for copy in own + loads:
        copy.start()
    pl.semaphore_wait(barrier, count - 1)

    @pl.loop(0, blocks)
    def _(c):
        there = lax.rem(mine + blocks - c, blocks)

        @pl.loop(0, block)
        def _(j):
            target = there * block + j

            @pl.when(target != me)
            def _():
                gate_copy(target, me).start()
                x_copy(target, me).start()

    for copy in own + loads:
        copy.wait()

    def stores(at):
        return [
            pltpu.make_async_copy(dx.at[at], dx_out.at[at], store_sem.at[0]),
            pltpu.make_async_copy(active.at[at], active_out.at[at], store_sem.at[1]),
            pltpu.make_async_copy(ginner.at[at], ginner_out.at[at], store_sem.at[2]),
            pltpu.make_async_copy(gs.at[at], gs_out.at[at], store_sem.at[3]),
        ]

    @pl.loop(0, blocks)
    def _(c):
        here = lax.rem(mine + c, blocks)
        first = here * block

        @pl.loop(0, block)
        def _(j):
            source = first + j

            @pl.when(source != me)
            def _():
                gate_copy(me, source).wait_recv()
                x_copy(me, source).wait_recv()

        at = pl.ds(pl.multiple_of(here * rows, rows), rows)
        group = pl.ds(first, block)
        x = xbuf[group].reshape(rows, xbuf.shape[2])

        @pl.loop(0, hidden // FTILE)
        def _(f):
            tile = pl.ds(pl.multiple_of(f * FTILE, FTILE), FTILE)
            value, grad = gelu_pair(dot_nn(x, win[:, tile]))
            active[at, tile] = value.astype(BF16)
            slope[:, tile] = grad

        result = dot_nn(active[at, :], wdown[...]).astype(BF16)
        outs[pl.ds(c * block, block)] = result.reshape(block, capp, result.shape[1])

        @pl.when(c < ahead)
        def _():
            @pl.loop(0, block)
            def _(j):
                @pl.when(first + j != me)
                def _():
                    out_copy(c, j).start()

        g = gbuf[group].astype(F32)
        diag = (
            lax.broadcasted_iota(jnp.int32, (block, capp, LANES), 1)
            == lax.broadcasted_iota(jnp.int32, (block, capp, LANES), 2)
        )
        gate = jnp.sum(gatebuf[group].astype(F32), axis=1)
        gate = jnp.sum(
            jnp.where(diag, gate[:, None, :], 0.0), axis=2, keepdims=True
        )
        gs[at, :] = (gate * g).astype(BF16).reshape(rows, g.shape[2])
        gg = jnp.sum(g * result.astype(F32).reshape(g.shape), axis=2, keepdims=True)
        gg = jnp.sum(jnp.where(diag, gg, 0.0), axis=1)
        which = lax.broadcasted_iota(jnp.int32, (block, 8, LANES), 1)
        high, mid, low = [part.astype(F32)[:, None, :] for part in split3(gg)]
        ggsend[group] = jnp.where(
            which == 0, high, jnp.where(which == 1, mid, jnp.where(which == 2, low, 0.0))
        ).astype(BF16)

        @pl.loop(0, block)
        def _(j):
            source = first + j

            @pl.when(source != me)
            def _():
                gg_copy(source, me).start()

        @pl.loop(0, hidden // FTILE)
        def _(f):
            tile = pl.ds(pl.multiple_of(f * FTILE, FTILE), FTILE)
            grad = dot_nt(gs[at, :], wdown[tile, :])
            ginner[at, tile] = (grad * slope[:, tile]).astype(BF16)

        dx[at, :] = dot_nt(ginner[at, :], win[...]).astype(BF16)

        for copy in stores(at):
            copy.start()

    for copy in stores(pl.ds(0, total)):
        copy.wait()
    keep = [
        pltpu.make_async_copy(xbuf, x_out, load_sem.at[0]),
        pltpu.make_async_copy(ggsend.at[me], ggbuf.at[me], self_sem.at[0]),
        pltpu.make_async_copy(outs.at[inner], out_got.at[inner], self_sem.at[1]),
        pltpu.make_async_copy(
            outs.at[pl.ds(ahead * block, count - ahead * block)], rest_out, load_sem.at[1]
        ),
    ]
    for copy in keep:
        copy.start()

    @pl.loop(0, count)
    def _(other):
        @pl.when(other != me)
        def _():
            x_copy(other, me).wait_send()
            gate_copy(other, me).wait_send()
            gg_copy(other, me).wait_send()
            gg_copy(me, other).wait_recv()

    @pl.loop(0, ahead * block)
    def _(i):
        @pl.when(i != inner)
        def _():
            out_wait(i // block, lax.rem(i, block)).wait_send()
            out_wait(i // block, lax.rem(i, block)).wait_recv()

    for copy in keep:
        copy.wait()
    last = pltpu.make_async_copy(ggbuf, gg_out, load_sem.at[1])
    last.start()
    last.wait()


def block_of(count, capp):
    block = 1
    while block * 4 <= count and block * 2 * capp <= 320:
        block *= 2
    return block


def expert(packed, gpack, grows, w_in, w_down):
    count, capp, width = packed.shape
    hidden = w_in.shape[1]
    block = block_of(count, capp)
    early = (count // block // 2) * block
    rows = block * capp
    total = count * capp
    sd = jax.ShapeDtypeStruct
    anyspec = pl.BlockSpec(memory_space=pl.ANY)
    dma = pltpu.SemaphoreType.DMA
    return pl.pallas_call(
        functools.partial(expert_kernel, block),
        in_specs=[anyspec] * 5,
        out_specs=(anyspec,) * 8,
        out_shape=(
            sd((total, width), BF16), sd((early, capp, width), BF16),
            sd((count - early, capp, width), BF16), sd((total, hidden), BF16), sd((total, hidden), BF16), sd((total, width), BF16), sd((count, capp, width), BF16),
            sd((count, 8, LANES), BF16),
        ),
        scratch_shapes=[
            pltpu.VMEM((count, capp, width), BF16), pltpu.VMEM((count, 8, LANES), BF16),
            pltpu.VMEM((count, capp, width), BF16), pltpu.VMEM((width, hidden), BF16),
            pltpu.VMEM((hidden, width), BF16), pltpu.VMEM((total, hidden), BF16),
            pltpu.VMEM((rows, hidden), F32), pltpu.VMEM((total, hidden), BF16),
            pltpu.VMEM((total, width), BF16), pltpu.VMEM((total, width), BF16),
            pltpu.VMEM((count, capp, width), BF16), pltpu.VMEM((count, 8, LANES), BF16),
            pltpu.VMEM((count, 8, LANES), BF16),
            dma((count,)), dma((count,)), dma((count,)), dma((count,)), dma((count,)), dma((count,)),
            dma((early,)), dma((early,)), dma((2,)), dma((3,)), dma((4,)),
        ],
        compiler_params=pltpu.CompilerParams(
            collective_id=0, has_side_effects=True, vmem_limit_bytes=62 * MIB
        ),
        cost_estimate=pl.CostEstimate(flops=60 * MICRO, bytes_accessed=60 * 1024 * 1024, transcendentals=0),
        name="expert",
    )(packed, gpack, grows, w_in, w_down)


def weights_kernel(active_ref, gs_ref, x_ref, ginner_ref, down_ref, in_ref, xt):
    @pl.when(pl.program_id(0) == 0)
    def _():
        total = x_ref.shape[0]
        for t in range(0, total, HALF):
            xt[:, t:t + HALF] = x_ref[t:t + HALF, :].T

    down_ref[0] = dot_tn(active_ref[...], gs_ref[...])
    in_ref[0] = dot_nn(xt[...], ginner_ref[...])


def weight_grads(active, gs, x, ginner):
    total, hidden = active.shape
    width = gs.shape[1]
    tile = HALF
    cols = pl.BlockSpec((total, tile), lambda i: (0, i))
    return pl.pallas_call(
        weights_kernel,
        grid=(hidden // tile,),
        in_specs=[cols, whole((total, width)), whole((total, width)), cols],
        out_specs=(
            pl.BlockSpec((1, tile, width), lambda i: (0, i, 0)),
            pl.BlockSpec((1, width, tile), lambda i: (0, 0, i)),
        ),
        out_shape=(
            jax.ShapeDtypeStruct((1, hidden, width), F32),
            jax.ShapeDtypeStruct((1, width, hidden), F32),
        ),
        scratch_shapes=[pltpu.VMEM((width, total), BF16)],
        compiler_params=pltpu.CompilerParams(vmem_limit_bytes=62 * MIB),
        cost_estimate=pl.CostEstimate(flops=18 * MICRO, bytes_accessed=36 * 1024 * 1024, transcendentals=0),
        name="weight_grads",
    )(active, gs, x, ginner)
PIECES = 32
BIG = 2
UNITS = BIG + GROUPS
TROWS = 16
LATE = 24
LAST_PHASE = 7


def norm_back(grad, source, gain):
    scale = lax.rsqrt(jnp.mean(source * source, axis=0, keepdims=True) + EPS)
    normed = source * scale
    scaled = grad * gain
    inner = jnp.mean(scaled * normed, axis=0, keepdims=True)
    part = grad * normed
    part = part[:, :LANES] + part[:, LANES:]
    return scale * (scaled - normed * inner), part


def back_kernel(
    block,
    dx_ref, gg_ref, slot_ref, pos_ref, ids_ref, route_ref, gate_ref, n2_ref, attn_ref,
    gain1_ref, gain2_ref, wr_ref, wout_ref, resid_any, g_any, hid_any, n1_any, q_any, k_any, v_any, p_any,
    wqkv_any, rel_any, rest_any,
    ingrad_any, out_got, big_out, small_out, early_out, late_out,
    gres, ga, gn1, dv, soft, hid_ref, n1_ref, q_ref, k_ref, v_ref, wqkv_ref, rel_ref, acc,
    *buffers_and_rest,
):
    buffers = buffers_and_rest[:16]
    inside = buffers[7].shape == big_out.shape
    big = buffers[:7] + (buffers[7] if inside else big_out,)
    small = buffers[8:15] + (buffers[15] if inside else small_out,)
    (
        early, early_got, late, late_got, send, recv, xsend, xrecv, esend, erecv, lsend, lrecv, osend, orecv, load_sem, store_sem, stage_sem, write_sem,
    ) = buffers_and_rest[16:]
    dq, dk = dv.at[pl.ds(0, GW)], dv.at[pl.ds(GW, GW)]
    step = pl.program_id(0)
    pair = pl.program_id(1)
    tok = g_any.shape[0]
    seqs = tok // LEN
    experts = route_ref.shape[0]
    total = dx_ref.shape[0]
    width = g_any.shape[1]
    narrow_n, wide_n = lax.axis_size("narrow"), lax.axis_size("wide")
    n, w = lax.axis_index("narrow"), lax.axis_index("wide")
    core, zed = lax.rem(w, 2), lax.rem(w // 2, 4)
    ex, why = lax.rem(n, 2), lax.rem(n // 2, 2)
    more_n = (narrow_n // 4) * (wide_n // 8)
    more_w = wide_n // 8
    more = (n // 4) * more_w + w // 8
    mesh_id = pl.DeviceIdType.MESH
    core_dev = (n, w + 1 - 2 * core)
    ex_dev = (n + 1 - 2 * ex, w)
    why_dev = (n + 2 - 4 * why, w)

    def zed_dev(step):
        return (n, w + 2 * (lax.rem(zed + step, 4) - zed))

    def more_dev(step):
        other = lax.rem(more + step, more_n)
        return (n + 4 * (other // more_w - more // more_w),
                w + 8 * (lax.rem(other, more_w) - lax.rem(more, more_w)))

    def unit(u):
        if isinstance(u, int):
            return (big, u, u) if u < BIG else (small, u - BIG, u)
        return small, u, u + BIG

    def ref(which, u):
        group, at, _ = unit(u)
        return group[which], at

    def view(which, u, *more):
        group, at, _ = unit(u)
        return group[which].at[(at,) + more]

    def land(u, q, at):
        return view(7, u, q, at)

    def spot(q):
        first, second = (ex, why) if q == 0 else (why, ex)
        b16 = core * 16
        b8 = b16 + first * 8
        b4 = b8 + second * 4
        return first, second, b16, b8, b4

    def remote(src, dst, k, u, q, dev):
        return pltpu.make_async_remote_copy(
            src_ref=src, dst_ref=dst, send_sem=send.at[k, unit(u)[2], q], recv_sem=recv.at[k, unit(u)[2], q],
            device_id=dev, device_id_type=mesh_id,
        )

    def outgoing(phase, u, q):
        first, second, b16, b8, b4 = spot(q)
        one, two = (ex_dev, why_dev) if q == 0 else (why_dev, ex_dev)
        if phase == 0:
            return [remote(view(0, u, q, pl.ds(16 - b16, 16)), view(2, u, q), 0, u, q, core_dev)]
        if phase == 1:
            src = view(0, u, q, pl.ds(b16 + (1 - first) * 8, 8))
            return [remote(src, view(3, u, q), 1, u, q, one)]
        if phase == 2:
            src = view(0, u, q, pl.ds(b8 + (1 - second) * 4, 4))
            return [remote(src, view(4, u, q), 2, u, q, two)]
        if phase == 3:
            return [
                remote(view(0, u, q, b4 + lax.rem(zed + step, 4)), view(5, u, q, step - 1),
                       2 + step, u, q, zed_dev(step))
                for step in (1, 2, 3)
            ]
        if phase == 4:
            mine = land(u, q, b4 + zed)
            return [remote(view(1, u, q), mine, 5 + step, u, q, zed_dev(step)) for step in (1, 2, 3)]
        if phase == 5:
            mine = land(u, q, pl.ds(b4, 4))
            return [remote(mine, mine, 9, u, q, two)]
        if phase == 6:
            mine = land(u, q, pl.ds(b8, 8))
            return [remote(mine, mine, 10, u, q, one)]
        mine = land(u, q, pl.ds(b16, 16))
        return [remote(mine, mine, 11, u, q, core_dev)]

    def incoming(phase, u, q):
        first, second, b16, b8, b4 = spot(q)
        if phase < 4:
            return outgoing(phase, u, q)
        if phase == 4:
            return [
                remote(view(1, u, q), land(u, q, b4 + lax.rem(zed + 4 - step, 4)),
                       5 + step, u, q, zed_dev(step))
                for step in (1, 2, 3)
            ]
        if phase == 5:
            there = land(u, q, pl.ds(b8 + (1 - second) * 4, 4))
            return [remote(there, there, 9, u, q, core_dev)]
        if phase == 6:
            there = land(u, q, pl.ds(b16 + (1 - first) * 8, 8))
            return [remote(there, there, 10, u, q, core_dev)]
        there = land(u, q, pl.ds(16 - b16, 16))
        return [remote(there, there, 11, u, q, core_dev)]

    def add(u, q, start, count, which):
        own, at = ref(0, u)
        got = ref(which, u)[0]

        @pl.loop(0, count)
        def _(i):
            own[at, q, start + i] = (
                own[at, q, start + i].astype(F32) + got[at, q, i].astype(F32)
            ).astype(BF16)

    def spread(u, q):
        (done, at), (extra, _) = ref(1, u), ref(6, u)
        extra[at, q, more] = done[at, q]
        copies = [
            pltpu.make_async_remote_copy(
                src_ref=view(6, u, q, more), dst_ref=view(6, u, q, more),
                send_sem=xsend.at[unit(u)[2], q, step], recv_sem=xrecv.at[unit(u)[2], q, step],
                device_id=more_dev(step), device_id_type=mesh_id,
            )
            for step in range(1, more_n)
        ]
        for copy in copies:
            copy.start()
        for step in range(1, more_n):
            other = lax.rem(more + more_n - step, more_n)
            pltpu.make_async_remote_copy(
                src_ref=view(6, u, q, more), dst_ref=view(6, u, q, other),
                send_sem=xsend.at[unit(u)[2], q, step], recv_sem=xrecv.at[unit(u)[2], q, step],
                device_id=more_dev(step), device_id_type=mesh_id,
            ).wait_recv()
        for copy in copies:
            copy.wait_send()
        total = extra[at, q, 0].astype(F32)
        for i in range(1, more_n):
            total = total + extra[at, q, i].astype(F32)
        done[at, q] = total.astype(BF16)

    def keep(u, q):
        at = spot(q)[4] + zed
        return pltpu.make_async_copy(view(1, u, q), land(u, q, at), store_sem.at[unit(u)[2], q])

    def settle(phase, u, q):
        first, second, b16, b8, b4 = spot(q)
        if phase == 0:
            add(u, q, b16, 16, 2)
        elif phase == 1:
            add(u, q, b8, 8, 3)
        elif phase == 2:
            add(u, q, b4, 4, 4)
        elif phase == 3:
            (own, at), (done, _), (got, _) = ref(0, u), ref(1, u), ref(5, u)
            done[at, q] = (
                own[at, q, b4 + zed].astype(F32) + got[at, q, 0].astype(F32)
                + (got[at, q, 1].astype(F32) + got[at, q, 2].astype(F32))
            ).astype(BF16)
            if more_n > 1:
                spread(u, q)
            keep(u, q).start()
        elif phase == 4:
            keep(u, q).wait()

    bits = []
    for axis, count in (("wide", wide_n), ("narrow", narrow_n)):
        size = 1
        while size < count:
            at = lax.rem((w if axis == "wide" else n) // size, 2)
            move = size - 2 * size * at
            bits.append((n, w + move) if axis == "wide" else (n + move, w))
            size *= 2
    levels = len(bits)
    early_levels = early_got.shape[0] if early.shape[0] > 1 else 0

    def swap(level, mine, got, ssem, rsem):
        return pltpu.make_async_remote_copy(
            src_ref=mine.at[level], dst_ref=got.at[level], send_sem=ssem.at[level],
            recv_sem=rsem.at[level], device_id=bits[level], device_id_type=mesh_id,
        )

    def climb(level, mine, got, ssem, rsem):
        copy = swap(level, mine, got, ssem, rsem)
        copy.wait_recv()
        copy.wait_send()
        mine[level + 1] = mine[level] + got[level]
        if level + 1 < levels:
            swap(level + 1, mine, got, ssem, rsem).start()

    def climb_early(level):
        climb(level, early, early_got, esend, erecv)

    def climb_late(level):
        climb(level, late, late_got, lsend, lrecv)

    count = narrow_n * wide_n
    blocks = count // block
    ahead = blocks // 2
    index = n * wide_n + w
    rest = rest_any.shape[0]

    def out_copy(i):
        target = lax.rem(index // block + ahead + i // block, blocks) * block + lax.rem(i, block)
        return pltpu.make_async_remote_copy(
            src_ref=rest_any.at[i],
            dst_ref=out_got.at[(i // block) * block + lax.rem(index, block)],
            send_sem=osend.at[i], recv_sem=orecv.at[(i // block) * block + lax.rem(index, block)],
            device_id=device_of(target), device_id_type=mesh_id,
        )

    def out_wait(i):
        return pltpu.make_async_remote_copy(
            src_ref=rest_any.at[i], dst_ref=out_got.at[i], send_sem=osend.at[i],
            recv_sem=orecv.at[i], device_id=core_dev, device_id_type=mesh_id,
        )

    def begin(u):
        for q in range(2):
            for copy in outgoing(0, u, q):
                copy.start()

    def advance(u, phase):
        for q in range(2):
            for copy in incoming(phase, u, q):
                copy.wait_recv()
            for copy in outgoing(phase, u, q):
                copy.wait_send()
            settle(phase, u, q)
            if phase < LAST_PHASE:
                for copy in outgoing(phase + 1, u, q):
                    copy.start()
        if inside and phase == LAST_PHASE:
            write_out(u).start()

    def write_out(u):
        group, at, flat = unit(u)
        out = big_out if u < BIG else small_out
        return pltpu.make_async_copy(group[7].at[at], out.at[at], write_sem.at[flat])

    def place(u, first, value):
        own, at = ref(0, u)
        half = own.shape[4]
        count = value.shape[1]
        blocks = value.reshape(PIECES, width // PIECES, count).astype(BF16)
        done = 0
        while done < count:
            q, within = (first + done) // half, (first + done) % half
            size = min(half - within, count - done)
            own[at, q, :, :, within:within + size] = blocks[:, :, done:done + size]
            done += size

    def soft_load(group):
        at = pl.ds(group * GROUP, GROUP)
        return pltpu.make_async_copy(p_any.at[at], soft.at[at], load_sem.at[group])

    pairs = ((n1_any, n1_ref), (wqkv_any, wqkv_ref), (v_any, v_ref), (k_any, k_ref), (q_any, q_ref),
             (rel_any, rel_ref))
    loads = [
        pltpu.make_async_copy(src, dst, load_sem.at[GROUPS + i]) for i, (src, dst) in enumerate(pairs)
    ]

    rows_load = [
        pltpu.make_async_copy(src, hid_ref, load_sem.at[GROUPS + 6 + i])
        for i, src in enumerate((g_any, hid_any))
    ]

    barrier = pltpu.get_barrier_semaphore()
    greet = [core_dev, ex_dev, why_dev] + [zed_dev(move) for move in (1, 2, 3)]
    greet += [more_dev(move) for move in range(1, more_n)] + bits

    @pl.when((step == 0) & (pair == 0))
    def _():
        first = pltpu.make_async_copy(resid_any, gres, stage_sem)
        first.start()
        rows_load[0].start()
        for group in range(GROUPS):
            soft_load(group).start()
        for copy in loads:
            copy.start()
        for dev in greet:
            pl.semaphore_signal(barrier, inc=1, device_id=dev, device_id_type=mesh_id)

        @pl.loop(0, rest)
        def _(i):
            source = lax.rem(
                index // block + 2 * blocks - ahead - i // block, blocks
            ) * block + lax.rem(i, block)
            pl.semaphore_signal(
                barrier, inc=1, device_id=device_of(source), device_id_type=mesh_id
            )

        pl.semaphore_wait(barrier, len(greet) + rest)

        @pl.loop(0, rest)
        def _(i):
            out_copy(i).start()

        hot = lax.broadcasted_iota(jnp.int32, (experts, tok), 0) == ids_ref[...]
        where = (
            lax.broadcasted_iota(jnp.int32, (LANES, tok), 0) == pos_ref[...]
        ).astype(F32).astype(BF16)
        grad_gate = jnp.zeros((1, tok), F32)
        for e in range(0, experts, 32):
            found = dot_nn(gg_ref[e:e + 32].reshape(256, LANES), where)
            found = jnp.sum(found.reshape(32, 8, tok), axis=1)
            grad_gate += jnp.sum(jnp.where(hot[e:e + 32], found, 0.0), axis=0, keepdims=True)
        first.wait()
        rows_load[0].wait()
        grad_logits = (
            (grad_gate * gate_ref[...]) * (hot.astype(F32) - route_ref[...])
        ).astype(BF16)
        early[0, :experts, :] = dot_nt(grad_logits, n2_ref[...])
        gain_grad = jnp.zeros((width, LANES), F32)
        for t in range(0, tok, HALF):
            cols = slice(t, t + HALF)
            gn2 = dot_tn(wr_ref[...], grad_logits[:, cols])
            size = total if total <= 1280 else 512
            for r in range(0, total, size):
                table = lax.broadcasted_iota(jnp.int32, (size, HALF), 0) + r == slot_ref[:, cols]
                gn2 = gn2 + dot_tn(dx_ref[r:r + size, :], table.astype(F32).astype(BF16))
            branch, part = norm_back(gn2, gres[:, cols], column(gain2_ref))
            gain_grad = gain_grad + part
            gr = hid_ref[t:t + HALF, :].astype(F32).T + branch
            gres[:, cols] = gr
            ga[:, cols] = gr.astype(BF16)
        early[0, experts:, :] = jnp.broadcast_to(
            jnp.sum(gain_grad.T, axis=0, keepdims=True), (8, width)
        )
        for c in range(0, width, HALF):
            place(0, c, dot_nt(attn_ref[...], ga[c:c + HALF, :]))
        rows_load[1].start()
        begin(0)
        if early_levels:
            swap(0, early, early_got, esend, erecv).start()
        for t in range(0, tok, HALF):
            cols = slice(t, t + HALF)
            ga[:, cols] = dot_nn(wout_ref[...], ga[:, cols]).astype(BF16)
        for group in range(GROUPS):
            soft_load(group).wait()

            @pl.loop(group * GROUP, (group + 1) * GROUP)
            def _(head):
                at = pl.ds(pl.multiple_of(head * HEAD_DIM, HEAD_DIM), HEAD_DIM)
                for s in range(seqs):
                    row = slice(s * LEN, (s + 1) * LEN)
                    dv[at, row] = dot_nt(ga[at, row], soft[head, s]).astype(BF16)

        loads[0].wait()
        for c in range(0, width, GW):
            place(1, c, dot_nt(n1_ref[...], dv[c:c + GW, :]))
        begin(1)
        loads[1].wait()
        for t in range(0, tok, HALF):
            gn1[:, t:t + HALF] = dot_nn(wqkv_ref[:, 2 * width:], dv[:, t:t + HALF])
        for copy in loads[2:5]:
            copy.wait()

    @pl.loop(0, PAIR)
    def _(h):
        turn = pair * PAIR + h
        head = step * GROUP + turn
        at = pl.ds(pl.multiple_of(turn * HEAD_DIM, HEAD_DIM), HEAD_DIM)
        all_at = pl.ds(pl.multiple_of(head * HEAD_DIM, HEAD_DIM), HEAD_DIM)
        for s in range(seqs):
            row = slice(s * LEN, (s + 1) * LEN)
            value = v_ref[all_at, row]
            for c in range(0, LEN, HALF):
                cols = slice(s * LEN + c, s * LEN + c + HALF)
                grad = ga[all_at, cols]
                inner = jnp.sum(
                    grad.astype(F32) * attn_ref[all_at, cols].astype(F32), axis=0, keepdims=True
                )
                gp = dot_tn(value, grad)
                soft[head, s, :, c:c + HALF] = (
                    soft[head, s, :, c:c + HALF].astype(F32) * (gp - inner)
                ).astype(BF16)
            ds = soft[head, s]
            factor = HEAD_DIM ** -0.5
            dq[at, row] = (dot_nn(k_ref[all_at, row], ds) * factor).astype(BF16)
            dk[at, row] = (dot_nt(q_ref[all_at, row], ds) * factor).astype(BF16)

        for number in range(HEADS):
            todo = [(u, phase) for u, phase, at_head in SCHEDULE if at_head == number]
            rise = [level for level, at_head in enumerate(EARLY_LEVELS)
                    if at_head == number and level < early_levels]
            if todo or rise:
                @pl.when(head == number)
                def _():
                    for u, phase in todo:
                        advance(u, phase)
                    for level in rise:
                        climb_early(level)

    @pl.when(pair == pl.num_programs(1) - 1)
    def _():
        for part, d in enumerate((dq, dk)):
            place(step, part * GW, dot_nt(n1_ref[...], d[...]))
        begin(step)
        for part, d in enumerate((dq, dk)):
            cols = pl.ds(pl.multiple_of(part * width + step * GW, GW), GW)
            gn1[...] += dot_nn(wqkv_ref[:, cols], d[...])

    @pl.when((step == pl.num_programs(0) - 1) & (pair == pl.num_programs(1) - 1))
    def _():
        planned = {(u, phase) for u, phase, at_head in SCHEDULE}
        left = {u: [phase for phase in range(LAST_PHASE + 1) if (u, phase) not in planned]
                for u in range(UNITS)}

        def push():
            for u in range(UNITS):
                if left[u]:
                    advance(u, left[u].pop(0))

        rows_load[1].wait()
        loads[5].wait()
        gain_grad = jnp.zeros((width, LANES), F32)
        for t in range(0, tok, HALF):
            cols = slice(t, t + HALF)
            x = hid_ref[t:t + HALF, :].astype(F32).T
            branch, part = norm_back(gn1[:, cols], x, column(gain1_ref))
            gain_grad = gain_grad + part
            gres[:, cols] = gres[:, cols] + branch
            if t == HALF:
                push()
        pltpu.make_async_copy(gres, ingrad_any, stage_sem).start()
        line = jnp.sum(gain_grad.T, axis=0, keepdims=True)
        late[0] = jnp.zeros((LATE, LANES), F32)
        for i in range(width // LANES):
            late[0, i:i + 1, :] = line[:, i * LANES:(i + 1) * LANES]
        push()
        lines = HEADS * seqs
        acc[...] = jnp.zeros_like(acc)
        chunks = 2
        for chunk in range(chunks):
            @pl.loop(chunk * (LEN // TROWS // chunks), (chunk + 1) * (LEN // TROWS // chunks))
            def _(r):
                base = pl.multiple_of(r * TROWS, TROWS)
                lhs = soft[:, :, pl.ds(base, TROWS), :].reshape(lines * TROWS, LEN)
                rel = rel_ref[pl.ds(base, TROWS), :]
                hot = (
                    rel[:, None, :]
                    == lax.broadcasted_iota(jnp.int32, (TROWS, BUCKETS, LEN), 1)
                ).astype(F32).astype(BF16).reshape(TROWS * BUCKETS, LEN)
                acc[...] += dot_nt(lhs, hot)

            push()
        rows = lax.broadcasted_iota(jnp.int32, acc.shape, 0) % TROWS
        cols = lax.broadcasted_iota(jnp.int32, acc.shape, 1) // BUCKETS
        kept = jnp.where(rows == cols, acc[...], 0.0)
        per_head = jnp.sum(kept.reshape(HEADS, seqs * TROWS, acc.shape[1]), axis=1)
        fold = (
            lax.broadcasted_iota(jnp.int32, (LANES, acc.shape[1]), 1) % BUCKETS
            == lax.broadcasted_iota(jnp.int32, (LANES, acc.shape[1]), 0)
        ).astype(F32)
        late[0, 8:8 + HEADS, :] = lax.dot_general(
            per_head, fold, (((1,), (1,)), ((), ())), precision=lax.Precision.HIGHEST,
            preferred_element_type=F32,
        )
        swap(0, late, late_got, lsend, lrecv).start()
        level = 0
        while any(left.values()) or level < levels:
            push()
            if level < levels:
                climb_late(level)
                level += 1
        for level in range(early_levels):
            if level >= len(EARLY_LEVELS):
                climb_early(level)
        pltpu.make_async_copy(gres, ingrad_any, stage_sem).wait()

        @pl.loop(0, rest)
        def _(i):
            out_wait(i).wait_send()
            out_wait(i).wait_recv()

        if inside:
            for u in range(UNITS):
                write_out(u).wait()
        early_out[...] = early[early_levels]
        late_out[...] = late[levels]


EARLY_MOST = 64
EARLY_LEVELS = (1, 3, 5, 7, 9)
SCHEDULE = (
    [(0, phase, at) for phase, at in enumerate((0, 2, 4, 6, 8, 10))]
    + [(1, phase, at) for phase, at in enumerate((1, 3, 5, 8, 11))]
    + [(2, phase, at) for phase, at in enumerate((5, 7, 10))]
    + [(3, phase, at) for phase, at in enumerate((9, 11))]
)


def back(dx, gg, slot, pos, ids, route, gate, resid, n2, attn, g, hidden, n1, q, k, v, p, gain1, gain2,
         w_router, w_out, w_qkv, relt, rest, block):
    tok, width = hidden.shape
    experts = w_router.shape[0]
    total = dx.shape[0]
    seqs = p.shape[1]
    narrow_n, wide_n = lax.axis_size("narrow"), lax.axis_size("wide")
    levels = (narrow_n * wide_n).bit_length() - 1
    more_n = (narrow_n // 4) * (wide_n // 8)
    early_levels = levels if experts <= EARLY_MOST else 0
    rows = width // PIECES
    anyspec = pl.BlockSpec(memory_space=pl.ANY)
    sd = jax.ShapeDtypeStruct
    dma = pltpu.SemaphoreType.DMA
    vm = pltpu.VMEM

    def bufs(number, half):
        return [
            vm((number, 2) + lead + (rows, half), BF16)
            for lead in ((PIECES,), (), (16,), (8,), (4,), (3,), (more_n,))
        ] + [vm((number, 2, PIECES, rows, half) if more_n == 1 else (8, LANES), BF16)]

    return pl.pallas_call(
        functools.partial(back_kernel, block),
        grid=(GROUPS, GROUP // PAIR),
        in_specs=[
            whole((total, width)), whole((experts, 8, LANES)), whole((1, tok)), whole((1, tok)),
            whole((1, tok)), whole((experts, tok)), whole((1, tok)), whole((width, tok)),
            whole((width, tok)), whole((1, width)), whole((1, width)),
            whole((experts, width)), whole((width, width)),
        ] + [anyspec] * 11,
        out_specs=(
            anyspec, anyspec, anyspec, anyspec, whole((experts + 8, width)), whole((LATE, LANES)),
        ),
        out_shape=(
            sd((width, tok), F32), sd(rest.shape, BF16), sd((BIG, 2, PIECES, rows, width // 2), BF16),
            sd((GROUPS, 2, PIECES, rows, GW), BF16),
            sd((experts + 8, width), F32), sd((LATE, LANES), F32),
        ),
        scratch_shapes=[
            vm((width, tok), F32), vm((width, tok), BF16), vm((width, tok), F32),
            vm((width, tok), BF16),
            vm((HEADS, seqs, LEN, LEN), BF16), vm((tok, width), BF16), vm((width, tok), BF16),
            vm((width, tok), BF16), vm((width, tok), BF16), vm((width, tok), BF16),
            vm(w_qkv.shape, BF16), vm((LEN, LEN), jnp.int32), vm((HEADS * seqs * TROWS, TROWS * BUCKETS), F32),
            *bufs(BIG, width // 2), *bufs(GROUPS, GW),
            vm((early_levels + 1, experts + 8, width), F32),
            vm((max(early_levels, 1), experts + 8, width) if early_levels else (1, 8, width), F32),
            vm((levels + 1, LATE, LANES), F32), vm((levels, LATE, LANES), F32),
            dma((12, UNITS, 2)), dma((12, UNITS, 2)), dma((UNITS, 2, more_n)),
            dma((UNITS, 2, more_n)), dma((levels,)), dma((levels,)), dma((levels,)), dma((levels,)),
            dma((rest.shape[0],)), dma((rest.shape[0],)),
            dma((GROUPS + 8,)), dma((UNITS, 2)), dma(()), dma((UNITS,)),
        ],
        compiler_params=pltpu.CompilerParams(
            collective_id=1, has_side_effects=True, vmem_limit_bytes=63 * MIB
        ),
        cost_estimate=pl.CostEstimate(flops=80 * MICRO, bytes_accessed=50 * MIB, transcendentals=0),
        name="back",
    )(
        dx, gg, slot, pos, ids, route, gate, n2, attn, gain1.reshape(1, width),
        gain2.reshape(1, width), w_router, w_out, resid, g, hidden, n1, q, k, v, p, w_qkv, relt, rest,
    )


def finish_kernel(
    early_ref, late_ref, slot_ref, gate_ref, resid_ref, big_ref, small_ref, grad_ref,
    router_ref, tail_ref,
    out_ref, qkv_ref, proj_ref, ingrad_ref, gain1_ref, gain2_ref, table_ref, routerg_ref,
):

    @pl.when(pl.program_id(0) == 0)
    def _():
        experts = routerg_ref.shape[0]
        for i in range(gain1_ref.shape[0] // LANES):
            gain1_ref[i * LANES:(i + 1) * LANES] = tail_ref[i, :]
        gain2_ref[...] = router_ref[experts, :]
        table_ref[...] = tail_ref[8:8 + HEADS, :BUCKETS]
        routerg_ref[...] = router_ref[:experts, :]

    ingrad_ref[...] = grad_ref[...].T
    rows_a = early_ref.shape[0]
    cols = slot_ref.shape[1]
    combined = None
    for base, ref in ((0, early_ref), (rows_a, late_ref)):
        table = (
            lax.broadcasted_iota(jnp.int32, (ref.shape[0], cols), 0) + base == slot_ref[...]
        )
        part = dot_tn(ref[...], table.astype(F32).astype(BF16))
        combined = part if combined is None else combined + part
    out_ref[...] = (resid_ref[...] + gate_ref[...] * combined).T.astype(BF16)
    rows = qkv_ref.shape[0]
    half = big_ref.shape[4]
    width = 2 * half
    for q in range(2):
        proj_ref[:, q * half:(q + 1) * half] = big_ref[0, q].astype(F32).reshape(rows, half)
        start = 2 * width + q * half
        qkv_ref[:, start:start + half] = big_ref[1, q].astype(F32).reshape(rows, half)
        for group in range(GROUPS):
            start = q * width + group * GW
            qkv_ref[:, start:start + GW] = small_ref[group, q].astype(F32).reshape(rows, GW)


def finish(out_a, out_b, slot, gate, resid, big, small, grad, router, tail):
    tok = slot.shape[1]
    width = resid.shape[0]
    steps = tok // HALF
    line = pl.BlockSpec((1, HALF), lambda i: (0, i))
    pieces = big.shape[2] // steps
    rows = width // steps
    return pl.pallas_call(
        finish_kernel,
        grid=(steps,),
        in_specs=[
            whole(out_a.shape), whole(out_b.shape), line, line,
            pl.BlockSpec((width, HALF), lambda i: (0, i)),
            pl.BlockSpec(big.shape[:2] + (pieces,) + big.shape[3:], lambda i: (0, 0, i, 0, 0)),
            pl.BlockSpec(small.shape[:2] + (pieces,) + small.shape[3:], lambda i: (0, 0, i, 0, 0)),
            pl.BlockSpec((width, HALF), lambda i: (0, i)), whole(router.shape), whole(tail.shape),
        ],
        out_specs=(
            pl.BlockSpec((HALF, width), lambda i: (i, 0)),
            pl.BlockSpec((rows, 3 * width), lambda i: (i, 0)),
            pl.BlockSpec((rows, width), lambda i: (i, 0)),
            pl.BlockSpec((HALF, width), lambda i: (i, 0)), whole((width,)), whole((width,)),
            whole((HEADS, BUCKETS)), whole((router.shape[0] - 8, width)),
        ),
        out_shape=(
            jax.ShapeDtypeStruct((tok, width), BF16),
            jax.ShapeDtypeStruct((width, 3 * width), F32),
            jax.ShapeDtypeStruct((width, width), F32),
            jax.ShapeDtypeStruct((tok, width), F32), jax.ShapeDtypeStruct((width,), F32),
            jax.ShapeDtypeStruct((width,), F32), jax.ShapeDtypeStruct((HEADS, BUCKETS), F32),
            jax.ShapeDtypeStruct((router.shape[0] - 8, width), F32),
        ),
        compiler_params=pltpu.CompilerParams(vmem_limit_bytes=62 * MIB),
        cost_estimate=pl.CostEstimate(flops=8 * MICRO, bytes_accessed=20 * MIB, transcendentals=0),
        name="finish",
    )(out_a, out_b, slot, gate, resid, big, small, grad, router, tail)


def matmul(a, b):
    return jnp.dot(a, b, preferred_element_type=F32)


AXES = ("narrow", "wide")


def exchange(v):
    return lax.all_to_all(v, AXES, split_axis=0, concat_axis=0, tiled=True)


def local(
    hidden_in, norm_gain_one, w_qkv, w_out, pos_table, norm_gain_two, w_router, w_in, w_down,
    expert_ids, segment_ids, rel_buckets, out_grad,
):
    experts = lax.axis_size("narrow") * lax.axis_size("wide")
    tok, width = hidden_in.shape
    w_router = w_router.T
    cap = max(2, (5 * tok + 4 * experts - 1) // (4 * experts))
    capp = (cap + 7) // 8 * 8
    rows = experts * capp
    ids = expert_ids.reshape(1, tok)
    slot, pos, g_packed = make_slots(experts, cap, capp, ids, out_grad)
    g_rows = exchange(g_packed.reshape(experts, capp, width))
    (n1, q, k, v, p, attn, resid, n2, route, gate, packed, gpack) = front(
        hidden_in, norm_gain_one, w_qkv, w_out, pos_table.T, norm_gain_two, w_router, ids, slot, pos,
        segment_ids, rel_buckets, rows,
    )
    block = block_of(experts, capp)
    dx, out_a, rest, active, ginner, gs, expert_in, gg = expert(
        packed.reshape(experts, capp, width), gpack, g_rows, w_in[0], w_down[0]
    )
    dx = exchange(dx.reshape(experts, capp, width)).reshape(rows, width)
    grad_w_down, grad_w_in = weight_grads(active, gs, expert_in.reshape(rows, width), ginner)
    dx, grad_w_down, grad_w_in = lax.optimization_barrier((dx, grad_w_down, grad_w_in))
    grad, out_b, big, small, early, late = back(
        dx, gg, slot, pos, ids, route, gate, resid, n2, attn, out_grad, hidden_in, n1, q, k, v, p,
        norm_gain_one, norm_gain_two, w_router, w_out, w_qkv, rel_buckets.T, rest, block,
    )
    if experts > EARLY_MOST:
        early = lax.psum(early, AXES)
    blocks = experts // block
    index = lax.axis_index("narrow") * lax.axis_size("wide") + lax.axis_index("wide")
    turn = lax.rem(index // block + blocks - ids // block, blocks)
    place = jnp.where(pos >= 0, (turn * block + lax.rem(ids, block)) * capp + pos, -1)
    layer_out, qkv_grad, out_grad_w, in_grad, gain1g, gain2g, tableg, routerg = finish(
        out_a.reshape(-1, width), out_b.reshape(-1, width), place, gate, resid, big, small, grad,
        early, late,
    )
    return (
        layer_out, in_grad, gain1g, qkv_grad, out_grad_w, tableg.T,
        gain2g, routerg.T, grad_w_in, grad_w_down,
    )


def solution(mesh):
    split = P(AXES, None)
    cube = P(AXES, None, None)
    return jax.shard_map(
        local,
        mesh=mesh,
        in_specs=(
            split, P(), P(), P(), P(), P(), P(), cube, cube, split, split, P(), split,
        ),
        out_specs=(split, split, P(), P(), P(), P(), P(), P(), cube, cube),
        check_vma=False,
    )
```

```python
import functools
import jax
import jax.numpy as jnp
from jax import lax
from jax.experimental import pallas as pl
from jax.experimental.pallas import tpu as pltpu
from jax.sharding import PartitionSpec as P

HEADS = 12
HEAD_DIM = 64
LEN = 512
BUCKETS = 32
EPS = 1e-06
LANES = 128
HALF = 256
GROUP = 4
PAIR = 2
GROUPS = HEADS // GROUP
GW = GROUP * HEAD_DIM
F32 = jnp.float32
BF16 = jnp.bfloat16
MIB = 1024 * 1024
MICRO = 1150000000


def dot_nn(a, b):
    return lax.dot_general(a, b, (((1,), (0,)), ((), ())), preferred_element_type=F32)


def dot_tn(a, b):
    return lax.dot_general(a, b, (((0,), (0,)), ((), ())), preferred_element_type=F32)


def dot_nt(a, b):
    return lax.dot_general(a, b, (((1,), (1,)), ((), ())), preferred_element_type=F32)


def whole(shape):
    rank = len(shape)
    return pl.BlockSpec(shape, lambda *g: (0,) * rank, pipeline_mode=pl.Buffered(1))


def split3(v):
    high = v.astype(BF16)
    rest = v - high.astype(F32)
    mid = rest.astype(BF16)
    low = (rest - mid.astype(F32)).astype(BF16)
    return high, mid, low


def slots_kernel(experts, cap, capp, ids_ref, g_ref, slot_ref, pos_ref, packed_ref):
    tok = ids_ref.shape[1]
    ids = ids_ref[...]
    hot = lax.broadcasted_iota(jnp.int32, (experts, tok), 0) == ids
    before = (
        lax.broadcasted_iota(jnp.int32, (tok, tok), 0)
        < lax.broadcasted_iota(jnp.int32, (tok, tok), 1)
    )
    counts = dot_nn(hot.astype(F32).astype(BF16), before.astype(F32).astype(BF16))
    pos = jnp.sum(jnp.where(hot, counts, 0.0), axis=0, keepdims=True).astype(jnp.int32)
    kept = pos < cap
    slot = jnp.where(kept, ids * capp + pos, -1)
    slot_ref[...] = slot
    pos_ref[...] = jnp.where(kept, pos, -1)
    rows = packed_ref.shape[0]
    step = 256

    @pl.loop(0, rows // step)
    def _(r):
        base = pl.multiple_of(r * step, step)
        table = (lax.broadcasted_iota(jnp.int32, (step, tok), 0) + base == slot)
        packed_ref[pl.ds(base, step), :] = dot_nn(
            table.astype(F32).astype(BF16), g_ref[...]
        ).astype(BF16)


def make_slots(experts, cap, capp, ids_row, g):
    tok, width = g.shape
    return pl.pallas_call(
        functools.partial(slots_kernel, experts, cap, capp),
        out_shape=(
            jax.ShapeDtypeStruct((1, tok), jnp.int32),
            jax.ShapeDtypeStruct((1, tok), jnp.int32),
            jax.ShapeDtypeStruct((experts * capp, width), BF16),
        ),
        compiler_params=pltpu.CompilerParams(vmem_limit_bytes=40 * MIB),
        cost_estimate=pl.CostEstimate(flops=5 * MICRO, bytes_accessed=4 * MIB, transcendentals=0),
        name="slots",
    )(ids_row, g)


def column(row_ref):
    row = row_ref[...]
    return jnp.broadcast_to(row, (8, row.shape[1])).T[:, :1]


def front_kernel(
    hid_ref, gain1_ref, wq_ref, wk_ref, wv_ref, wout_ref, tab_ref, gain2_ref, wr_ref,
    ids_ref, slot_ref, pos_ref, segr_ref, rel_ref,
    n1_ref, q_ref, k_ref, v_ref, p_ref, attn_ref, resid_ref, n2_ref, route_ref, gate_ref,
    packed_ref, gpack_ref,
    relt, mask, bias, lines,
):
    step = pl.program_id(0)
    seqs = segr_ref.shape[0]
    tok = hid_ref.shape[0]

    @pl.when(step == 0)
    def _():
        for t in range(0, tok, HALF):
            x = hid_ref[t:t + HALF, :].astype(F32).T
            scale = lax.rsqrt(jnp.mean(x * x, axis=0, keepdims=True) + EPS)
            n1_ref[:, t:t + HALF] = (x * scale * column(gain1_ref)).astype(BF16)
        relt[...] = rel_ref[...].T
        lines[...] = jnp.zeros_like(lines)
        lines[:HEADS, :BUCKETS] = tab_ref[...]
        for s in range(seqs):
            line = segr_ref[s:s + 1, :]
            across = jnp.broadcast_to(line, (LEN, LEN))
            mask[s] = jnp.where(across.T == across, 0.0, -1000000000.0)

    for w_ref, o_ref in ((wq_ref, q_ref), (wk_ref, k_ref), (wv_ref, v_ref)):
        o_ref[...] = dot_tn(w_ref[...], n1_ref[...]).astype(BF16)

    @pl.loop(0, GROUP)
    def _(h):
        head = step * GROUP + h
        row = lines[pl.ds(head, 1), :]
        line = jnp.broadcast_to(row, (LEN, LANES))
        for c in range(0, LEN, LANES):
            bias[:, c:c + LANES] = jnp.take_along_axis(line, relt[:, c:c + LANES], axis=1)
        at = pl.ds(pl.multiple_of(h * HEAD_DIM, HEAD_DIM), HEAD_DIM)
        out_at = pl.ds(pl.multiple_of(head * HEAD_DIM, HEAD_DIM), HEAD_DIM)
        for s in range(seqs):
            key = k_ref[at, s * LEN:(s + 1) * LEN]
            value = v_ref[at, s * LEN:(s + 1) * LEN]
            for c in range(0, LEN, HALF):
                cols = slice(s * LEN + c, s * LEN + c + HALF)
                query = q_ref[at, cols] * jnp.asarray(HEAD_DIM ** -0.5, BF16)
                score = dot_tn(key, query) + bias[:, c:c + HALF] + mask[s, :, c:c + HALF]
                peak = jnp.max(score, axis=0, keepdims=True)
                weight = jnp.exp(score - peak)
                total = jnp.sum(weight, axis=0, keepdims=True)
                prob = (weight * (1.0 / total)).astype(BF16)
                p_ref[h, s, :, c:c + HALF] = prob
                attn_ref[out_at, cols] = dot_nn(value, prob).astype(BF16)

    @pl.when(step == pl.num_programs(0) - 1)
    def _():
        experts = route_ref.shape[0]
        for t in range(0, tok, HALF):
            cols = slice(t, t + HALF)
            x = hid_ref[t:t + HALF, :].astype(F32).T
            resid = x + dot_tn(wout_ref[...], attn_ref[:, cols])
            resid_ref[:, cols] = resid
            scale = lax.rsqrt(jnp.mean(resid * resid, axis=0, keepdims=True) + EPS)
            n2 = (resid * scale * column(gain2_ref)).astype(BF16)
            n2_ref[:, cols] = n2
            logits = dot_nn(wr_ref[...], n2)
            top = jnp.max(logits, axis=0, keepdims=True)
            e = jnp.exp(logits - top)
            route = e / jnp.sum(e, axis=0, keepdims=True)
            route_ref[:, cols] = route
            hot = lax.broadcasted_iota(jnp.int32, (experts, HALF), 0) == ids_ref[:, cols]
            gate_ref[:, cols] = jnp.sum(jnp.where(hot, route, 0.0), axis=0, keepdims=True)
        hot = lax.broadcasted_iota(jnp.int32, (experts, tok), 0) == ids_ref[...]
        gates = jnp.where(hot, gate_ref[...], 0.0)
        place = (
            lax.broadcasted_iota(jnp.int32, (LANES, tok), 0) == pos_ref[...]
        ).astype(F32).astype(BF16)
        parts = [dot_nt(part, place) for part in split3(gates)]
        which = lax.broadcasted_iota(jnp.int32, (experts, 8, LANES), 1)
        spread = [jnp.broadcast_to(part[:, None, :], which.shape) for part in parts]
        gpack_ref[...] = jnp.where(
            which == 0, spread[0],
            jnp.where(which == 1, spread[1], jnp.where(which == 2, spread[2], 0.0)),
        ).astype(BF16)
        rows = packed_ref.shape[0]

        @pl.loop(0, rows // HALF)
        def _(r):
            base = pl.multiple_of(r * HALF, HALF)
            table = (lax.broadcasted_iota(jnp.int32, (HALF, tok), 0) + base == slot_ref[...])
            packed_ref[pl.ds(base, HALF), :] = dot_nt(
                table.astype(F32).astype(BF16), n2_ref[...]
            ).astype(BF16)


def front(hidden, gain1, w_qkv, w_out, table, gain2, w_router, ids, slot, pos, seg, rel, rows):
    tok, width = hidden.shape
    experts = w_router.shape[0]
    seqs = seg.shape[0]
    wspec = lambda part: pl.BlockSpec((width, GW), lambda i: (0, part * GROUPS + i))
    qspec = pl.BlockSpec((GW, tok), lambda i: (i, 0))
    sd = jax.ShapeDtypeStruct
    outs = (
        sd((width, tok), BF16), sd((width, tok), BF16), sd((width, tok), BF16),
        sd((width, tok), BF16), sd((HEADS, seqs, LEN, LEN), BF16), sd((width, tok), BF16),
        sd((width, tok), F32), sd((width, tok), BF16), sd((experts, tok), F32), sd((1, tok), F32),
        sd((rows, width), BF16), sd((experts, 8, LANES), BF16),
    )
    return pl.pallas_call(
        front_kernel,
        grid=(GROUPS,),
        in_specs=[
            whole((tok, width)), whole((1, width)), wspec(0), wspec(1), wspec(2),
            whole((width, width)), whole((HEADS, BUCKETS)), whole((1, width)),
            whole((experts, width)), whole((1, tok)), whole((1, tok)), whole((1, tok)),
            whole((seqs, LEN)), whole((LEN, LEN)),
        ],
        out_specs=(
            whole((width, tok)), qspec, qspec, qspec,
            pl.BlockSpec((GROUP, seqs, LEN, LEN), lambda i: (i, 0, 0, 0)),
            whole((width, tok)), whole((width, tok)), whole((width, tok)),
            whole((experts, tok)), whole((1, tok)), whole((rows, width)),
            whole((experts, 8, LANES)),
        ),
        out_shape=outs,
        scratch_shapes=[
            pltpu.VMEM((LEN, LEN), jnp.int32),
            pltpu.VMEM((seqs, LEN, LEN), F32),
            pltpu.VMEM((LEN, LEN), F32),
            pltpu.VMEM((16, LANES), F32),
        ],
        compiler_params=pltpu.CompilerParams(vmem_limit_bytes=58 * MIB),
        cost_estimate=pl.CostEstimate(flops=50 * MICRO, bytes_accessed=30 * MIB, transcendentals=0),
        name="front",
    )(
        hidden, gain1.reshape(1, width), w_qkv, w_qkv, w_qkv, w_out, table,
        gain2.reshape(1, width), w_router, ids, slot, pos,
        seg, rel,
    )


def combine_kernel(rows_ref, slot_ref, gate_ref, resid_ref, out_ref):
    total = rows_ref.shape[0]
    cols = slot_ref.shape[1]
    table = lax.broadcasted_iota(jnp.int32, (total, cols), 0) == slot_ref[...]
    combined = dot_tn(rows_ref[...], table.astype(F32).astype(BF16))
    out_ref[...] = (resid_ref[...] + gate_ref[...] * combined).T.astype(BF16)


def combine(rows, slot, gate, resid):
    total, width = rows.shape
    tok = slot.shape[1]
    line = pl.BlockSpec((1, HALF), lambda i: (0, i))
    return pl.pallas_call(
        combine_kernel,
        grid=(tok // HALF,),
        in_specs=[
            whole((total, width)), line, line, pl.BlockSpec((width, HALF), lambda i: (0, i)),
        ],
        out_specs=pl.BlockSpec((HALF, width), lambda i: (i, 0)),
        out_shape=jax.ShapeDtypeStruct((tok, width), BF16),
        compiler_params=pltpu.CompilerParams(vmem_limit_bytes=40 * MIB),
        cost_estimate=pl.CostEstimate(flops=6 * MICRO, bytes_accessed=8 * MIB, transcendentals=0),
        name="combine",
    )(rows, slot, gate, resid)


CUBE = 0.044715
ROOT = 0.7978845608028654
FTILE = 768


def gelu_pair(x):
    square = x * x
    t = jnp.tanh(ROOT * (x + CUBE * (x * square)))
    half = 0.5 + 0.5 * t
    slope = half + (0.5 * x) * (1.0 - t * t) * (ROOT + (3.0 * CUBE * ROOT) * square)
    return x * half, slope


def device_of(index):
    wide = lax.axis_size("wide")
    return (index // wide, lax.rem(index, wide))


def expert_kernel(
    block,
    packed, gpack, grows, w_in, w_down,
    dx_out, out_got, rest_out, active_out, ginner_out, gs_out, x_out, gg_out,
    xbuf, gatebuf, gbuf, win, wdown, active, slope, ginner, gs, dx, outs, ggsend, ggbuf,
    x_send, x_recv, gate_send, gate_recv, gg_ssem, gg_rsem, o_send, o_recv, self_sem, load_sem, store_sem,
):
    count = lax.axis_size("narrow") * lax.axis_size("wide")
    me = lax.axis_index("narrow") * lax.axis_size("wide") + lax.axis_index("wide")
    blocks = count // block
    mine = me // block
    capp = packed.shape[1]
    rows = block * capp
    total = count * capp
    hidden = w_in.shape[1]
    mesh_id = pl.DeviceIdType.MESH

    def x_copy(target, source):
        return pltpu.make_async_remote_copy(
            src_ref=packed.at[target], dst_ref=xbuf.at[source], send_sem=x_send.at[target],
            recv_sem=x_recv.at[source], device_id=device_of(target), device_id_type=mesh_id,
        )

    def gate_copy(target, source):
        return pltpu.make_async_remote_copy(
            src_ref=gpack.at[target], dst_ref=gatebuf.at[source], send_sem=gate_send.at[target],
            recv_sem=gate_recv.at[source], device_id=device_of(target), device_id_type=mesh_id,
        )

    def gg_copy(target, source):
        return pltpu.make_async_remote_copy(
            src_ref=ggsend.at[target], dst_ref=ggbuf.at[source], send_sem=gg_ssem.at[target],
            recv_sem=gg_rsem.at[source], device_id=device_of(target), device_id_type=mesh_id,
        )

    ahead = blocks // 2
    inner = lax.rem(me, block)

    def out_copy(c, j):
        target = lax.rem(mine + c, blocks) * block + j
        return pltpu.make_async_remote_copy(
            src_ref=outs.at[c * block + j], dst_ref=out_got.at[c * block + inner],
            send_sem=o_send.at[c * block + j], recv_sem=o_recv.at[c * block + inner],
            device_id=device_of(target), device_id_type=mesh_id,
        )

    def out_wait(c, j):
        return pltpu.make_async_remote_copy(
            src_ref=outs.at[c * block + j], dst_ref=out_got.at[c * block + j],
            send_sem=o_send.at[c * block + j], recv_sem=o_recv.at[c * block + j],
            device_id=device_of(lax.rem(me + 1, count)), device_id_type=mesh_id,
        )

    barrier = pltpu.get_barrier_semaphore()

    @pl.loop(1, count)
    def _(s):
        pl.semaphore_signal(
            barrier, inc=1, device_id=device_of(lax.rem(me + s, count)), device_id_type=mesh_id
        )

    loads = [
        pltpu.make_async_copy(w_in, win, load_sem.at[0]),
        pltpu.make_async_copy(w_down, wdown, load_sem.at[1]),
        pltpu.make_async_copy(grows, gbuf, load_sem.at[2]),
    ]
    own = [
        pltpu.make_async_copy(packed.at[me], xbuf.at[me], self_sem.at[0]),
        pltpu.make_async_copy(gpack.at[me], gatebuf.at[me], self_sem.at[1]),
    ]
    for copy in own + loads:
        copy.start()
    pl.semaphore_wait(barrier, count - 1)

    @pl.loop(0, blocks)
    def _(c):
        there = lax.rem(mine + blocks - c, blocks)

        @pl.loop(0, block)
        def _(j):
            target = there * block + j

            @pl.when(target != me)
            def _():
                gate_copy(target, me).start()
                x_copy(target, me).start()

    for copy in own + loads:
        copy.wait()

    def stores(at):
        return [
            pltpu.make_async_copy(dx.at[at], dx_out.at[at], store_sem.at[0]),
            pltpu.make_async_copy(active.at[at], active_out.at[at], store_sem.at[1]),
            pltpu.make_async_copy(ginner.at[at], ginner_out.at[at], store_sem.at[2]),
            pltpu.make_async_copy(gs.at[at], gs_out.at[at], store_sem.at[3]),
        ]

    @pl.loop(0, blocks)
    def _(c):
        here = lax.rem(mine + c, blocks)
        first = here * block

        @pl.loop(0, block)
        def _(j):
            source = first + j

            @pl.when(source != me)
            def _():
                gate_copy(me, source).wait_recv()
                x_copy(me, source).wait_recv()

        at = pl.ds(pl.multiple_of(here * rows, rows), rows)
        group = pl.ds(first, block)
        x = xbuf[group].reshape(rows, xbuf.shape[2])

        @pl.loop(0, hidden // FTILE)
        def _(f):
            tile = pl.ds(pl.multiple_of(f * FTILE, FTILE), FTILE)
            value, grad = gelu_pair(dot_nn(x, win[:, tile]))
            active[at, tile] = value.astype(BF16)
            slope[:, tile] = grad

        result = dot_nn(active[at, :], wdown[...]).astype(BF16)
        outs[pl.ds(c * block, block)] = result.reshape(block, capp, result.shape[1])

        @pl.when(c < ahead)
        def _():
            @pl.loop(0, block)
            def _(j):
                @pl.when(first + j != me)
                def _():
                    out_copy(c, j).start()

        g = gbuf[group].astype(F32)
        diag = (
            lax.broadcasted_iota(jnp.int32, (block, capp, LANES), 1)
            == lax.broadcasted_iota(jnp.int32, (block, capp, LANES), 2)
        )
        gate = jnp.sum(gatebuf[group].astype(F32), axis=1)
        gate = jnp.sum(
            jnp.where(diag, gate[:, None, :], 0.0), axis=2, keepdims=True
        )
        gs[at, :] = (gate * g).astype(BF16).reshape(rows, g.shape[2])
        gg = jnp.sum(g * result.astype(F32).reshape(g.shape), axis=2, keepdims=True)
        gg = jnp.sum(jnp.where(diag, gg, 0.0), axis=1)
        which = lax.broadcasted_iota(jnp.int32, (block, 8, LANES), 1)
        high, mid, low = [part.astype(F32)[:, None, :] for part in split3(gg)]
        ggsend[group] = jnp.where(
            which == 0, high, jnp.where(which == 1, mid, jnp.where(which == 2, low, 0.0))
        ).astype(BF16)

        @pl.loop(0, block)
        def _(j):
            source = first + j

            @pl.when(source != me)
            def _():
                gg_copy(source, me).start()

        @pl.loop(0, hidden // FTILE)
        def _(f):
            tile = pl.ds(pl.multiple_of(f * FTILE, FTILE), FTILE)
            grad = dot_nt(gs[at, :], wdown[tile, :])
            ginner[at, tile] = (grad * slope[:, tile]).astype(BF16)

        dx[at, :] = dot_nt(ginner[at, :], win[...]).astype(BF16)

        for copy in stores(at):
            copy.start()

    for copy in stores(pl.ds(0, total)):
        copy.wait()
    keep = [
        pltpu.make_async_copy(xbuf, x_out, load_sem.at[0]),
        pltpu.make_async_copy(ggsend.at[me], ggbuf.at[me], self_sem.at[0]),
        pltpu.make_async_copy(outs.at[inner], out_got.at[inner], self_sem.at[1]),
        pltpu.make_async_copy(
            outs.at[pl.ds(ahead * block, count - ahead * block)], rest_out, load_sem.at[1]
        ),
    ]
    for copy in keep:
        copy.start()

    @pl.loop(0, count)
    def _(other):
        @pl.when(other != me)
        def _():
            x_copy(other, me).wait_send()
            gate_copy(other, me).wait_send()
            gg_copy(other, me).wait_send()
            gg_copy(me, other).wait_recv()

    @pl.loop(0, ahead * block)
    def _(i):
        @pl.when(i != inner)
        def _():
            out_wait(i // block, lax.rem(i, block)).wait_send()
            out_wait(i // block, lax.rem(i, block)).wait_recv()

    for copy in keep:
        copy.wait()
    last = pltpu.make_async_copy(ggbuf, gg_out, load_sem.at[1])
    last.start()
    last.wait()


def block_of(count, capp):
    block = 1
    while block * 4 <= count and block * 2 * capp <= 320:
        block *= 2
    return block


def expert(packed, gpack, grows, w_in, w_down):
    count, capp, width = packed.shape
    hidden = w_in.shape[1]
    block = block_of(count, capp)
    early = (count // block // 2) * block
    rows = block * capp
    total = count * capp
    sd = jax.ShapeDtypeStruct
    anyspec = pl.BlockSpec(memory_space=pl.ANY)
    dma = pltpu.SemaphoreType.DMA
    return pl.pallas_call(
        functools.partial(expert_kernel, block),
        in_specs=[anyspec] * 5,
        out_specs=(anyspec,) * 8,
        out_shape=(
            sd((total, width), BF16), sd((early, capp, width), BF16),
            sd((count - early, capp, width), BF16), sd((total, hidden), BF16), sd((total, hidden), BF16), sd((total, width), BF16), sd((count, capp, width), BF16),
            sd((count, 8, LANES), BF16),
        ),
        scratch_shapes=[
            pltpu.VMEM((count, capp, width), BF16), pltpu.VMEM((count, 8, LANES), BF16),
            pltpu.VMEM((count, capp, width), BF16), pltpu.VMEM((width, hidden), BF16),
            pltpu.VMEM((hidden, width), BF16), pltpu.VMEM((total, hidden), BF16),
            pltpu.VMEM((rows, hidden), F32), pltpu.VMEM((total, hidden), BF16),
            pltpu.VMEM((total, width), BF16), pltpu.VMEM((total, width), BF16),
            pltpu.VMEM((count, capp, width), BF16), pltpu.VMEM((count, 8, LANES), BF16),
            pltpu.VMEM((count, 8, LANES), BF16),
            dma((count,)), dma((count,)), dma((count,)), dma((count,)), dma((count,)), dma((count,)),
            dma((early,)), dma((early,)), dma((2,)), dma((3,)), dma((4,)),
        ],
        compiler_params=pltpu.CompilerParams(
            collective_id=0, has_side_effects=True, vmem_limit_bytes=62 * MIB
        ),
        cost_estimate=pl.CostEstimate(flops=60 * MICRO, bytes_accessed=60 * 1024 * 1024, transcendentals=0),
        name="expert",
    )(packed, gpack, grows, w_in, w_down)


def weights_kernel(active_ref, gs_ref, x_ref, ginner_ref, down_ref, in_ref, xt):
    @pl.when(pl.program_id(0) == 0)
    def _():
        total = x_ref.shape[0]
        for t in range(0, total, HALF):
            xt[:, t:t + HALF] = x_ref[t:t + HALF, :].T

    down_ref[0] = dot_tn(active_ref[...], gs_ref[...])
    in_ref[0] = dot_nn(xt[...], ginner_ref[...])


def weight_grads(active, gs, x, ginner):
    total, hidden = active.shape
    width = gs.shape[1]
    tile = HALF
    cols = pl.BlockSpec((total, tile), lambda i: (0, i))
    return pl.pallas_call(
        weights_kernel,
        grid=(hidden // tile,),
        in_specs=[cols, whole((total, width)), whole((total, width)), cols],
        out_specs=(
            pl.BlockSpec((1, tile, width), lambda i: (0, i, 0)),
            pl.BlockSpec((1, width, tile), lambda i: (0, 0, i)),
        ),
        out_shape=(
            jax.ShapeDtypeStruct((1, hidden, width), F32),
            jax.ShapeDtypeStruct((1, width, hidden), F32),
        ),
        scratch_shapes=[pltpu.VMEM((width, total), BF16)],
        compiler_params=pltpu.CompilerParams(vmem_limit_bytes=62 * MIB),
        cost_estimate=pl.CostEstimate(flops=18 * MICRO, bytes_accessed=36 * 1024 * 1024, transcendentals=0),
        name="weight_grads",
    )(active, gs, x, ginner)
PIECES = 32
BIG = 2
UNITS = BIG + GROUPS
TROWS = 16
LATE = 24
LAST_PHASE = 7


def norm_back(grad, source, gain):
    scale = lax.rsqrt(jnp.mean(source * source, axis=0, keepdims=True) + EPS)
    normed = source * scale
    scaled = grad * gain
    inner = jnp.mean(scaled * normed, axis=0, keepdims=True)
    part = grad * normed
    part = part[:, :LANES] + part[:, LANES:]
    return scale * (scaled - normed * inner), part


def back_kernel(
    block,
    dx_ref, gg_ref, slot_ref, pos_ref, ids_ref, route_ref, gate_ref, n2_ref, attn_ref,
    gain1_ref, gain2_ref, wr_ref, wout_ref, resid_any, g_any, hid_any, n1_any, q_any, k_any, v_any, p_any,
    wqkv_any, rel_any, rest_any,
    ingrad_any, out_got, big_out, small_out, early_out, late_out,
    gres, ga, gn1, dv, soft, hid_ref, n1_ref, q_ref, k_ref, v_ref, wqkv_ref, rel_ref, acc,
    *buffers_and_rest,
):
    buffers = buffers_and_rest[:16]
    inside = buffers[7].shape == big_out.shape
    big = buffers[:7] + (buffers[7] if inside else big_out,)
    small = buffers[8:15] + (buffers[15] if inside else small_out,)
    (
        early, early_got, late, late_got, send, recv, xsend, xrecv, esend, erecv, lsend, lrecv, osend, orecv, load_sem, store_sem, stage_sem, write_sem,
    ) = buffers_and_rest[16:]
    dq, dk = dv.at[pl.ds(0, GW)], dv.at[pl.ds(GW, GW)]
    step = pl.program_id(0)
    pair = pl.program_id(1)
    tok = g_any.shape[0]
    seqs = tok // LEN
    experts = route_ref.shape[0]
    total = dx_ref.shape[0]
    width = g_any.shape[1]
    narrow_n, wide_n = lax.axis_size("narrow"), lax.axis_size("wide")
    n, w = lax.axis_index("narrow"), lax.axis_index("wide")
    core, zed = lax.rem(w, 2), lax.rem(w // 2, 4)
    ex, why = lax.rem(n, 2), lax.rem(n // 2, 2)
    more_n = (narrow_n // 4) * (wide_n // 8)
    more_w = wide_n // 8
    more = (n // 4) * more_w + w // 8
    mesh_id = pl.DeviceIdType.MESH
    core_dev = (n, w + 1 - 2 * core)
    ex_dev = (n + 1 - 2 * ex, w)
    why_dev = (n + 2 - 4 * why, w)

    def zed_dev(step):
        return (n, w + 2 * (lax.rem(zed + step, 4) - zed))

    def more_dev(step):
        other = lax.rem(more + step, more_n)
        return (n + 4 * (other // more_w - more // more_w),
                w + 8 * (lax.rem(other, more_w) - lax.rem(more, more_w)))

    def unit(u):
        if isinstance(u, int):
            return (big, u, u) if u < BIG else (small, u - BIG, u)
        return small, u, u + BIG

    def ref(which, u):
        group, at, _ = unit(u)
        return group[which], at

    def view(which, u, *more):
        group, at, _ = unit(u)
        return group[which].at[(at,) + more]

    def land(u, q, at):
        return view(7, u, q, at)

    def spot(q):
        first, second = (ex, why) if q == 0 else (why, ex)
        b16 = core * 16
        b8 = b16 + first * 8
        b4 = b8 + second * 4
        return first, second, b16, b8, b4

    def remote(src, dst, k, u, q, dev):
        return pltpu.make_async_remote_copy(
            src_ref=src, dst_ref=dst, send_sem=send.at[k, unit(u)[2], q], recv_sem=recv.at[k, unit(u)[2], q],
            device_id=dev, device_id_type=mesh_id,
        )

    def outgoing(phase, u, q):
        first, second, b16, b8, b4 = spot(q)
        one, two = (ex_dev, why_dev) if q == 0 else (why_dev, ex_dev)
        if phase == 0:
            return [remote(view(0, u, q, pl.ds(16 - b16, 16)), view(2, u, q), 0, u, q, core_dev)]
        if phase == 1:
            src = view(0, u, q, pl.ds(b16 + (1 - first) * 8, 8))
            return [remote(src, view(3, u, q), 1, u, q, one)]
        if phase == 2:
            src = view(0, u, q, pl.ds(b8 + (1 - second) * 4, 4))
            return [remote(src, view(4, u, q), 2, u, q, two)]
        if phase == 3:
            return [
                remote(view(0, u, q, b4 + lax.rem(zed + step, 4)), view(5, u, q, step - 1),
                       2 + step, u, q, zed_dev(step))
                for step in (1, 2, 3)
            ]
        if phase == 4:
            mine = land(u, q, b4 + zed)
            return [remote(view(1, u, q), mine, 5 + step, u, q, zed_dev(step)) for step in (1, 2, 3)]
        if phase == 5:
            mine = land(u, q, pl.ds(b4, 4))
            return [remote(mine, mine, 9, u, q, two)]
        if phase == 6:
            mine = land(u, q, pl.ds(b8, 8))
            return [remote(mine, mine, 10, u, q, one)]
        mine = land(u, q, pl.ds(b16, 16))
        return [remote(mine, mine, 11, u, q, core_dev)]

    def incoming(phase, u, q):
        first, second, b16, b8, b4 = spot(q)
        if phase < 4:
            return outgoing(phase, u, q)
        if phase == 4:
            return [
                remote(view(1, u, q), land(u, q, b4 + lax.rem(zed + 4 - step, 4)),
                       5 + step, u, q, zed_dev(step))
                for step in (1, 2, 3)
            ]
        if phase == 5:
            there = land(u, q, pl.ds(b8 + (1 - second) * 4, 4))
            return [remote(there, there, 9, u, q, core_dev)]
        if phase == 6:
            there = land(u, q, pl.ds(b16 + (1 - first) * 8, 8))
            return [remote(there, there, 10, u, q, core_dev)]
        there = land(u, q, pl.ds(16 - b16, 16))
        return [remote(there, there, 11, u, q, core_dev)]

    def add(u, q, start, count, which):
        own, at = ref(0, u)
        got = ref(which, u)[0]

        @pl.loop(0, count)
        def _(i):
            own[at, q, start + i] = (
                own[at, q, start + i].astype(F32) + got[at, q, i].astype(F32)
            ).astype(BF16)

    def spread(u, q):
        (done, at), (extra, _) = ref(1, u), ref(6, u)
        extra[at, q, more] = done[at, q]
        copies = [
            pltpu.make_async_remote_copy(
                src_ref=view(6, u, q, more), dst_ref=view(6, u, q, more),
                send_sem=xsend.at[unit(u)[2], q, step], recv_sem=xrecv.at[unit(u)[2], q, step],
                device_id=more_dev(step), device_id_type=mesh_id,
            )
            for step in range(1, more_n)
        ]
        for copy in copies:
            copy.start()
        for step in range(1, more_n):
            other = lax.rem(more + more_n - step, more_n)
            pltpu.make_async_remote_copy(
                src_ref=view(6, u, q, more), dst_ref=view(6, u, q, other),
                send_sem=xsend.at[unit(u)[2], q, step], recv_sem=xrecv.at[unit(u)[2], q, step],
                device_id=more_dev(step), device_id_type=mesh_id,
            ).wait_recv()
        for copy in copies:
            copy.wait_send()
        total = extra[at, q, 0].astype(F32)
        for i in range(1, more_n):
            total = total + extra[at, q, i].astype(F32)
        done[at, q] = total.astype(BF16)

    def keep(u, q):
        at = spot(q)[4] + zed
        return pltpu.make_async_copy(view(1, u, q), land(u, q, at), store_sem.at[unit(u)[2], q])

    def settle(phase, u, q):
        first, second, b16, b8, b4 = spot(q)
        if phase == 0:
            add(u, q, b16, 16, 2)
        elif phase == 1:
            add(u, q, b8, 8, 3)
        elif phase == 2:
            add(u, q, b4, 4, 4)
        elif phase == 3:
            (own, at), (done, _), (got, _) = ref(0, u), ref(1, u), ref(5, u)
            done[at, q] = (
                own[at, q, b4 + zed].astype(F32) + got[at, q, 0].astype(F32)
                + (got[at, q, 1].astype(F32) + got[at, q, 2].astype(F32))
            ).astype(BF16)
            if more_n > 1:
                spread(u, q)
            keep(u, q).start()
        elif phase == 4:
            keep(u, q).wait()

    bits = []
    for axis, count in (("wide", wide_n), ("narrow", narrow_n)):
        size = 1
        while size < count:
            at = lax.rem((w if axis == "wide" else n) // size, 2)
            move = size - 2 * size * at
            bits.append((n, w + move) if axis == "wide" else (n + move, w))
            size *= 2
    levels = len(bits)
    early_levels = early_got.shape[0] if early.shape[0] > 1 else 0

    def swap(level, mine, got, ssem, rsem):
        return pltpu.make_async_remote_copy(
            src_ref=mine.at[level], dst_ref=got.at[level], send_sem=ssem.at[level],
            recv_sem=rsem.at[level], device_id=bits[level], device_id_type=mesh_id,
        )

    def climb(level, mine, got, ssem, rsem):
        copy = swap(level, mine, got, ssem, rsem)
        copy.wait_recv()
        copy.wait_send()
        mine[level + 1] = mine[level] + got[level]
        if level + 1 < levels:
            swap(level + 1, mine, got, ssem, rsem).start()

    def climb_early(level):
        climb(level, early, early_got, esend, erecv)

    def climb_late(level):
        climb(level, late, late_got, lsend, lrecv)

    count = narrow_n * wide_n
    blocks = count // block
    ahead = blocks // 2
    index = n * wide_n + w
    rest = rest_any.shape[0]

    def out_copy(i):
        target = lax.rem(index // block + ahead + i // block, blocks) * block + lax.rem(i, block)
        return pltpu.make_async_remote_copy(
            src_ref=rest_any.at[i],
            dst_ref=out_got.at[(i // block) * block + lax.rem(index, block)],
            send_sem=osend.at[i], recv_sem=orecv.at[(i // block) * block + lax.rem(index, block)],
            device_id=device_of(target), device_id_type=mesh_id,
        )

    def out_wait(i):
        return pltpu.make_async_remote_copy(
            src_ref=rest_any.at[i], dst_ref=out_got.at[i], send_sem=osend.at[i],
            recv_sem=orecv.at[i], device_id=core_dev, device_id_type=mesh_id,
        )

    def begin(u):
        for q in range(2):
            for copy in outgoing(0, u, q):
                copy.start()

    def advance(u, phase):
        for q in range(2):
            for copy in incoming(phase, u, q):
                copy.wait_recv()
            for copy in outgoing(phase, u, q):
                copy.wait_send()
            settle(phase, u, q)
            if phase < LAST_PHASE:
                for copy in outgoing(phase + 1, u, q):
                    copy.start()
        if inside and phase == LAST_PHASE:
            write_out(u).start()

    def write_out(u):
        group, at, flat = unit(u)
        out = big_out if u < BIG else small_out
        return pltpu.make_async_copy(group[7].at[at], out.at[at], write_sem.at[flat])

    def place(u, first, value):
        own, at = ref(0, u)
        half = own.shape[4]
        count = value.shape[1]
        blocks = value.reshape(PIECES, width // PIECES, count).astype(BF16)
        done = 0
        while done < count:
            q, within = (first + done) // half, (first + done) % half
            size = min(half - within, count - done)
            own[at, q, :, :, within:within + size] = blocks[:, :, done:done + size]
            done += size

    def soft_load(group):
        at = pl.ds(group * GROUP, GROUP)
        return pltpu.make_async_copy(p_any.at[at], soft.at[at], load_sem.at[group])

    pairs = ((n1_any, n1_ref), (wqkv_any, wqkv_ref), (v_any, v_ref), (k_any, k_ref), (q_any, q_ref),
             (rel_any, rel_ref))
    loads = [
        pltpu.make_async_copy(src, dst, load_sem.at[GROUPS + i]) for i, (src, dst) in enumerate(pairs)
    ]

    rows_load = [
        pltpu.make_async_copy(src, hid_ref, load_sem.at[GROUPS + 6 + i])
        for i, src in enumerate((g_any, hid_any))
    ]

    barrier = pltpu.get_barrier_semaphore()
    greet = [core_dev, ex_dev, why_dev] + [zed_dev(move) for move in (1, 2, 3)]
    greet += [more_dev(move) for move in range(1, more_n)] + bits

    @pl.when((step == 0) & (pair == 0))
    def _():
        first = pltpu.make_async_copy(resid_any, gres, stage_sem)
        first.start()
        rows_load[0].start()
        for group in range(GROUPS):
            soft_load(group).start()
        for copy in loads:
            copy.start()
        for dev in greet:
            pl.semaphore_signal(barrier, inc=1, device_id=dev, device_id_type=mesh_id)

        @pl.loop(0, rest)
        def _(i):
            source = lax.rem(
                index // block + 2 * blocks - ahead - i // block, blocks
            ) * block + lax.rem(i, block)
            pl.semaphore_signal(
                barrier, inc=1, device_id=device_of(source), device_id_type=mesh_id
            )

        pl.semaphore_wait(barrier, len(greet) + rest)

        @pl.loop(0, rest)
        def _(i):
            out_copy(i).start()

        hot = lax.broadcasted_iota(jnp.int32, (experts, tok), 0) == ids_ref[...]
        where = (
            lax.broadcasted_iota(jnp.int32, (LANES, tok), 0) == pos_ref[...]
        ).astype(F32).astype(BF16)
        grad_gate = jnp.zeros((1, tok), F32)
        for e in range(0, experts, 32):
            found = dot_nn(gg_ref[e:e + 32].reshape(256, LANES), where)
            found = jnp.sum(found.reshape(32, 8, tok), axis=1)
            grad_gate += jnp.sum(jnp.where(hot[e:e + 32], found, 0.0), axis=0, keepdims=True)
        first.wait()
        rows_load[0].wait()
        grad_logits = (
            (grad_gate * gate_ref[...]) * (hot.astype(F32) - route_ref[...])
        ).astype(BF16)
        early[0, :experts, :] = dot_nt(grad_logits, n2_ref[...])
        gain_grad = jnp.zeros((width, LANES), F32)
        for t in range(0, tok, HALF):
            cols = slice(t, t + HALF)
            gn2 = dot_tn(wr_ref[...], grad_logits[:, cols])
            size = total if total <= 1280 else 512
            for r in range(0, total, size):
                table = lax.broadcasted_iota(jnp.int32, (size, HALF), 0) + r == slot_ref[:, cols]
                gn2 = gn2 + dot_tn(dx_ref[r:r + size, :], table.astype(F32).astype(BF16))
            branch, part = norm_back(gn2, gres[:, cols], column(gain2_ref))
            gain_grad = gain_grad + part
            gr = hid_ref[t:t + HALF, :].astype(F32).T + branch
            gres[:, cols] = gr
            ga[:, cols] = gr.astype(BF16)
        early[0, experts:, :] = jnp.broadcast_to(
            jnp.sum(gain_grad.T, axis=0, keepdims=True), (8, width)
        )
        for c in range(0, width, HALF):
            place(0, c, dot_nt(attn_ref[...], ga[c:c + HALF, :]))
        rows_load[1].start()
        begin(0)
        if early_levels:
            swap(0, early, early_got, esend, erecv).start()
        for t in range(0, tok, HALF):
            cols = slice(t, t + HALF)
            ga[:, cols] = dot_nn(wout_ref[...], ga[:, cols]).astype(BF16)
        for group in range(GROUPS):
            soft_load(group).wait()

            @pl.loop(group * GROUP, (group + 1) * GROUP)
            def _(head):
                at = pl.ds(pl.multiple_of(head * HEAD_DIM, HEAD_DIM), HEAD_DIM)
                for s in range(seqs):
                    row = slice(s * LEN, (s + 1) * LEN)
                    dv[at, row] = dot_nt(ga[at, row], soft[head, s]).astype(BF16)

        loads[0].wait()
        for c in range(0, width, GW):
            place(1, c, dot_nt(n1_ref[...], dv[c:c + GW, :]))
        begin(1)
        loads[1].wait()
        for t in range(0, tok, HALF):
            gn1[:, t:t + HALF] = dot_nn(wqkv_ref[:, 2 * width:], dv[:, t:t + HALF])
        for copy in loads[2:5]:
            copy.wait()

    @pl.loop(0, PAIR)
    def _(h):
        turn = pair * PAIR + h
        head = step * GROUP + turn
        at = pl.ds(pl.multiple_of(turn * HEAD_DIM, HEAD_DIM), HEAD_DIM)
        all_at = pl.ds(pl.multiple_of(head * HEAD_DIM, HEAD_DIM), HEAD_DIM)
        for s in range(seqs):
            row = slice(s * LEN, (s + 1) * LEN)
            value = v_ref[all_at, row]
            for c in range(0, LEN, HALF):
                cols = slice(s * LEN + c, s * LEN + c + HALF)
                grad = ga[all_at, cols]
                inner = jnp.sum(
                    grad.astype(F32) * attn_ref[all_at, cols].astype(F32), axis=0, keepdims=True
                )
                gp = dot_tn(value, grad)
                soft[head, s, :, c:c + HALF] = (
                    soft[head, s, :, c:c + HALF].astype(F32) * (gp - inner)
                ).astype(BF16)
            ds = soft[head, s]
            factor = HEAD_DIM ** -0.5
            dq[at, row] = (dot_nn(k_ref[all_at, row], ds) * factor).astype(BF16)
            dk[at, row] = (dot_nt(q_ref[all_at, row], ds) * factor).astype(BF16)

        for number in range(HEADS):
            todo = [(u, phase) for u, phase, at_head in SCHEDULE if at_head == number]
            rise = [level for level, at_head in enumerate(EARLY_LEVELS)
                    if at_head == number and level < early_levels]
            if todo or rise:
                @pl.when(head == number)
                def _():
                    for u, phase in todo:
                        advance(u, phase)
                    for level in rise:
                        climb_early(level)

    @pl.when(pair == pl.num_programs(1) - 1)
    def _():
        for part, d in enumerate((dq, dk)):
            place(step, part * GW, dot_nt(n1_ref[...], d[...]))
        begin(step)
        for part, d in enumerate((dq, dk)):
            cols = pl.ds(pl.multiple_of(part * width + step * GW, GW), GW)
            gn1[...] += dot_nn(wqkv_ref[:, cols], d[...])

    @pl.when((step == pl.num_programs(0) - 1) & (pair == pl.num_programs(1) - 1))
    def _():
        planned = {(u, phase) for u, phase, at_head in SCHEDULE}
        left = {u: [phase for phase in range(LAST_PHASE + 1) if (u, phase) not in planned]
                for u in range(UNITS)}

        def push():
            for u in range(UNITS):
                if left[u]:
                    advance(u, left[u].pop(0))

        rows_load[1].wait()
        loads[5].wait()
        gain_grad = jnp.zeros((width, LANES), F32)
        for t in range(0, tok, HALF):
            cols = slice(t, t + HALF)
            x = hid_ref[t:t + HALF, :].astype(F32).T
            branch, part = norm_back(gn1[:, cols], x, column(gain1_ref))
            gain_grad = gain_grad + part
            gres[:, cols] = gres[:, cols] + branch
            if t == HALF:
                push()
        pltpu.make_async_copy(gres, ingrad_any, stage_sem).start()
        line = jnp.sum(gain_grad.T, axis=0, keepdims=True)
        late[0] = jnp.zeros((LATE, LANES), F32)
        for i in range(width // LANES):
            late[0, i:i + 1, :] = line[:, i * LANES:(i + 1) * LANES]
        push()
        lines = HEADS * seqs
        acc[...] = jnp.zeros_like(acc)
        chunks = 2
        for chunk in range(chunks):
            @pl.loop(chunk * (LEN // TROWS // chunks), (chunk + 1) * (LEN // TROWS // chunks))
            def _(r):
                base = pl.multiple_of(r * TROWS, TROWS)
                lhs = soft[:, :, pl.ds(base, TROWS), :].reshape(lines * TROWS, LEN)
                rel = rel_ref[pl.ds(base, TROWS), :]
                hot = (
                    rel[:, None, :]
                    == lax.broadcasted_iota(jnp.int32, (TROWS, BUCKETS, LEN), 1)
                ).astype(F32).astype(BF16).reshape(TROWS * BUCKETS, LEN)
                acc[...] += dot_nt(lhs, hot)

            push()
        rows = lax.broadcasted_iota(jnp.int32, acc.shape, 0) % TROWS
        cols = lax.broadcasted_iota(jnp.int32, acc.shape, 1) // BUCKETS
        kept = jnp.where(rows == cols, acc[...], 0.0)
        per_head = jnp.sum(kept.reshape(HEADS, seqs * TROWS, acc.shape[1]), axis=1)
        fold = (
            lax.broadcasted_iota(jnp.int32, (LANES, acc.shape[1]), 1) % BUCKETS
            == lax.broadcasted_iota(jnp.int32, (LANES, acc.shape[1]), 0)
        ).astype(F32)
        late[0, 8:8 + HEADS, :] = lax.dot_general(
            per_head, fold, (((1,), (1,)), ((), ())), precision=lax.Precision.HIGHEST,
            preferred_element_type=F32,
        )
        swap(0, late, late_got, lsend, lrecv).start()
        level = 0
        while any(left.values()) or level < levels:
            push()
            if level < levels:
                climb_late(level)
                level += 1
        for level in range(early_levels):
            if level >= len(EARLY_LEVELS):
                climb_early(level)
        pltpu.make_async_copy(gres, ingrad_any, stage_sem).wait()

        @pl.loop(0, rest)
        def _(i):
            out_wait(i).wait_send()
            out_wait(i).wait_recv()

        if inside:
            for u in range(UNITS):
                write_out(u).wait()
        early_out[...] = early[early_levels]
        late_out[...] = late[levels]


EARLY_MOST = 64
EARLY_LEVELS = (1, 3, 5, 7, 9)
SCHEDULE = (
    [(0, phase, at) for phase, at in enumerate((1, 3, 5, 7, 9, 11))]
    + [(1, phase, at) for phase, at in enumerate((3, 6, 9))]
    + [(2, phase, at) for phase, at in enumerate((6, 8, 11))]
    + [(3, phase, at) for phase, at in enumerate((10,))]
)


def back(dx, gg, slot, pos, ids, route, gate, resid, n2, attn, g, hidden, n1, q, k, v, p, gain1, gain2,
         w_router, w_out, w_qkv, relt, rest, block):
    tok, width = hidden.shape
    experts = w_router.shape[0]
    total = dx.shape[0]
    seqs = p.shape[1]
    narrow_n, wide_n = lax.axis_size("narrow"), lax.axis_size("wide")
    levels = (narrow_n * wide_n).bit_length() - 1
    more_n = (narrow_n // 4) * (wide_n // 8)
    early_levels = levels if experts <= EARLY_MOST else 0
    rows = width // PIECES
    anyspec = pl.BlockSpec(memory_space=pl.ANY)
    sd = jax.ShapeDtypeStruct
    dma = pltpu.SemaphoreType.DMA
    vm = pltpu.VMEM

    def bufs(number, half):
        return [
            vm((number, 2) + lead + (rows, half), BF16)
            for lead in ((PIECES,), (), (16,), (8,), (4,), (3,), (more_n,))
        ] + [vm((number, 2, PIECES, rows, half) if more_n == 1 else (8, LANES), BF16)]

    return pl.pallas_call(
        functools.partial(back_kernel, block),
        grid=(GROUPS, GROUP // PAIR),
        in_specs=[
            whole((total, width)), whole((experts, 8, LANES)), whole((1, tok)), whole((1, tok)),
            whole((1, tok)), whole((experts, tok)), whole((1, tok)), whole((width, tok)),
            whole((width, tok)), whole((1, width)), whole((1, width)),
            whole((experts, width)), whole((width, width)),
        ] + [anyspec] * 11,
        out_specs=(
            anyspec, anyspec, anyspec, anyspec, whole((experts + 8, width)), whole((LATE, LANES)),
        ),
        out_shape=(
            sd((width, tok), F32), sd(rest.shape, BF16), sd((BIG, 2, PIECES, rows, width // 2), BF16),
            sd((GROUPS, 2, PIECES, rows, GW), BF16),
            sd((experts + 8, width), F32), sd((LATE, LANES), F32),
        ),
        scratch_shapes=[
            vm((width, tok), F32), vm((width, tok), BF16), vm((width, tok), F32),
            vm((width, tok), BF16),
            vm((HEADS, seqs, LEN, LEN), BF16), vm((tok, width), BF16), vm((width, tok), BF16),
            vm((width, tok), BF16), vm((width, tok), BF16), vm((width, tok), BF16),
            vm(w_qkv.shape, BF16), vm((LEN, LEN), jnp.int32), vm((HEADS * seqs * TROWS, TROWS * BUCKETS), F32),
            *bufs(BIG, width // 2), *bufs(GROUPS, GW),
            vm((early_levels + 1, experts + 8, width), F32),
            vm((max(early_levels, 1), experts + 8, width) if early_levels else (1, 8, width), F32),
            vm((levels + 1, LATE, LANES), F32), vm((levels, LATE, LANES), F32),
            dma((12, UNITS, 2)), dma((12, UNITS, 2)), dma((UNITS, 2, more_n)),
            dma((UNITS, 2, more_n)), dma((levels,)), dma((levels,)), dma((levels,)), dma((levels,)),
            dma((rest.shape[0],)), dma((rest.shape[0],)),
            dma((GROUPS + 8,)), dma((UNITS, 2)), dma(()), dma((UNITS,)),
        ],
        compiler_params=pltpu.CompilerParams(
            collective_id=1, has_side_effects=True, vmem_limit_bytes=63 * MIB
        ),
        cost_estimate=pl.CostEstimate(flops=80 * MICRO, bytes_accessed=50 * MIB, transcendentals=0),
        name="back",
    )(
        dx, gg, slot, pos, ids, route, gate, n2, attn, gain1.reshape(1, width),
        gain2.reshape(1, width), w_router, w_out, resid, g, hidden, n1, q, k, v, p, w_qkv, relt, rest,
    )


def finish_kernel(
    early_ref, late_ref, slot_ref, gate_ref, resid_ref, big_ref, small_ref, grad_ref,
    router_ref, tail_ref,
    out_ref, qkv_ref, proj_ref, ingrad_ref, gain1_ref, gain2_ref, table_ref, routerg_ref,
):

    @pl.when(pl.program_id(0) == 0)
    def _():
        experts = routerg_ref.shape[0]
        for i in range(gain1_ref.shape[0] // LANES):
            gain1_ref[i * LANES:(i + 1) * LANES] = tail_ref[i, :]
        gain2_ref[...] = router_ref[experts, :]
        table_ref[...] = tail_ref[8:8 + HEADS, :BUCKETS]
        routerg_ref[...] = router_ref[:experts, :]

    ingrad_ref[...] = grad_ref[...].T
    rows_a = early_ref.shape[0]
    cols = slot_ref.shape[1]
    combined = None
    for base, ref in ((0, early_ref), (rows_a, late_ref)):
        table = (
            lax.broadcasted_iota(jnp.int32, (ref.shape[0], cols), 0) + base == slot_ref[...]
        )
        part = dot_tn(ref[...], table.astype(F32).astype(BF16))
        combined = part if combined is None else combined + part
    out_ref[...] = (resid_ref[...] + gate_ref[...] * combined).T.astype(BF16)
    rows = qkv_ref.shape[0]
    half = big_ref.shape[4]
    width = 2 * half
    for q in range(2):
        proj_ref[:, q * half:(q + 1) * half] = big_ref[0, q].astype(F32).reshape(rows, half)
        start = 2 * width + q * half
        qkv_ref[:, start:start + half] = big_ref[1, q].astype(F32).reshape(rows, half)
        for group in range(GROUPS):
            start = q * width + group * GW
            qkv_ref[:, start:start + GW] = small_ref[group, q].astype(F32).reshape(rows, GW)


def finish(out_a, out_b, slot, gate, resid, big, small, grad, router, tail):
    tok = slot.shape[1]
    width = resid.shape[0]
    steps = tok // HALF
    line = pl.BlockSpec((1, HALF), lambda i: (0, i))
    pieces = big.shape[2] // steps
    rows = width // steps
    return pl.pallas_call(
        finish_kernel,
        grid=(steps,),
        in_specs=[
            whole(out_a.shape), whole(out_b.shape), line, line,
            pl.BlockSpec((width, HALF), lambda i: (0, i)),
            pl.BlockSpec(big.shape[:2] + (pieces,) + big.shape[3:], lambda i: (0, 0, i, 0, 0)),
            pl.BlockSpec(small.shape[:2] + (pieces,) + small.shape[3:], lambda i: (0, 0, i, 0, 0)),
            pl.BlockSpec((width, HALF), lambda i: (0, i)), whole(router.shape), whole(tail.shape),
        ],
        out_specs=(
            pl.BlockSpec((HALF, width), lambda i: (i, 0)),
            pl.BlockSpec((rows, 3 * width), lambda i: (i, 0)),
            pl.BlockSpec((rows, width), lambda i: (i, 0)),
            pl.BlockSpec((HALF, width), lambda i: (i, 0)), whole((width,)), whole((width,)),
            whole((HEADS, BUCKETS)), whole((router.shape[0] - 8, width)),
        ),
        out_shape=(
            jax.ShapeDtypeStruct((tok, width), BF16),
            jax.ShapeDtypeStruct((width, 3 * width), F32),
            jax.ShapeDtypeStruct((width, width), F32),
            jax.ShapeDtypeStruct((tok, width), F32), jax.ShapeDtypeStruct((width,), F32),
            jax.ShapeDtypeStruct((width,), F32), jax.ShapeDtypeStruct((HEADS, BUCKETS), F32),
            jax.ShapeDtypeStruct((router.shape[0] - 8, width), F32),
        ),
        compiler_params=pltpu.CompilerParams(vmem_limit_bytes=62 * MIB),
        cost_estimate=pl.CostEstimate(flops=8 * MICRO, bytes_accessed=20 * MIB, transcendentals=0),
        name="finish",
    )(out_a, out_b, slot, gate, resid, big, small, grad, router, tail)


def matmul(a, b):
    return jnp.dot(a, b, preferred_element_type=F32)


AXES = ("narrow", "wide")


def exchange(v):
    return lax.all_to_all(v, AXES, split_axis=0, concat_axis=0, tiled=True)


def local(
    hidden_in, norm_gain_one, w_qkv, w_out, pos_table, norm_gain_two, w_router, w_in, w_down,
    expert_ids, segment_ids, rel_buckets, out_grad,
):
    experts = lax.axis_size("narrow") * lax.axis_size("wide")
    tok, width = hidden_in.shape
    w_router = w_router.T
    cap = max(2, (5 * tok + 4 * experts - 1) // (4 * experts))
    capp = (cap + 7) // 8 * 8
    rows = experts * capp
    ids = expert_ids.reshape(1, tok)
    slot, pos, g_packed = make_slots(experts, cap, capp, ids, out_grad)
    g_rows = exchange(g_packed.reshape(experts, capp, width))
    (n1, q, k, v, p, attn, resid, n2, route, gate, packed, gpack) = front(
        hidden_in, norm_gain_one, w_qkv, w_out, pos_table.T, norm_gain_two, w_router, ids, slot, pos,
        segment_ids, rel_buckets, rows,
    )
    block = block_of(experts, capp)
    dx, out_a, rest, active, ginner, gs, expert_in, gg = expert(
        packed.reshape(experts, capp, width), gpack, g_rows, w_in[0], w_down[0]
    )
    dx = exchange(dx.reshape(experts, capp, width)).reshape(rows, width)
    grad_w_down, grad_w_in = weight_grads(active, gs, expert_in.reshape(rows, width), ginner)
    dx, grad_w_down, grad_w_in = lax.optimization_barrier((dx, grad_w_down, grad_w_in))
    grad, out_b, big, small, early, late = back(
        dx, gg, slot, pos, ids, route, gate, resid, n2, attn, out_grad, hidden_in, n1, q, k, v, p,
        norm_gain_one, norm_gain_two, w_router, w_out, w_qkv, rel_buckets.T, rest, block,
    )
    if experts > EARLY_MOST:
        early = lax.psum(early, AXES)
    blocks = experts // block
    index = lax.axis_index("narrow") * lax.axis_size("wide") + lax.axis_index("wide")
    turn = lax.rem(index // block + blocks - ids // block, blocks)
    place = jnp.where(pos >= 0, (turn * block + lax.rem(ids, block)) * capp + pos, -1)
    layer_out, qkv_grad, out_grad_w, in_grad, gain1g, gain2g, tableg, routerg = finish(
        out_a.reshape(-1, width), out_b.reshape(-1, width), place, gate, resid, big, small, grad,
        early, late,
    )
    return (
        layer_out, in_grad, gain1g, qkv_grad, out_grad_w, tableg.T,
        gain2g, routerg.T, grad_w_in, grad_w_down,
    )


def solution(mesh):
    split = P(AXES, None)
    cube = P(AXES, None, None)
    return jax.shard_map(
        local,
        mesh=mesh,
        in_specs=(
            split, P(), P(), P(), P(), P(), P(), cube, cube, split, split, P(), split,
        ),
        out_specs=(split, split, P(), P(), P(), P(), P(), P(), cube, cube),
        check_vma=False,
    )
```

```python
import functools
import jax
import jax.numpy as jnp
from jax import lax
from jax.experimental import pallas as pl
from jax.experimental.pallas import tpu as pltpu
from jax.sharding import PartitionSpec as P

HEADS = 12
HEAD_DIM = 64
LEN = 512
BUCKETS = 32
EPS = 1e-06
LANES = 128
HALF = 256
GROUP = 4
PAIR = 2
GROUPS = HEADS // GROUP
GW = GROUP * HEAD_DIM
F32 = jnp.float32
BF16 = jnp.bfloat16
MIB = 1024 * 1024
MICRO = 1150000000


def dot_nn(a, b):
    return lax.dot_general(a, b, (((1,), (0,)), ((), ())), preferred_element_type=F32)


def dot_tn(a, b):
    return lax.dot_general(a, b, (((0,), (0,)), ((), ())), preferred_element_type=F32)


def dot_nt(a, b):
    return lax.dot_general(a, b, (((1,), (1,)), ((), ())), preferred_element_type=F32)


def whole(shape):
    rank = len(shape)
    return pl.BlockSpec(shape, lambda *g: (0,) * rank, pipeline_mode=pl.Buffered(1))


def split3(v):
    high = v.astype(BF16)
    rest = v - high.astype(F32)
    mid = rest.astype(BF16)
    low = (rest - mid.astype(F32)).astype(BF16)
    return high, mid, low


def slots_kernel(experts, cap, capp, ids_ref, g_ref, slot_ref, pos_ref, packed_ref):
    tok = ids_ref.shape[1]
    ids = ids_ref[...]
    hot = lax.broadcasted_iota(jnp.int32, (experts, tok), 0) == ids
    before = (
        lax.broadcasted_iota(jnp.int32, (tok, tok), 0)
        < lax.broadcasted_iota(jnp.int32, (tok, tok), 1)
    )
    counts = dot_nn(hot.astype(F32).astype(BF16), before.astype(F32).astype(BF16))
    pos = jnp.sum(jnp.where(hot, counts, 0.0), axis=0, keepdims=True).astype(jnp.int32)
    kept = pos < cap
    slot = jnp.where(kept, ids * capp + pos, -1)
    slot_ref[...] = slot
    pos_ref[...] = jnp.where(kept, pos, -1)
    rows = packed_ref.shape[0]
    step = 256

    @pl.loop(0, rows // step)
    def _(r):
        base = pl.multiple_of(r * step, step)
        table = (lax.broadcasted_iota(jnp.int32, (step, tok), 0) + base == slot)
        packed_ref[pl.ds(base, step), :] = dot_nn(
            table.astype(F32).astype(BF16), g_ref[...]
        ).astype(BF16)


def make_slots(experts, cap, capp, ids_row, g):
    tok, width = g.shape
    return pl.pallas_call(
        functools.partial(slots_kernel, experts, cap, capp),
        out_shape=(
            jax.ShapeDtypeStruct((1, tok), jnp.int32),
            jax.ShapeDtypeStruct((1, tok), jnp.int32),
            jax.ShapeDtypeStruct((experts * capp, width), BF16),
        ),
        compiler_params=pltpu.CompilerParams(vmem_limit_bytes=40 * MIB),
        cost_estimate=pl.CostEstimate(flops=5 * MICRO, bytes_accessed=4 * MIB, transcendentals=0),
        name="slots",
    )(ids_row, g)


def column(row_ref):
    row = row_ref[...]
    return jnp.broadcast_to(row, (8, row.shape[1])).T[:, :1]


def front_kernel(
    hid_ref, gain1_ref, wq_ref, wk_ref, wv_ref, wout_ref, tab_ref, gain2_ref, wr_ref,
    ids_ref, slot_ref, pos_ref, segr_ref, rel_ref,
    n1_ref, q_ref, k_ref, v_ref, p_ref, attn_ref, resid_ref, n2_ref, route_ref, gate_ref,
    packed_ref, gpack_ref,
    relt, mask, bias, lines,
):
    step = pl.program_id(0)
    seqs = segr_ref.shape[0]
    tok = hid_ref.shape[0]

    @pl.when(step == 0)
    def _():
        for t in range(0, tok, HALF):
            x = hid_ref[t:t + HALF, :].astype(F32).T
            scale = lax.rsqrt(jnp.mean(x * x, axis=0, keepdims=True) + EPS)
            n1_ref[:, t:t + HALF] = (x * scale * column(gain1_ref)).astype(BF16)
        relt[...] = rel_ref[...].T
        lines[...] = jnp.zeros_like(lines)
        lines[:HEADS, :BUCKETS] = tab_ref[...]
        for s in range(seqs):
            line = segr_ref[s:s + 1, :]
            across = jnp.broadcast_to(line, (LEN, LEN))
            mask[s] = jnp.where(across.T == across, 0.0, -1000000000.0)

    for w_ref, o_ref in ((wq_ref, q_ref), (wk_ref, k_ref), (wv_ref, v_ref)):
        o_ref[...] = dot_tn(w_ref[...], n1_ref[...]).astype(BF16)

    @pl.loop(0, GROUP)
    def _(h):
        head = step * GROUP + h
        row = lines[pl.ds(head, 1), :]
        line = jnp.broadcast_to(row, (LEN, LANES))
        for c in range(0, LEN, LANES):
            bias[:, c:c + LANES] = jnp.take_along_axis(line, relt[:, c:c + LANES], axis=1)
        at = pl.ds(pl.multiple_of(h * HEAD_DIM, HEAD_DIM), HEAD_DIM)
        out_at = pl.ds(pl.multiple_of(head * HEAD_DIM, HEAD_DIM), HEAD_DIM)
        for s in range(seqs):
            key = k_ref[at, s * LEN:(s + 1) * LEN]
            value = v_ref[at, s * LEN:(s + 1) * LEN]
            for c in range(0, LEN, HALF):
                cols = slice(s * LEN + c, s * LEN + c + HALF)
                query = q_ref[at, cols] * jnp.asarray(HEAD_DIM ** -0.5, BF16)
                score = dot_tn(key, query) + bias[:, c:c + HALF] + mask[s, :, c:c + HALF]
                peak = jnp.max(score, axis=0, keepdims=True)
                weight = jnp.exp(score - peak)
                total = jnp.sum(weight, axis=0, keepdims=True)
                prob = (weight * (1.0 / total)).astype(BF16)
                p_ref[h, s, :, c:c + HALF] = prob
                attn_ref[out_at, cols] = dot_nn(value, prob).astype(BF16)

    @pl.when(step == pl.num_programs(0) - 1)
    def _():
        experts = route_ref.shape[0]
        for t in range(0, tok, HALF):
            cols = slice(t, t + HALF)
            x = hid_ref[t:t + HALF, :].astype(F32).T
            resid = x + dot_tn(wout_ref[...], attn_ref[:, cols])
            resid_ref[:, cols] = resid
            scale = lax.rsqrt(jnp.mean(resid * resid, axis=0, keepdims=True) + EPS)
            n2 = (resid * scale * column(gain2_ref)).astype(BF16)
            n2_ref[:, cols] = n2
            logits = dot_nn(wr_ref[...], n2)
            top = jnp.max(logits, axis=0, keepdims=True)
            e = jnp.exp(logits - top)
            route = e / jnp.sum(e, axis=0, keepdims=True)
            route_ref[:, cols] = route
            hot = lax.broadcasted_iota(jnp.int32, (experts, HALF), 0) == ids_ref[:, cols]
            gate_ref[:, cols] = jnp.sum(jnp.where(hot, route, 0.0), axis=0, keepdims=True)
        hot = lax.broadcasted_iota(jnp.int32, (experts, tok), 0) == ids_ref[...]
        gates = jnp.where(hot, gate_ref[...], 0.0)
        place = (
            lax.broadcasted_iota(jnp.int32, (LANES, tok), 0) == pos_ref[...]
        ).astype(F32).astype(BF16)
        parts = [dot_nt(part, place) for part in split3(gates)]
        which = lax.broadcasted_iota(jnp.int32, (experts, 8, LANES), 1)
        spread = [jnp.broadcast_to(part[:, None, :], which.shape) for part in parts]
        gpack_ref[...] = jnp.where(
            which == 0, spread[0],
            jnp.where(which == 1, spread[1], jnp.where(which == 2, spread[2], 0.0)),
        ).astype(BF16)
        rows = packed_ref.shape[0]

        @pl.loop(0, rows // HALF)
        def _(r):
            base = pl.multiple_of(r * HALF, HALF)
            table = (lax.broadcasted_iota(jnp.int32, (HALF, tok), 0) + base == slot_ref[...])
            packed_ref[pl.ds(base, HALF), :] = dot_nt(
                table.astype(F32).astype(BF16), n2_ref[...]
            ).astype(BF16)


def front(hidden, gain1, w_qkv, w_out, table, gain2, w_router, ids, slot, pos, seg, rel, rows):
    tok, width = hidden.shape
    experts = w_router.shape[0]
    seqs = seg.shape[0]
    wspec = lambda part: pl.BlockSpec((width, GW), lambda i: (0, part * GROUPS + i))
    qspec = pl.BlockSpec((GW, tok), lambda i: (i, 0))
    sd = jax.ShapeDtypeStruct
    outs = (
        sd((width, tok), BF16), sd((width, tok), BF16), sd((width, tok), BF16),
        sd((width, tok), BF16), sd((HEADS, seqs, LEN, LEN), BF16), sd((width, tok), BF16),
        sd((width, tok), F32), sd((width, tok), BF16), sd((experts, tok), F32), sd((1, tok), F32),
        sd((rows, width), BF16), sd((experts, 8, LANES), BF16),
    )
    return pl.pallas_call(
        front_kernel,
        grid=(GROUPS,),
        in_specs=[
            whole((tok, width)), whole((1, width)), wspec(0), wspec(1), wspec(2),
            whole((width, width)), whole((HEADS, BUCKETS)), whole((1, width)),
            whole((experts, width)), whole((1, tok)), whole((1, tok)), whole((1, tok)),
            whole((seqs, LEN)), whole((LEN, LEN)),
        ],
        out_specs=(
            whole((width, tok)), qspec, qspec, qspec,
            pl.BlockSpec((GROUP, seqs, LEN, LEN), lambda i: (i, 0, 0, 0)),
            whole((width, tok)), whole((width, tok)), whole((width, tok)),
            whole((experts, tok)), whole((1, tok)), whole((rows, width)),
            whole((experts, 8, LANES)),
        ),
        out_shape=outs,
        scratch_shapes=[
            pltpu.VMEM((LEN, LEN), jnp.int32),
            pltpu.VMEM((seqs, LEN, LEN), F32),
            pltpu.VMEM((LEN, LEN), F32),
            pltpu.VMEM((16, LANES), F32),
        ],
        compiler_params=pltpu.CompilerParams(vmem_limit_bytes=58 * MIB),
        cost_estimate=pl.CostEstimate(flops=50 * MICRO, bytes_accessed=30 * MIB, transcendentals=0),
        name="front",
    )(
        hidden, gain1.reshape(1, width), w_qkv, w_qkv, w_qkv, w_out, table,
        gain2.reshape(1, width), w_router, ids, slot, pos,
        seg, rel,
    )


def combine_kernel(rows_ref, slot_ref, gate_ref, resid_ref, out_ref):
    total = rows_ref.shape[0]
    cols = slot_ref.shape[1]
    table = lax.broadcasted_iota(jnp.int32, (total, cols), 0) == slot_ref[...]
    combined = dot_tn(rows_ref[...], table.astype(F32).astype(BF16))
    out_ref[...] = (resid_ref[...] + gate_ref[...] * combined).T.astype(BF16)


def combine(rows, slot, gate, resid):
    total, width = rows.shape
    tok = slot.shape[1]
    line = pl.BlockSpec((1, HALF), lambda i: (0, i))
    return pl.pallas_call(
        combine_kernel,
        grid=(tok // HALF,),
        in_specs=[
            whole((total, width)), line, line, pl.BlockSpec((width, HALF), lambda i: (0, i)),
        ],
        out_specs=pl.BlockSpec((HALF, width), lambda i: (i, 0)),
        out_shape=jax.ShapeDtypeStruct((tok, width), BF16),
        compiler_params=pltpu.CompilerParams(vmem_limit_bytes=40 * MIB),
        cost_estimate=pl.CostEstimate(flops=6 * MICRO, bytes_accessed=8 * MIB, transcendentals=0),
        name="combine",
    )(rows, slot, gate, resid)


CUBE = 0.044715
ROOT = 0.7978845608028654
FTILE = 768


def gelu_pair(x):
    square = x * x
    t = jnp.tanh(ROOT * (x + CUBE * (x * square)))
    half = 0.5 + 0.5 * t
    slope = half + (0.5 * x) * (1.0 - t * t) * (ROOT + (3.0 * CUBE * ROOT) * square)
    return x * half, slope


def device_of(index):
    wide = lax.axis_size("wide")
    return (index // wide, lax.rem(index, wide))


def expert_kernel(
    block,
    packed, gpack, grows, w_in, w_down,
    dx_out, out_got, rest_out, active_out, ginner_out, gs_out, x_out, gg_out,
    xbuf, gatebuf, gbuf, win, wdown, active, slope, ginner, gs, dx, outs, ggsend, ggbuf,
    x_send, x_recv, gate_send, gate_recv, gg_ssem, gg_rsem, o_send, o_recv, self_sem, load_sem, store_sem,
):
    count = lax.axis_size("narrow") * lax.axis_size("wide")
    me = lax.axis_index("narrow") * lax.axis_size("wide") + lax.axis_index("wide")
    blocks = count // block
    mine = me // block
    capp = packed.shape[1]
    rows = block * capp
    total = count * capp
    hidden = w_in.shape[1]
    mesh_id = pl.DeviceIdType.MESH

    def x_copy(target, source):
        return pltpu.make_async_remote_copy(
            src_ref=packed.at[target], dst_ref=xbuf.at[source], send_sem=x_send.at[target],
            recv_sem=x_recv.at[source], device_id=device_of(target), device_id_type=mesh_id,
        )

    def gate_copy(target, source):
        return pltpu.make_async_remote_copy(
            src_ref=gpack.at[target], dst_ref=gatebuf.at[source], send_sem=gate_send.at[target],
            recv_sem=gate_recv.at[source], device_id=device_of(target), device_id_type=mesh_id,
        )

    def gg_copy(target, source):
        return pltpu.make_async_remote_copy(
            src_ref=ggsend.at[target], dst_ref=ggbuf.at[source], send_sem=gg_ssem.at[target],
            recv_sem=gg_rsem.at[source], device_id=device_of(target), device_id_type=mesh_id,
        )

    ahead = blocks // 2
    inner = lax.rem(me, block)

    def out_copy(c, j):
        target = lax.rem(mine + c, blocks) * block + j
        return pltpu.make_async_remote_copy(
            src_ref=outs.at[c * block + j], dst_ref=out_got.at[c * block + inner],
            send_sem=o_send.at[c * block + j], recv_sem=o_recv.at[c * block + inner],
            device_id=device_of(target), device_id_type=mesh_id,
        )

    def out_wait(c, j):
        return pltpu.make_async_remote_copy(
            src_ref=outs.at[c * block + j], dst_ref=out_got.at[c * block + j],
            send_sem=o_send.at[c * block + j], recv_sem=o_recv.at[c * block + j],
            device_id=device_of(lax.rem(me + 1, count)), device_id_type=mesh_id,
        )

    barrier = pltpu.get_barrier_semaphore()

    @pl.loop(1, count)
    def _(s):
        pl.semaphore_signal(
            barrier, inc=1, device_id=device_of(lax.rem(me + s, count)), device_id_type=mesh_id
        )

    loads = [
        pltpu.make_async_copy(w_in, win, load_sem.at[0]),
        pltpu.make_async_copy(w_down, wdown, load_sem.at[1]),
        pltpu.make_async_copy(grows, gbuf, load_sem.at[2]),
    ]
    own = [
        pltpu.make_async_copy(packed.at[me], xbuf.at[me], self_sem.at[0]),
        pltpu.make_async_copy(gpack.at[me], gatebuf.at[me], self_sem.at[1]),
    ]
    for copy in own + loads:
        copy.start()
    pl.semaphore_wait(barrier, count - 1)

    @pl.loop(0, blocks)
    def _(c):
        there = lax.rem(mine + blocks - c, blocks)

        @pl.loop(0, block)
        def _(j):
            target = there * block + j

            @pl.when(target != me)
            def _():
                gate_copy(target, me).start()
                x_copy(target, me).start()

    for copy in own + loads:
        copy.wait()

    def stores(at):
        return [
            pltpu.make_async_copy(dx.at[at], dx_out.at[at], store_sem.at[0]),
            pltpu.make_async_copy(active.at[at], active_out.at[at], store_sem.at[1]),
            pltpu.make_async_copy(ginner.at[at], ginner_out.at[at], store_sem.at[2]),
            pltpu.make_async_copy(gs.at[at], gs_out.at[at], store_sem.at[3]),
        ]

    @pl.loop(0, blocks)
    def _(c):
        here = lax.rem(mine + c, blocks)
        first = here * block

        @pl.loop(0, block)
        def _(j):
            source = first + j

            @pl.when(source != me)
            def _():
                gate_copy(me, source).wait_recv()
                x_copy(me, source).wait_recv()

        at = pl.ds(pl.multiple_of(here * rows, rows), rows)
        group = pl.ds(first, block)
        x = xbuf[group].reshape(rows, xbuf.shape[2])

        @pl.loop(0, hidden // FTILE)
        def _(f):
            tile = pl.ds(pl.multiple_of(f * FTILE, FTILE), FTILE)
            value, grad = gelu_pair(dot_nn(x, win[:, tile]))
            active[at, tile] = value.astype(BF16)
            slope[:, tile] = grad

        result = dot_nn(active[at, :], wdown[...]).astype(BF16)
        outs[pl.ds(c * block, block)] = result.reshape(block, capp, result.shape[1])

        @pl.when(c < ahead)
        def _():
            @pl.loop(0, block)
            def _(j):
                @pl.when(first + j != me)
                def _():
                    out_copy(c, j).start()

        g = gbuf[group].astype(F32)
        diag = (
            lax.broadcasted_iota(jnp.int32, (block, capp, LANES), 1)
            == lax.broadcasted_iota(jnp.int32, (block, capp, LANES), 2)
        )
        gate = jnp.sum(gatebuf[group].astype(F32), axis=1)
        gate = jnp.sum(
            jnp.where(diag, gate[:, None, :], 0.0), axis=2, keepdims=True
        )
        gs[at, :] = (gate * g).astype(BF16).reshape(rows, g.shape[2])
        gg = jnp.sum(g * result.astype(F32).reshape(g.shape), axis=2, keepdims=True)
        gg = jnp.sum(jnp.where(diag, gg, 0.0), axis=1)
        which = lax.broadcasted_iota(jnp.int32, (block, 8, LANES), 1)
        high, mid, low = [part.astype(F32)[:, None, :] for part in split3(gg)]
        ggsend[group] = jnp.where(
            which == 0, high, jnp.where(which == 1, mid, jnp.where(which == 2, low, 0.0))
        ).astype(BF16)

        @pl.loop(0, block)
        def _(j):
            source = first + j

            @pl.when(source != me)
            def _():
                gg_copy(source, me).start()

        @pl.loop(0, hidden // FTILE)
        def _(f):
            tile = pl.ds(pl.multiple_of(f * FTILE, FTILE), FTILE)
            grad = dot_nt(gs[at, :], wdown[tile, :])
            ginner[at, tile] = (grad * slope[:, tile]).astype(BF16)

        dx[at, :] = dot_nt(ginner[at, :], win[...]).astype(BF16)

        for copy in stores(at):
            copy.start()

    for copy in stores(pl.ds(0, total)):
        copy.wait()
    keep = [
        pltpu.make_async_copy(xbuf, x_out, load_sem.at[0]),
        pltpu.make_async_copy(ggsend.at[me], ggbuf.at[me], self_sem.at[0]),
        pltpu.make_async_copy(outs.at[inner], out_got.at[inner], self_sem.at[1]),
        pltpu.make_async_copy(
            outs.at[pl.ds(ahead * block, count - ahead * block)], rest_out, load_sem.at[1]
        ),
    ]
    for copy in keep:
        copy.start()

    @pl.loop(0, count)
    def _(other):
        @pl.when(other != me)
        def _():
            x_copy(other, me).wait_send()
            gate_copy(other, me).wait_send()
            gg_copy(other, me).wait_send()
            gg_copy(me, other).wait_recv()

    @pl.loop(0, ahead * block)
    def _(i):
        @pl.when(i != inner)
        def _():
            out_wait(i // block, lax.rem(i, block)).wait_send()
            out_wait(i // block, lax.rem(i, block)).wait_recv()

    for copy in keep:
        copy.wait()
    last = pltpu.make_async_copy(ggbuf, gg_out, load_sem.at[1])
    last.start()
    last.wait()


def block_of(count, capp):
    block = 1
    while block * 4 <= count and block * 2 * capp <= 320:
        block *= 2
    return block


def expert(packed, gpack, grows, w_in, w_down):
    count, capp, width = packed.shape
    hidden = w_in.shape[1]
    block = block_of(count, capp)
    early = (count // block // 2) * block
    rows = block * capp
    total = count * capp
    sd = jax.ShapeDtypeStruct
    anyspec = pl.BlockSpec(memory_space=pl.ANY)
    dma = pltpu.SemaphoreType.DMA
    return pl.pallas_call(
        functools.partial(expert_kernel, block),
        in_specs=[anyspec] * 5,
        out_specs=(anyspec,) * 8,
        out_shape=(
            sd((total, width), BF16), sd((early, capp, width), BF16),
            sd((count - early, capp, width), BF16), sd((total, hidden), BF16), sd((total, hidden), BF16), sd((total, width), BF16), sd((count, capp, width), BF16),
            sd((count, 8, LANES), BF16),
        ),
        scratch_shapes=[
            pltpu.VMEM((count, capp, width), BF16), pltpu.VMEM((count, 8, LANES), BF16),
            pltpu.VMEM((count, capp, width), BF16), pltpu.VMEM((width, hidden), BF16),
            pltpu.VMEM((hidden, width), BF16), pltpu.VMEM((total, hidden), BF16),
            pltpu.VMEM((rows, hidden), F32), pltpu.VMEM((total, hidden), BF16),
            pltpu.VMEM((total, width), BF16), pltpu.VMEM((total, width), BF16),
            pltpu.VMEM((count, capp, width), BF16), pltpu.VMEM((count, 8, LANES), BF16),
            pltpu.VMEM((count, 8, LANES), BF16),
            dma((count,)), dma((count,)), dma((count,)), dma((count,)), dma((count,)), dma((count,)),
            dma((early,)), dma((early,)), dma((2,)), dma((3,)), dma((4,)),
        ],
        compiler_params=pltpu.CompilerParams(
            collective_id=0, has_side_effects=True, vmem_limit_bytes=62 * MIB
        ),
        cost_estimate=pl.CostEstimate(flops=60 * MICRO, bytes_accessed=60 * 1024 * 1024, transcendentals=0),
        name="expert",
    )(packed, gpack, grows, w_in, w_down)


def weights_kernel(active_ref, gs_ref, x_ref, ginner_ref, down_ref, in_ref, xt):
    @pl.when(pl.program_id(0) == 0)
    def _():
        total = x_ref.shape[0]
        for t in range(0, total, HALF):
            xt[:, t:t + HALF] = x_ref[t:t + HALF, :].T

    down_ref[0] = dot_tn(active_ref[...], gs_ref[...])
    in_ref[0] = dot_nn(xt[...], ginner_ref[...])


def weight_grads(active, gs, x, ginner):
    total, hidden = active.shape
    width = gs.shape[1]
    tile = HALF
    cols = pl.BlockSpec((total, tile), lambda i: (0, i))
    return pl.pallas_call(
        weights_kernel,
        grid=(hidden // tile,),
        in_specs=[cols, whole((total, width)), whole((total, width)), cols],
        out_specs=(
            pl.BlockSpec((1, tile, width), lambda i: (0, i, 0)),
            pl.BlockSpec((1, width, tile), lambda i: (0, 0, i)),
        ),
        out_shape=(
            jax.ShapeDtypeStruct((1, hidden, width), F32),
            jax.ShapeDtypeStruct((1, width, hidden), F32),
        ),
        scratch_shapes=[pltpu.VMEM((width, total), BF16)],
        compiler_params=pltpu.CompilerParams(vmem_limit_bytes=62 * MIB),
        cost_estimate=pl.CostEstimate(flops=18 * MICRO, bytes_accessed=36 * 1024 * 1024, transcendentals=0),
        name="weight_grads",
    )(active, gs, x, ginner)
PIECES = 32
BIG = 2
UNITS = BIG + GROUPS
TROWS = 16
LATE = 24
LAST_PHASE = 7


def norm_back(grad, source, gain):
    scale = lax.rsqrt(jnp.mean(source * source, axis=0, keepdims=True) + EPS)
    normed = source * scale
    scaled = grad * gain
    inner = jnp.mean(scaled * normed, axis=0, keepdims=True)
    part = grad * normed
    part = part[:, :LANES] + part[:, LANES:]
    return scale * (scaled - normed * inner), part


def back_kernel(
    block,
    dx_ref, gg_ref, slot_ref, pos_ref, ids_ref, route_ref, gate_ref, n2_ref, attn_ref,
    gain1_ref, gain2_ref, wr_ref, wout_ref, resid_any, g_any, hid_any, n1_any, q_any, k_any, v_any, p_any,
    wqkv_any, rel_any, rest_any,
    ingrad_any, out_got, big_out, small_out, early_out, late_out,
    gres, ga, gn1, dv, soft, hid_ref, n1_ref, q_ref, k_ref, v_ref, wqkv_ref, rel_ref, acc,
    *buffers_and_rest,
):
    buffers = buffers_and_rest[:16]
    inside = buffers[7].shape == big_out.shape
    big = buffers[:7] + (buffers[7] if inside else big_out,)
    small = buffers[8:15] + (buffers[15] if inside else small_out,)
    (
        early, early_got, late, late_got, send, recv, xsend, xrecv, esend, erecv, lsend, lrecv, osend, orecv, load_sem, store_sem, stage_sem, write_sem,
    ) = buffers_and_rest[16:]
    dq, dk = dv.at[pl.ds(0, GW)], dv.at[pl.ds(GW, GW)]
    step = pl.program_id(0)
    pair = pl.program_id(1)
    tok = g_any.shape[0]
    seqs = tok // LEN
    experts = route_ref.shape[0]
    total = dx_ref.shape[0]
    width = g_any.shape[1]
    narrow_n, wide_n = lax.axis_size("narrow"), lax.axis_size("wide")
    n, w = lax.axis_index("narrow"), lax.axis_index("wide")
    core, zed = lax.rem(w, 2), lax.rem(w // 2, 4)
    ex, why = lax.rem(n, 2), lax.rem(n // 2, 2)
    more_n = (narrow_n // 4) * (wide_n // 8)
    more_w = wide_n // 8
    more = (n // 4) * more_w + w // 8
    mesh_id = pl.DeviceIdType.MESH
    core_dev = (n, w + 1 - 2 * core)
    ex_dev = (n + 1 - 2 * ex, w)
    why_dev = (n + 2 - 4 * why, w)

    def zed_dev(step):
        return (n, w + 2 * (lax.rem(zed + step, 4) - zed))

    def more_dev(step):
        other = lax.rem(more + step, more_n)
        return (n + 4 * (other // more_w - more // more_w),
                w + 8 * (lax.rem(other, more_w) - lax.rem(more, more_w)))

    def unit(u):
        if isinstance(u, int):
            return (big, u, u) if u < BIG else (small, u - BIG, u)
        return small, u, u + BIG

    def ref(which, u):
        group, at, _ = unit(u)
        return group[which], at

    def view(which, u, *more):
        group, at, _ = unit(u)
        return group[which].at[(at,) + more]

    def land(u, q, at):
        return view(7, u, q, at)

    def spot(q):
        first, second = (ex, why) if q == 0 else (why, ex)
        b16 = core * 16
        b8 = b16 + first * 8
        b4 = b8 + second * 4
        return first, second, b16, b8, b4

    def remote(src, dst, k, u, q, dev):
        return pltpu.make_async_remote_copy(
            src_ref=src, dst_ref=dst, send_sem=send.at[k, unit(u)[2], q], recv_sem=recv.at[k, unit(u)[2], q],
            device_id=dev, device_id_type=mesh_id,
        )

    def outgoing(phase, u, q):
        first, second, b16, b8, b4 = spot(q)
        one, two = (ex_dev, why_dev) if q == 0 else (why_dev, ex_dev)
        if phase == 0:
            return [remote(view(0, u, q, pl.ds(16 - b16, 16)), view(2, u, q), 0, u, q, core_dev)]
        if phase == 1:
            src = view(0, u, q, pl.ds(b16 + (1 - first) * 8, 8))
            return [remote(src, view(3, u, q), 1, u, q, one)]
        if phase == 2:
            src = view(0, u, q, pl.ds(b8 + (1 - second) * 4, 4))
            return [remote(src, view(4, u, q), 2, u, q, two)]
        if phase == 3:
            return [
                remote(view(0, u, q, b4 + lax.rem(zed + step, 4)), view(5, u, q, step - 1),
                       2 + step, u, q, zed_dev(step))
                for step in (1, 2, 3)
            ]
        if phase == 4:
            mine = land(u, q, b4 + zed)
            return [remote(view(1, u, q), mine, 5 + step, u, q, zed_dev(step)) for step in (1, 2, 3)]
        if phase == 5:
            mine = land(u, q, pl.ds(b4, 4))
            return [remote(mine, mine, 9, u, q, two)]
        if phase == 6:
            mine = land(u, q, pl.ds(b8, 8))
            return [remote(mine, mine, 10, u, q, one)]
        mine = land(u, q, pl.ds(b16, 16))
        return [remote(mine, mine, 11, u, q, core_dev)]

    def incoming(phase, u, q):
        first, second, b16, b8, b4 = spot(q)
        if phase < 4:
            return outgoing(phase, u, q)
        if phase == 4:
            return [
                remote(view(1, u, q), land(u, q, b4 + lax.rem(zed + 4 - step, 4)),
                       5 + step, u, q, zed_dev(step))
                for step in (1, 2, 3)
            ]
        if phase == 5:
            there = land(u, q, pl.ds(b8 + (1 - second) * 4, 4))
            return [remote(there, there, 9, u, q, core_dev)]
        if phase == 6:
            there = land(u, q, pl.ds(b16 + (1 - first) * 8, 8))
            return [remote(there, there, 10, u, q, core_dev)]
        there = land(u, q, pl.ds(16 - b16, 16))
        return [remote(there, there, 11, u, q, core_dev)]

    def add(u, q, start, count, which):
        own, at = ref(0, u)
        got = ref(which, u)[0]

        @pl.loop(0, count)
        def _(i):
            own[at, q, start + i] = (
                own[at, q, start + i].astype(F32) + got[at, q, i].astype(F32)
            ).astype(BF16)

    def spread(u, q):
        (done, at), (extra, _) = ref(1, u), ref(6, u)
        extra[at, q, more] = done[at, q]
        copies = [
            pltpu.make_async_remote_copy(
                src_ref=view(6, u, q, more), dst_ref=view(6, u, q, more),
                send_sem=xsend.at[unit(u)[2], q, step], recv_sem=xrecv.at[unit(u)[2], q, step],
                device_id=more_dev(step), device_id_type=mesh_id,
            )
            for step in range(1, more_n)
        ]
        for copy in copies:
            copy.start()
        for step in range(1, more_n):
            other = lax.rem(more + more_n - step, more_n)
            pltpu.make_async_remote_copy(
                src_ref=view(6, u, q, more), dst_ref=view(6, u, q, other),
                send_sem=xsend.at[unit(u)[2], q, step], recv_sem=xrecv.at[unit(u)[2], q, step],
                device_id=more_dev(step), device_id_type=mesh_id,
            ).wait_recv()
        for copy in copies:
            copy.wait_send()
        total = extra[at, q, 0].astype(F32)
        for i in range(1, more_n):
            total = total + extra[at, q, i].astype(F32)
        done[at, q] = total.astype(BF16)

    def keep(u, q):
        at = spot(q)[4] + zed
        return pltpu.make_async_copy(view(1, u, q), land(u, q, at), store_sem.at[unit(u)[2], q])

    def settle(phase, u, q):
        first, second, b16, b8, b4 = spot(q)
        if phase == 0:
            add(u, q, b16, 16, 2)
        elif phase == 1:
            add(u, q, b8, 8, 3)
        elif phase == 2:
            add(u, q, b4, 4, 4)
        elif phase == 3:
            (own, at), (done, _), (got, _) = ref(0, u), ref(1, u), ref(5, u)
            done[at, q] = (
                own[at, q, b4 + zed].astype(F32) + got[at, q, 0].astype(F32)
                + (got[at, q, 1].astype(F32) + got[at, q, 2].astype(F32))
            ).astype(BF16)
            if more_n > 1:
                spread(u, q)
            keep(u, q).start()
        elif phase == 4:
            keep(u, q).wait()

    bits = []
    for axis, count in (("wide", wide_n), ("narrow", narrow_n)):
        size = 1
        while size < count:
            at = lax.rem((w if axis == "wide" else n) // size, 2)
            move = size - 2 * size * at
            bits.append((n, w + move) if axis == "wide" else (n + move, w))
            size *= 2
    levels = len(bits)
    early_levels = early_got.shape[0] if early.shape[0] > 1 else 0

    def swap(level, mine, got, ssem, rsem):
        return pltpu.make_async_remote_copy(
            src_ref=mine.at[level], dst_ref=got.at[level], send_sem=ssem.at[level],
            recv_sem=rsem.at[level], device_id=bits[level], device_id_type=mesh_id,
        )

    def climb(level, mine, got, ssem, rsem):
        copy = swap(level, mine, got, ssem, rsem)
        copy.wait_recv()
        copy.wait_send()
        mine[level + 1] = mine[level] + got[level]
        if level + 1 < levels:
            swap(level + 1, mine, got, ssem, rsem).start()

    def climb_early(level):
        climb(level, early, early_got, esend, erecv)

    def climb_late(level):
        climb(level, late, late_got, lsend, lrecv)

    count = narrow_n * wide_n
    blocks = count // block
    ahead = blocks // 2
    index = n * wide_n + w
    rest = rest_any.shape[0]

    def out_copy(i):
        target = lax.rem(index // block + ahead + i // block, blocks) * block + lax.rem(i, block)
        return pltpu.make_async_remote_copy(
            src_ref=rest_any.at[i],
            dst_ref=out_got.at[(i // block) * block + lax.rem(index, block)],
            send_sem=osend.at[i], recv_sem=orecv.at[(i // block) * block + lax.rem(index, block)],
            device_id=device_of(target), device_id_type=mesh_id,
        )

    def out_wait(i):
        return pltpu.make_async_remote_copy(
            src_ref=rest_any.at[i], dst_ref=out_got.at[i], send_sem=osend.at[i],
            recv_sem=orecv.at[i], device_id=core_dev, device_id_type=mesh_id,
        )

    def begin(u):
        for q in range(2):
            for copy in outgoing(0, u, q):
                copy.start()

    def advance(u, phase):
        for q in range(2):
            for copy in incoming(phase, u, q):
                copy.wait_recv()
            for copy in outgoing(phase, u, q):
                copy.wait_send()
            settle(phase, u, q)
            if phase < LAST_PHASE:
                for copy in outgoing(phase + 1, u, q):
                    copy.start()
        if inside and phase == LAST_PHASE:
            write_out(u).start()

    def write_out(u):
        group, at, flat = unit(u)
        out = big_out if u < BIG else small_out
        return pltpu.make_async_copy(group[7].at[at], out.at[at], write_sem.at[flat])

    def place(u, first, value):
        own, at = ref(0, u)
        half = own.shape[4]
        count = value.shape[1]
        blocks = value.reshape(PIECES, width // PIECES, count).astype(BF16)
        done = 0
        while done < count:
            q, within = (first + done) // half, (first + done) % half
            size = min(half - within, count - done)
            own[at, q, :, :, within:within + size] = blocks[:, :, done:done + size]
            done += size

    def soft_load(group):
        at = pl.ds(group * GROUP, GROUP)
        return pltpu.make_async_copy(p_any.at[at], soft.at[at], load_sem.at[group])

    pairs = ((n1_any, n1_ref), (wqkv_any, wqkv_ref), (v_any, v_ref), (k_any, k_ref), (q_any, q_ref),
             (rel_any, rel_ref))
    loads = [
        pltpu.make_async_copy(src, dst, load_sem.at[GROUPS + i]) for i, (src, dst) in enumerate(pairs)
    ]

    rows_load = [
        pltpu.make_async_copy(src, hid_ref, load_sem.at[GROUPS + 6 + i])
        for i, src in enumerate((g_any, hid_any))
    ]

    barrier = pltpu.get_barrier_semaphore()
    greet = [core_dev, ex_dev, why_dev] + [zed_dev(move) for move in (1, 2, 3)]
    greet += [more_dev(move) for move in range(1, more_n)] + bits

    @pl.when((step == 0) & (pair == 0))
    def _():
        first = pltpu.make_async_copy(resid_any, gres, stage_sem)
        first.start()
        rows_load[0].start()
        for group in range(GROUPS):
            soft_load(group).start()
        for copy in loads:
            copy.start()
        for dev in greet:
            pl.semaphore_signal(barrier, inc=1, device_id=dev, device_id_type=mesh_id)

        @pl.loop(0, rest)
        def _(i):
            source = lax.rem(
                index // block + 2 * blocks - ahead - i // block, blocks
            ) * block + lax.rem(i, block)
            pl.semaphore_signal(
                barrier, inc=1, device_id=device_of(source), device_id_type=mesh_id
            )

        pl.semaphore_wait(barrier, len(greet) + rest)

        @pl.loop(0, rest)
        def _(i):
            out_copy(i).start()

        hot = lax.broadcasted_iota(jnp.int32, (experts, tok), 0) == ids_ref[...]
        where = (
            lax.broadcasted_iota(jnp.int32, (LANES, tok), 0) == pos_ref[...]
        ).astype(F32).astype(BF16)
        grad_gate = jnp.zeros((1, tok), F32)
        for e in range(0, experts, 32):
            found = dot_nn(gg_ref[e:e + 32].reshape(256, LANES), where)
            found = jnp.sum(found.reshape(32, 8, tok), axis=1)
            grad_gate += jnp.sum(jnp.where(hot[e:e + 32], found, 0.0), axis=0, keepdims=True)
        first.wait()
        rows_load[0].wait()
        grad_logits = (
            (grad_gate * gate_ref[...]) * (hot.astype(F32) - route_ref[...])
        ).astype(BF16)
        early[0, :experts, :] = dot_nt(grad_logits, n2_ref[...])
        gain_grad = jnp.zeros((width, LANES), F32)
        for t in range(0, tok, HALF):
            cols = slice(t, t + HALF)
            gn2 = dot_tn(wr_ref[...], grad_logits[:, cols])
            size = total if total <= 1280 else 512
            for r in range(0, total, size):
                table = lax.broadcasted_iota(jnp.int32, (size, HALF), 0) + r == slot_ref[:, cols]
                gn2 = gn2 + dot_tn(dx_ref[r:r + size, :], table.astype(F32).astype(BF16))
            branch, part = norm_back(gn2, gres[:, cols], column(gain2_ref))
            gain_grad = gain_grad + part
            gr = hid_ref[t:t + HALF, :].astype(F32).T + branch
            gres[:, cols] = gr
            ga[:, cols] = gr.astype(BF16)
        early[0, experts:, :] = jnp.broadcast_to(
            jnp.sum(gain_grad.T, axis=0, keepdims=True), (8, width)
        )
        for c in range(0, width, HALF):
            place(0, c, dot_nt(attn_ref[...], ga[c:c + HALF, :]))
        rows_load[1].start()
        begin(0)
        if early_levels:
            swap(0, early, early_got, esend, erecv).start()
        for t in range(0, tok, HALF):
            cols = slice(t, t + HALF)
            ga[:, cols] = dot_nn(wout_ref[...], ga[:, cols]).astype(BF16)
        for group in range(GROUPS):
            soft_load(group).wait()

            @pl.loop(group * GROUP, (group + 1) * GROUP)
            def _(head):
                at = pl.ds(pl.multiple_of(head * HEAD_DIM, HEAD_DIM), HEAD_DIM)
                for s in range(seqs):
                    row = slice(s * LEN, (s + 1) * LEN)
                    dv[at, row] = dot_nt(ga[at, row], soft[head, s]).astype(BF16)

        loads[0].wait()
        for c in range(0, width, GW):
            place(1, c, dot_nt(n1_ref[...], dv[c:c + GW, :]))
        begin(1)
        loads[1].wait()
        for t in range(0, tok, HALF):
            gn1[:, t:t + HALF] = dot_nn(wqkv_ref[:, 2 * width:], dv[:, t:t + HALF])
        for copy in loads[2:5]:
            copy.wait()

    @pl.loop(0, PAIR)
    def _(h):
        turn = pair * PAIR + h
        head = step * GROUP + turn
        at = pl.ds(pl.multiple_of(turn * HEAD_DIM, HEAD_DIM), HEAD_DIM)
        all_at = pl.ds(pl.multiple_of(head * HEAD_DIM, HEAD_DIM), HEAD_DIM)
        for s in range(seqs):
            row = slice(s * LEN, (s + 1) * LEN)
            value = v_ref[all_at, row]
            for c in range(0, LEN, HALF):
                cols = slice(s * LEN + c, s * LEN + c + HALF)
                grad = ga[all_at, cols]
                inner = jnp.sum(
                    grad.astype(F32) * attn_ref[all_at, cols].astype(F32), axis=0, keepdims=True
                )
                gp = dot_tn(value, grad)
                soft[head, s, :, c:c + HALF] = (
                    soft[head, s, :, c:c + HALF].astype(F32) * (gp - inner)
                ).astype(BF16)
            ds = soft[head, s]
            factor = HEAD_DIM ** -0.5
            dq[at, row] = (dot_nn(k_ref[all_at, row], ds) * factor).astype(BF16)
            dk[at, row] = (dot_nt(q_ref[all_at, row], ds) * factor).astype(BF16)

        for number in range(HEADS):
            todo = [(u, phase) for u, phase, at_head in SCHEDULE if at_head == number]
            rise = [level for level, at_head in enumerate(EARLY_LEVELS)
                    if at_head == number and level < early_levels]
            if todo or rise:
                @pl.when(head == number)
                def _():
                    for u, phase in todo:
                        advance(u, phase)
                    for level in rise:
                        climb_early(level)

    @pl.when(pair == pl.num_programs(1) - 1)
    def _():
        for part, d in enumerate((dq, dk)):
            place(step, part * GW, dot_nt(n1_ref[...], d[...]))
        begin(step)
        for part, d in enumerate((dq, dk)):
            cols = pl.ds(pl.multiple_of(part * width + step * GW, GW), GW)
            gn1[...] += dot_nn(wqkv_ref[:, cols], d[...])

    @pl.when((step == pl.num_programs(0) - 1) & (pair == pl.num_programs(1) - 1))
    def _():
        planned = {(u, phase) for u, phase, at_head in SCHEDULE}
        left = {u: [phase for phase in range(LAST_PHASE + 1) if (u, phase) not in planned]
                for u in range(UNITS)}

        def push():
            for u in range(UNITS):
                if left[u]:
                    advance(u, left[u].pop(0))

        rows_load[1].wait()
        loads[5].wait()
        gain_grad = jnp.zeros((width, LANES), F32)
        for t in range(0, tok, HALF):
            cols = slice(t, t + HALF)
            x = hid_ref[t:t + HALF, :].astype(F32).T
            branch, part = norm_back(gn1[:, cols], x, column(gain1_ref))
            gain_grad = gain_grad + part
            gres[:, cols] = gres[:, cols] + branch
            if t == HALF:
                push()
        pltpu.make_async_copy(gres, ingrad_any, stage_sem).start()
        line = jnp.sum(gain_grad.T, axis=0, keepdims=True)
        late[0] = jnp.zeros((LATE, LANES), F32)
        for i in range(width // LANES):
            late[0, i:i + 1, :] = line[:, i * LANES:(i + 1) * LANES]
        push()
        lines = HEADS * seqs
        acc[...] = jnp.zeros_like(acc)
        chunks = 2
        for chunk in range(chunks):
            @pl.loop(chunk * (LEN // TROWS // chunks), (chunk + 1) * (LEN // TROWS // chunks))
            def _(r):
                base = pl.multiple_of(r * TROWS, TROWS)
                lhs = soft[:, :, pl.ds(base, TROWS), :].reshape(lines * TROWS, LEN)
                rel = rel_ref[pl.ds(base, TROWS), :]
                hot = (
                    rel[:, None, :]
                    == lax.broadcasted_iota(jnp.int32, (TROWS, BUCKETS, LEN), 1)
                ).astype(F32).astype(BF16).reshape(TROWS * BUCKETS, LEN)
                acc[...] += dot_nt(lhs, hot)

            push()
        rows = lax.broadcasted_iota(jnp.int32, acc.shape, 0) % TROWS
        cols = lax.broadcasted_iota(jnp.int32, acc.shape, 1) // BUCKETS
        kept = jnp.where(rows == cols, acc[...], 0.0)
        per_head = jnp.sum(kept.reshape(HEADS, seqs * TROWS, acc.shape[1]), axis=1)
        fold = (
            lax.broadcasted_iota(jnp.int32, (LANES, acc.shape[1]), 1) % BUCKETS
            == lax.broadcasted_iota(jnp.int32, (LANES, acc.shape[1]), 0)
        ).astype(F32)
        late[0, 8:8 + HEADS, :] = lax.dot_general(
            per_head, fold, (((1,), (1,)), ((), ())), precision=lax.Precision.HIGHEST,
            preferred_element_type=F32,
        )
        swap(0, late, late_got, lsend, lrecv).start()
        level = 0
        while any(left.values()) or level < levels:
            push()
            if level < levels:
                climb_late(level)
                level += 1
        for level in range(early_levels):
            if level >= len(EARLY_LEVELS):
                climb_early(level)
        pltpu.make_async_copy(gres, ingrad_any, stage_sem).wait()

        @pl.loop(0, rest)
        def _(i):
            out_wait(i).wait_send()
            out_wait(i).wait_recv()

        if inside:
            for u in range(UNITS):
                write_out(u).wait()
        early_out[...] = early[early_levels]
        late_out[...] = late[levels]


EARLY_MOST = 64
EARLY_LEVELS = (1, 3, 5, 7, 9)
SCHEDULE = (
    [(0, phase, at) for phase, at in enumerate((1, 3, 5, 7, 9, 11))]
    + [(1, phase, at) for phase, at in enumerate((3, 5, 7, 9, 11))]
    + [(2, phase, at) for phase, at in enumerate((7, 9, 11))]
    + [(3, phase, at) for phase, at in enumerate((11,))]
)


def back(dx, gg, slot, pos, ids, route, gate, resid, n2, attn, g, hidden, n1, q, k, v, p, gain1, gain2,
         w_router, w_out, w_qkv, relt, rest, block):
    tok, width = hidden.shape
    experts = w_router.shape[0]
    total = dx.shape[0]
    seqs = p.shape[1]
    narrow_n, wide_n = lax.axis_size("narrow"), lax.axis_size("wide")
    levels = (narrow_n * wide_n).bit_length() - 1
    more_n = (narrow_n // 4) * (wide_n // 8)
    early_levels = levels if experts <= EARLY_MOST else 0
    rows = width // PIECES
    anyspec = pl.BlockSpec(memory_space=pl.ANY)
    sd = jax.ShapeDtypeStruct
    dma = pltpu.SemaphoreType.DMA
    vm = pltpu.VMEM

    def bufs(number, half):
        return [
            vm((number, 2) + lead + (rows, half), BF16)
            for lead in ((PIECES,), (), (16,), (8,), (4,), (3,), (more_n,))
        ] + [vm((number, 2, PIECES, rows, half) if more_n == 1 else (8, LANES), BF16)]

    return pl.pallas_call(
        functools.partial(back_kernel, block),
        grid=(GROUPS, GROUP // PAIR),
        in_specs=[
            whole((total, width)), whole((experts, 8, LANES)), whole((1, tok)), whole((1, tok)),
            whole((1, tok)), whole((experts, tok)), whole((1, tok)), whole((width, tok)),
            whole((width, tok)), whole((1, width)), whole((1, width)),
            whole((experts, width)), whole((width, width)),
        ] + [anyspec] * 11,
        out_specs=(
            anyspec, anyspec, anyspec, anyspec, whole((experts + 8, width)), whole((LATE, LANES)),
        ),
        out_shape=(
            sd((width, tok), F32), sd(rest.shape, BF16), sd((BIG, 2, PIECES, rows, width // 2), BF16),
            sd((GROUPS, 2, PIECES, rows, GW), BF16),
            sd((experts + 8, width), F32), sd((LATE, LANES), F32),
        ),
        scratch_shapes=[
            vm((width, tok), F32), vm((width, tok), BF16), vm((width, tok), F32),
            vm((width, tok), BF16),
            vm((HEADS, seqs, LEN, LEN), BF16), vm((tok, width), BF16), vm((width, tok), BF16),
            vm((width, tok), BF16), vm((width, tok), BF16), vm((width, tok), BF16),
            vm(w_qkv.shape, BF16), vm((LEN, LEN), jnp.int32), vm((HEADS * seqs * TROWS, TROWS * BUCKETS), F32),
            *bufs(BIG, width // 2), *bufs(GROUPS, GW),
            vm((early_levels + 1, experts + 8, width), F32),
            vm((max(early_levels, 1), experts + 8, width) if early_levels else (1, 8, width), F32),
            vm((levels + 1, LATE, LANES), F32), vm((levels, LATE, LANES), F32),
            dma((12, UNITS, 2)), dma((12, UNITS, 2)), dma((UNITS, 2, more_n)),
            dma((UNITS, 2, more_n)), dma((levels,)), dma((levels,)), dma((levels,)), dma((levels,)),
            dma((rest.shape[0],)), dma((rest.shape[0],)),
            dma((GROUPS + 8,)), dma((UNITS, 2)), dma(()), dma((UNITS,)),
        ],
        compiler_params=pltpu.CompilerParams(
            collective_id=1, has_side_effects=True, vmem_limit_bytes=63 * MIB
        ),
        cost_estimate=pl.CostEstimate(flops=80 * MICRO, bytes_accessed=50 * MIB, transcendentals=0),
        name="back",
    )(
        dx, gg, slot, pos, ids, route, gate, n2, attn, gain1.reshape(1, width),
        gain2.reshape(1, width), w_router, w_out, resid, g, hidden, n1, q, k, v, p, w_qkv, relt, rest,
    )


def finish_kernel(
    early_ref, late_ref, slot_ref, gate_ref, resid_ref, big_ref, small_ref, grad_ref,
    router_ref, tail_ref,
    out_ref, qkv_ref, proj_ref, ingrad_ref, gain1_ref, gain2_ref, table_ref, routerg_ref,
):

    @pl.when(pl.program_id(0) == 0)
    def _():
        experts = routerg_ref.shape[0]
        for i in range(gain1_ref.shape[0] // LANES):
            gain1_ref[i * LANES:(i + 1) * LANES] = tail_ref[i, :]
        gain2_ref[...] = router_ref[experts, :]
        table_ref[...] = tail_ref[8:8 + HEADS, :BUCKETS]
        routerg_ref[...] = router_ref[:experts, :]

    ingrad_ref[...] = grad_ref[...].T
    rows_a = early_ref.shape[0]
    cols = slot_ref.shape[1]
    combined = None
    for base, ref in ((0, early_ref), (rows_a, late_ref)):
        table = (
            lax.broadcasted_iota(jnp.int32, (ref.shape[0], cols), 0) + base == slot_ref[...]
        )
        part = dot_tn(ref[...], table.astype(F32).astype(BF16))
        combined = part if combined is None else combined + part
    out_ref[...] = (resid_ref[...] + gate_ref[...] * combined).T.astype(BF16)
    rows = qkv_ref.shape[0]
    half = big_ref.shape[4]
    width = 2 * half
    for q in range(2):
        proj_ref[:, q * half:(q + 1) * half] = big_ref[0, q].astype(F32).reshape(rows, half)
        start = 2 * width + q * half
        qkv_ref[:, start:start + half] = big_ref[1, q].astype(F32).reshape(rows, half)
        for group in range(GROUPS):
            start = q * width + group * GW
            qkv_ref[:, start:start + GW] = small_ref[group, q].astype(F32).reshape(rows, GW)


def finish(out_a, out_b, slot, gate, resid, big, small, grad, router, tail):
    tok = slot.shape[1]
    width = resid.shape[0]
    steps = tok // HALF
    line = pl.BlockSpec((1, HALF), lambda i: (0, i))
    pieces = big.shape[2] // steps
    rows = width // steps
    return pl.pallas_call(
        finish_kernel,
        grid=(steps,),
        in_specs=[
            whole(out_a.shape), whole(out_b.shape), line, line,
            pl.BlockSpec((width, HALF), lambda i: (0, i)),
            pl.BlockSpec(big.shape[:2] + (pieces,) + big.shape[3:], lambda i: (0, 0, i, 0, 0)),
            pl.BlockSpec(small.shape[:2] + (pieces,) + small.shape[3:], lambda i: (0, 0, i, 0, 0)),
            pl.BlockSpec((width, HALF), lambda i: (0, i)), whole(router.shape), whole(tail.shape),
        ],
        out_specs=(
            pl.BlockSpec((HALF, width), lambda i: (i, 0)),
            pl.BlockSpec((rows, 3 * width), lambda i: (i, 0)),
            pl.BlockSpec((rows, width), lambda i: (i, 0)),
            pl.BlockSpec((HALF, width), lambda i: (i, 0)), whole((width,)), whole((width,)),
            whole((HEADS, BUCKETS)), whole((router.shape[0] - 8, width)),
        ),
        out_shape=(
            jax.ShapeDtypeStruct((tok, width), BF16),
            jax.ShapeDtypeStruct((width, 3 * width), F32),
            jax.ShapeDtypeStruct((width, width), F32),
            jax.ShapeDtypeStruct((tok, width), F32), jax.ShapeDtypeStruct((width,), F32),
            jax.ShapeDtypeStruct((width,), F32), jax.ShapeDtypeStruct((HEADS, BUCKETS), F32),
            jax.ShapeDtypeStruct((router.shape[0] - 8, width), F32),
        ),
        compiler_params=pltpu.CompilerParams(vmem_limit_bytes=62 * MIB),
        cost_estimate=pl.CostEstimate(flops=8 * MICRO, bytes_accessed=20 * MIB, transcendentals=0),
        name="finish",
    )(out_a, out_b, slot, gate, resid, big, small, grad, router, tail)


def matmul(a, b):
    return jnp.dot(a, b, preferred_element_type=F32)


AXES = ("narrow", "wide")


def exchange(v):
    return lax.all_to_all(v, AXES, split_axis=0, concat_axis=0, tiled=True)


def local(
    hidden_in, norm_gain_one, w_qkv, w_out, pos_table, norm_gain_two, w_router, w_in, w_down,
    expert_ids, segment_ids, rel_buckets, out_grad,
):
    experts = lax.axis_size("narrow") * lax.axis_size("wide")
    tok, width = hidden_in.shape
    w_router = w_router.T
    cap = max(2, (5 * tok + 4 * experts - 1) // (4 * experts))
    capp = (cap + 7) // 8 * 8
    rows = experts * capp
    ids = expert_ids.reshape(1, tok)
    slot, pos, g_packed = make_slots(experts, cap, capp, ids, out_grad)
    g_rows = exchange(g_packed.reshape(experts, capp, width))
    (n1, q, k, v, p, attn, resid, n2, route, gate, packed, gpack) = front(
        hidden_in, norm_gain_one, w_qkv, w_out, pos_table.T, norm_gain_two, w_router, ids, slot, pos,
        segment_ids, rel_buckets, rows,
    )
    block = block_of(experts, capp)
    dx, out_a, rest, active, ginner, gs, expert_in, gg = expert(
        packed.reshape(experts, capp, width), gpack, g_rows, w_in[0], w_down[0]
    )
    dx = exchange(dx.reshape(experts, capp, width)).reshape(rows, width)
    grad_w_down, grad_w_in = weight_grads(active, gs, expert_in.reshape(rows, width), ginner)
    dx, grad_w_down, grad_w_in = lax.optimization_barrier((dx, grad_w_down, grad_w_in))
    grad, out_b, big, small, early, late = back(
        dx, gg, slot, pos, ids, route, gate, resid, n2, attn, out_grad, hidden_in, n1, q, k, v, p,
        norm_gain_one, norm_gain_two, w_router, w_out, w_qkv, rel_buckets.T, rest, block,
    )
    if experts > EARLY_MOST:
        early = lax.psum(early, AXES)
    blocks = experts // block
    index = lax.axis_index("narrow") * lax.axis_size("wide") + lax.axis_index("wide")
    turn = lax.rem(index // block + blocks - ids // block, blocks)
    place = jnp.where(pos >= 0, (turn * block + lax.rem(ids, block)) * capp + pos, -1)
    layer_out, qkv_grad, out_grad_w, in_grad, gain1g, gain2g, tableg, routerg = finish(
        out_a.reshape(-1, width), out_b.reshape(-1, width), place, gate, resid, big, small, grad,
        early, late,
    )
    return (
        layer_out, in_grad, gain1g, qkv_grad, out_grad_w, tableg.T,
        gain2g, routerg.T, grad_w_in, grad_w_down,
    )


def solution(mesh):
    split = P(AXES, None)
    cube = P(AXES, None, None)
    return jax.shard_map(
        local,
        mesh=mesh,
        in_specs=(
            split, P(), P(), P(), P(), P(), P(), cube, cube, split, split, P(), split,
        ),
        out_specs=(split, split, P(), P(), P(), P(), P(), P(), cube, cube),
        check_vma=False,
    )
```
